256 devices in a mesh: rep: 32 (over x_hi, z, core), head: 8 (over x_lo, y).
Axes of the slice: x: 4 (x_hi: 2, x_lo: 2; x = x_hi * 2 + x_lo), y: 4, z: 8, core: 2. Of those that a mesh axis runs over, the one named last changes fastest.
Arguments:
- queries: bfloat16 [4096, 32, 128], P('rep', 'head'), may hold values from -6 to 6
- tree_keys: bfloat16 [4096, 8, 128], P('rep', 'head'), may hold values from -160 to 160
- tree_values: bfloat16 [4096, 8, 128], P('rep', 'head'), may hold values from -6 to 6
- prefix_keys: bfloat16 [128, 8, 128, 128], P('rep', 'head'), may hold values from -6 to 6
- prefix_values: bfloat16 [128, 8, 128, 128], P('rep', 'head'), may hold values from -6 to 6
- tree_parent: int32 [4096], P('rep'), may hold values from 0 to 62, as said below
- page_table: int32 [64, 16], P('rep'), may hold values from 0 to 127, all different within a row
- out_weight: bfloat16 [4096, 5120], P('head'), may hold values from -1.5 to 1.5
Outputs:
- mixed: bfloat16 [4096, 5120], P(('rep', 'head'))
The draws below stay inside these ranges and needn't reach their ends.
Inputs may be any that keep to these rules, and one draw needn't show every extreme that they name: `tree_parent`: within each session a row's parent is an earlier row, the first row being its own parent. `page_table`: each session names 16 different pages; every page is named by some session.
All inputs are finite; a program needn't handle non-finite values.
Results may differ from the reference program's by a relative error of at most 0.019.
Values may be sent and summed in bfloat16 or wider, within the bound.
No kernel may reach another device: no remote copies, remote signals or barrier semaphores. Data moves between devices by JAX's collectives and lax.ppermute only.
A program may use at most 64 MiB of HBM per device.

```python
import jax
import jax.numpy as jnp
from jax import lax

D = 5120
QH = 32
KVH = 8
HD = 128
TREE = 64
PAGE = 128
USED = 16
SESSIONS = 64
ROWS = 4096
PAGES = 128


def shared_queries(key):
    base_key = jax.random.fold_in(key, 101)
    bell = jnp.clip(jax.random.normal(jax.random.fold_in(base_key, 1), (ROWS, QH, HD), jnp.float32), -6.0, 6.0)
    return bell


def draw_queries(key, part):
    values = shared_queries(key)
    return values.astype(jnp.bfloat16)


def draw_tree_keys(key, part):
    key = jax.random.fold_in(key, 5)
    bell = jnp.clip(jax.random.normal(jax.random.fold_in(key, 1), (ROWS, KVH, HD), jnp.float32), -6.0, 6.0)
    base = bell
    keys = base
    keys = jnp.clip(keys, -160.0, 160.0)
    return keys.astype(jnp.bfloat16)


def draw_tree_parent(key, part):
    key = jax.random.fold_in(key, 7)
    local = jnp.arange(ROWS, dtype=jnp.int32) % TREE
    raw = jax.random.randint(key, (ROWS,), 0, 1 << 20, dtype=jnp.int32)
    pick = raw % jnp.maximum(local, 1)
    parent = jnp.where(local == 0, 0, pick)
    parent = jnp.where(local == TREE - 1, TREE - 2, parent)
    return parent.astype(jnp.int32)


def block_scale(rng, dims, shards, least, largest):
    def one(axis_at, shards_of):
        steps = jax.random.uniform(jax.random.fold_in(jax.random.fold_in(rng, 6), axis_at), (shards_of,), jnp.float32, least / len(shards), largest / len(shards))
        return jnp.repeat(jnp.exp(steps), dims[axis_at] // shards_of).reshape((-1,) + (1,) * (len(dims) - axis_at - 1))

    factor_of = one(*shards[0])
    for cut in shards[1:]:
        factor_of = factor_of * one(*cut)
    return factor_of


def different_ones(key, rows, count, top, lift):
    ranking = jax.random.permutation(jax.random.fold_in(key, 1), count)
    favour = ranking
    for power in range(3):
        favour = favour * favour // count
    favour = favour * lift // count
    chance = jax.random.randint(jax.random.fold_in(key, 2), (rows, count), 0, 4096) + favour
    sure = jax.random.permutation(jax.random.fold_in(key, 3), rows)[jnp.arange(count) % rows]
    chance = jnp.where(jnp.arange(rows)[:, None] == sure[None, :], 1 << 14, chance)
    priority = chance * count + jnp.arange(count)
    return lax.top_k(priority.astype(jnp.int32), top)[1].astype(jnp.int32)


def noise(rng, dims, deviation, most, pieces=(), kind=jnp.bfloat16):
    drawn = deviation * jax.random.normal(rng, dims, jnp.float32)
    if pieces:
        drawn = drawn * block_scale(rng, dims, pieces, -0.22, 0.18)
    return jnp.clip(drawn, -most, most).astype(kind)


def setup_inputs(seed: int = 0) -> dict:
    splits = jax.random.split(jax.random.key(seed), 9)
    queries = draw_queries(jax.random.fold_in(splits[8], 71), 0)
    tree_keys = draw_tree_keys(jax.random.fold_in(splits[8], 71), 0)
    tree_values = noise(splits[2], (ROWS, KVH, HD), 1.0, 6.0, ((0, 32), (1, 8)))
    prefix_keys = noise(splits[3], (PAGES, KVH, PAGE, HD), 1.0, 6.0, ((0, 32), (1, 8)))
    prefix_values = noise(splits[4], (PAGES, KVH, PAGE, HD), 1.0, 6.0, ((0, 32), (1, 8)))
    tree_parent = draw_tree_parent(jax.random.fold_in(splits[8], 71), 0)
    page_table = different_ones(splits[6], SESSIONS, PAGES, USED, 2048)
    out_weight = noise(splits[7], (QH * HD, D), 0.25, 1.5, ((0, 8),))
    return {"queries": queries, "tree_keys": tree_keys, "tree_values": tree_values, "prefix_keys": prefix_keys, "prefix_values": prefix_values, "tree_parent": tree_parent, "page_table": page_table, "out_weight": out_weight}


def ancestors(parent):
    count = parent.shape[0]
    onehot = (parent[:, None] == jnp.arange(count, dtype=jnp.int32)[None, :]).astype(jnp.float32)
    reach = jnp.eye(count, dtype=jnp.float32) + onehot
    for level in range(count.bit_length()):
        reach = jnp.minimum(jnp.dot(reach, reach, precision=lax.Precision.HIGHEST), 1.0)
    return reach > 0.5


def reference(queries, tree_keys, tree_values, prefix_keys, prefix_values, tree_parent, page_table, out_weight):
    group = QH // KVH
    scale = HD ** -0.5

    def one_session(index):
        first = index * TREE
        query = lax.dynamic_slice_in_dim(queries, first, TREE, 0).astype(jnp.float32).reshape(TREE, KVH, group, HD)
        t_keys = lax.dynamic_slice_in_dim(tree_keys, first, TREE, 0).astype(jnp.float32)
        t_vals = lax.dynamic_slice_in_dim(tree_values, first, TREE, 0).astype(jnp.float32)
        parent = lax.dynamic_slice_in_dim(tree_parent, first, TREE, 0)
        visible = ancestors(parent)
        pages = page_table[index]
        p_keys = jnp.take(prefix_keys, pages, axis=0).astype(jnp.float32).transpose(1, 0, 2, 3).reshape(KVH, USED * PAGE, HD)
        p_vals = jnp.take(prefix_values, pages, axis=0).astype(jnp.float32).transpose(1, 0, 2, 3).reshape(KVH, USED * PAGE, HD)
        s_pre = jnp.einsum('tkgd,kpd->kgtp', query, p_keys) * scale
        s_tree = jnp.einsum('tkgd,ukd->kgtu', query, t_keys) * scale
        s_tree = jnp.where(visible[None, None], s_tree, -1e30)
        top = jnp.maximum(jnp.max(s_pre, axis=-1), jnp.max(s_tree, axis=-1))
        e_pre = jnp.exp(s_pre - top[..., None])
        e_tree = jnp.exp(s_tree - top[..., None])
        total = jnp.sum(e_pre, axis=-1) + jnp.sum(e_tree, axis=-1)
        b_pre = lax.optimization_barrier(e_pre.astype(jnp.bfloat16)).astype(jnp.float32)
        b_tree = lax.optimization_barrier(e_tree.astype(jnp.bfloat16)).astype(jnp.float32)
        numer = jnp.einsum('kgtp,kpd->kgtd', b_pre, p_vals) + jnp.einsum('kgtu,ukd->kgtd', b_tree, t_vals)
        result = numer / total[..., None]
        return result.transpose(2, 0, 1, 3).reshape(TREE, QH * HD).astype(jnp.bfloat16)

    attn = lax.map(one_session, jnp.arange(SESSIONS, dtype=jnp.int32)).reshape(ROWS, QH * HD)
    return jnp.dot(attn, out_weight, preferred_element_type=jnp.float32).astype(jnp.bfloat16)
```

```python
import functools
import math

import jax
import jax.numpy as jnp
from jax import lax
from jax.experimental import pallas as pl
from jax.experimental.pallas import tpu as pltpu
from jax.sharding import PartitionSpec as P

NEG = -1e30
Z = 8
GROUP = 4
LOCAL_PAGES = 4
TREE = 64
QROWS = 256
HD = 128
SESS = 8
C2 = (HD ** -0.5) * math.log2(math.e)
BF = jnp.bfloat16
F32 = jnp.float32

NEAR = (0, -1, 1, -2, 2)
FAR = (-3, 3, 4)


def rep_of(xh, z, c):
    return xh * 16 + (z % Z) * 2 + c


def z_perm(k):
    return [(rep_of(a, z, c), rep_of(a, z + k, c)) for a in range(2) for z in range(Z) for c in range(2)]


def group_perm(r):
    return [(rep_of(a, z, c), rep_of(a ^ (r >> 1), z, c ^ (r & 1))) for a in range(2) for z in range(Z) for c in range(2)]


def pair_step(entry, q_ref, kv, m_ref, l_ref, a_ref):
    s = entry >> 8
    k_at = entry & 255
    scores = lax.dot_general(kv[k_at], q_ref[s & (SESS - 1)], (((1,), (1,)), ((), ())), preferred_element_type=F32)
    old = m_ref[s]
    new = jnp.maximum(old, jnp.max(scores, axis=0, keepdims=True))
    probs = jnp.exp2(scores * C2 - new * C2)
    fix = jnp.exp2((old - new) * C2)
    m_ref[s] = new
    l_ref[s] = l_ref[s] * fix + jnp.sum(probs, axis=0, keepdims=True)
    part = lax.dot_general(kv[k_at + LOCAL_PAGES], probs.astype(BF), (((0,), (0,)), ((), ())), preferred_element_type=F32)
    a_ref[s] = a_ref[s] * fix + part


def all_pairs(count, entry_at, q_ref, kv, streams):
    @pl.loop(0, lax.shift_right_logical(count + 1, 1))
    def _(i):
        for r, (m_ref, l_ref, a_ref) in enumerate(streams):
            pair_step(entry_at(2 * i + r), q_ref, kv, m_ref, l_ref, a_ref)


def clear(streams):
    for m_ref, l_ref, a_ref in streams:
        m_ref[...] = jnp.full(m_ref.shape, NEG, F32)
        l_ref[...] = jnp.zeros(l_ref.shape, F32)
        a_ref[...] = jnp.zeros(a_ref.shape, F32)


def merge(states):
    top = functools.reduce(jnp.maximum, [m for m, _, _ in states])
    ws = [jnp.exp2((m - top) * C2) for m, _, _ in states]
    total = sum(w * l for w, (_, l, _) in zip(ws, states))
    acc = sum(w * a for w, (_, _, a) in zip(ws, states))
    return top, total, acc


def near_kernel(*refs):
    nb = len(NEAR)
    tbl, map_near, map_far, parent, tk, tv, q_ref = refs[:7]
    blocks = refs[7:7 + nb]
    list_far, m_out, l_out, a_out = refs[7 + nb:11 + nb]
    kv, m0, l0, a0, m1, l1, a1, list_near, sems = refs[11 + nb:]
    copies = [pltpu.make_async_copy(b, kv.at[pl.ds(i * 8, 8)], sems.at[i]) for i, b in enumerate(blocks)]
    for cp in copies:
        cp.start()
    clear(((m0, l0, a0), (m1, l1, a1)))

    def scan(s, counts):
        n, f = counts
        for j in range(16):
            page = tbl[s, j]
            owner = lax.shift_right_logical(page, 2)
            entry = s * 256 + (page & 3)
            near = map_near[owner]
            far = map_far[owner]
            list_near[n] = entry + near
            list_far[f + 1] = entry + far
            n = n + (near >= 0).astype(jnp.int32)
            f = f + (far >= 0).astype(jnp.int32)
        return n, f

    n, f = lax.fori_loop(0, SESS, scan, (jnp.int32(0), jnp.int32(0)))
    list_near[n] = jnp.int32(SESS * 256)
    list_far[f + 1] = jnp.int32(SESS * 256)
    list_far[0] = f

    lane = lax.broadcasted_iota(jnp.int32, (TREE, TREE), 1)
    eye = (lax.broadcasted_iota(jnp.int32, (TREE, TREE), 0) == lane).astype(F32)
    widen = (
        lax.broadcasted_iota(jnp.int32, (TREE, QROWS), 0)
        == lax.shift_right_logical(lax.broadcasted_iota(jnp.int32, (TREE, QROWS), 1), 2)
    ).astype(BF)
    for s in range(2):
        rows = pl.ds(s * TREE, TREE)
        reach = jnp.minimum(eye + (parent[rows, :] == lane).astype(F32), 1.0)
        for _ in range(7):
            half = reach.astype(BF)
            reach = jnp.minimum(jnp.dot(half, half, preferred_element_type=F32), 1.0)
        seen = lax.dot_general(reach.astype(BF), widen, (((0,), (0,)), ((), ())), preferred_element_type=F32)
        scores = lax.dot_general(tk[rows, :], q_ref[s], (((1,), (1,)), ((), ())), preferred_element_type=F32)
        scores = jnp.where(seen > 0.5, scores, NEG)
        top = jnp.max(scores, axis=0, keepdims=True)
        probs = jnp.exp2(scores * C2 - top * C2)
        m0[s] = top
        l0[s] = jnp.sum(probs, axis=0, keepdims=True)
        a0[s] = lax.dot_general(tv[rows, :], probs.astype(BF), (((0,), (0,)), ((), ())), preferred_element_type=F32)

    for cp in copies:
        cp.wait()
    all_pairs(n, lambda i: list_near[i], q_ref, kv, ((m0, l0, a0), (m1, l1, a1)))
    for s in range(SESS):
        top, total, acc = merge(((m0[s], l0[s], a0[s]), (m1[s], l1[s], a1[s])))
        m_out[s] = top
        l_out[s] = total
        a_out[s] = acc


def far_kernel(*refs):
    nb = len(FAR)
    list_far, q_ref = refs[:2]
    blocks = refs[2:2 + nb]
    m_in, l_in, a_in = refs[2 + nb:5 + nb]
    own = refs[5 + nb]
    outs = refs[6 + nb:9 + nb]
    kv, m0, l0, a0, m1, l1, a1, sems = refs[9 + nb:]
    copies = [pltpu.make_async_copy(b, kv.at[pl.ds(i * 8, 8)], sems.at[i]) for i, b in enumerate(blocks)]
    for cp in copies:
        cp.start()
    clear(((m0, l0, a0), (m1, l1, a1)))
    for cp in copies:
        cp.wait()
    all_pairs(list_far[0], lambda i: list_far[i + 1], q_ref, kv, ((m0, l0, a0), (m1, l1, a1)))
    for s in range(SESS):
        top, total, acc = merge(
            ((m_in[s], l_in[s], a_in[s]), (m0[s], l0[s], a0[s]), (m1[s], l1[s], a1[s]))
        )
        some = total > 0.0
        safe = jnp.where(some, total, 1.0)
        acc = acc * (1.0 / safe)
        lse = jnp.where(some, top * C2 + jnp.log2(safe), NEG)
        lanes = pl.ds((s % 2) * QROWS, QROWS)
        if s < 2:
            own[pl.ds(0, HD), lanes] = acc
            own[pl.ds(HD, 8), lanes] = jnp.broadcast_to(lse, (8, QROWS))
        else:
            out = outs[s // 2 - 1]
            out[pl.ds(0, HD), lanes] = acc.astype(BF)
            hi = lse.astype(BF).astype(F32)
            mid = (lse - hi).astype(BF).astype(F32)
            low = lse - hi - mid
            row = lax.broadcasted_iota(jnp.int32, (16, QROWS), 0)
            parts = jnp.where(row == 0, hi, jnp.where(row == 1, mid, jnp.where(row == 2, low, 0.0)))
            out[pl.ds(HD, 16), lanes] = parts.astype(BF)


def project_kernel(head_ref, own, p1, p2, p3, w_ref, *refs):
    outs = refs[:8]
    rows_f32, attn = refs[8:]

    @pl.when(pl.program_id(0) == 0)
    def _():
        lses = [own[HD:HD + 1, :]]
        vals = [own[:HD, :]]
        for p in (p1, p2, p3):
            tail = p[HD:HD + 16, :].astype(F32)
            lses.append(tail[0:1] + tail[1:2] + tail[2:3])
            vals.append(p[:HD, :].astype(F32))
        top = functools.reduce(jnp.maximum, lses)
        ws = [jnp.exp2(x - top) for x in lses]
        inv = 1.0 / sum(ws)
        mixed = sum(v * (w * inv) for v, w in zip(vals, ws))
        rows_f32[...] = mixed.T
        for k in range(8):
            first = (head_ref[0] ^ k) * 64
            for h in range(4):
                block = rows_f32[pl.ds(first + h, 16, stride=4), :]
                attn[pl.ds(k * 16, 16), pl.ds(h * HD, HD)] = block.astype(BF)

    res = jnp.dot(attn[...], w_ref[...], preferred_element_type=F32).astype(BF)
    for k in range(8):
        outs[k][...] = res[k * 16:(k + 1) * 16]


VMEM = pl.BlockSpec(memory_space=pltpu.VMEM)
SMEM = pl.BlockSpec(memory_space=pltpu.SMEM)
ANY = pl.BlockSpec(memory_space=pl.ANY)


def stream_scratch():
    return [
        pltpu.VMEM((SESS + 1, 1, QROWS), F32),
        pltpu.VMEM((SESS + 1, 1, QROWS), F32),
        pltpu.VMEM((SESS + 1, HD, QROWS), F32),
    ]


def on_device(
    queries, tree_keys, tree_values, prefix_keys, prefix_values, tree_parent, page_table, out_weight
):
    rep = lax.axis_index("rep")
    head = lax.axis_index("head")
    kv = jnp.concatenate([prefix_keys, prefix_values], axis=0).reshape(8, 128, HD)
    up1 = lax.ppermute(kv, "rep", z_perm(1))
    dn1 = lax.ppermute(kv, "rep", z_perm(-1))
    up2 = lax.ppermute(kv, "rep", z_perm(2))
    dn2 = lax.ppermute(kv, "rep", z_perm(-2))
    q_own = queries.reshape(2 * QROWS, HD)
    table_rows = jnp.pad(page_table.reshape(1, 32).astype(BF), ((0, 15), (0, 96)))
    sent = jnp.concatenate([q_own, table_rows], axis=0)
    got = [lax.ppermute(sent, "rep", group_perm(r)) for r in (1, 2, 3)]
    q_all = jnp.concatenate([q_own] + [g[:2 * QROWS] for g in got], axis=0).reshape(SESS, QROWS, HD)
    tables = [page_table] + [g[2 * QROWS, :32].astype(jnp.int32).reshape(2, 16) for g in got]
    table = jnp.concatenate(tables, axis=0)
    up3 = lax.ppermute(up2, "rep", z_perm(1))
    dn3 = lax.ppermute(dn2, "rep", z_perm(-1))
    up4 = lax.ppermute(up2, "rep", z_perm(2))

    reps = jnp.arange(32, dtype=jnp.int32)
    same = ((reps ^ rep) & 17) == 0
    step = ((reps >> 1) - (rep >> 1)) & 7

    def place(offsets):
        at = jnp.full((32,), -100000, jnp.int32)
        for i, k in enumerate(offsets):
            at = jnp.where(same & (step == k % Z), i * 8, at)
        return at

    blocks_near = [kv, up1, dn1, up2, dn2]
    blocks_far = [up3, dn3, up4]
    nn, nf = len(NEAR), len(FAR)
    state = [
        jax.ShapeDtypeStruct((SESS, 1, QROWS), F32),
        jax.ShapeDtypeStruct((SESS, 1, QROWS), F32),
        jax.ShapeDtypeStruct((SESS, HD, QROWS), F32),
    ]
    list_far, m, l, a = pl.pallas_call(
        near_kernel,
        out_shape=[jax.ShapeDtypeStruct((160,), jnp.int32)] + state,
        in_specs=[SMEM] * 3 + [VMEM] * 4 + [ANY] * nn,
        out_specs=[SMEM, VMEM, VMEM, VMEM],
        scratch_shapes=[pltpu.VMEM((8 * nn, 128, HD), BF)]
        + stream_scratch()
        + stream_scratch()
        + [pltpu.SMEM((160,), jnp.int32), pltpu.SemaphoreType.DMA((nn,))],
        compiler_params=pltpu.CompilerParams(vmem_limit_bytes=24 << 20),
        cost_estimate=pl.CostEstimate(flops=4 * 10**9, bytes_accessed=4 << 20, transcendentals=1 << 20),
        name="near_pages",
    )(
        table, place(NEAR), place(FAR), tree_parent.reshape(-1, 1), tree_keys.reshape(-1, HD),
        tree_values.reshape(-1, HD), q_all, *blocks_near,
    )
    own, p1, p2, p3 = pl.pallas_call(
        far_kernel,
        out_shape=[jax.ShapeDtypeStruct((HD + 8, 2 * QROWS), F32)]
        + [jax.ShapeDtypeStruct((HD + 16, 2 * QROWS), BF)] * 3,
        in_specs=[SMEM, VMEM] + [ANY] * nf + [VMEM] * 3,
        out_specs=[VMEM] * 4,
        scratch_shapes=[pltpu.VMEM((8 * nf, 128, HD), BF)]
        + stream_scratch()
        + stream_scratch()
        + [pltpu.SemaphoreType.DMA((nf,))],
        compiler_params=pltpu.CompilerParams(vmem_limit_bytes=24 << 20),
        cost_estimate=pl.CostEstimate(flops=2 * 10**9, bytes_accessed=4 << 20, transcendentals=1 << 20),
        name="far_pages",
    )(list_far, q_all, *blocks_far, m, l, a)
    back = [lax.ppermute(p, "rep", group_perm(r)) for r, p in ((1, p1), (2, p2), (3, p3))]
    cols = 1024
    width = out_weight.shape[1]
    parts = pl.pallas_call(
        project_kernel,
        grid=(width // cols,),
        out_shape=[jax.ShapeDtypeStruct((16, width), BF)] * 8,
        in_specs=[SMEM]
        + [pl.BlockSpec((HD + 8, 2 * QROWS), lambda i: (0, 0))]
        + [pl.BlockSpec((HD + 16, 2 * QROWS), lambda i: (0, 0))] * 3
        + [pl.BlockSpec((512, cols), lambda i: (0, i))],
        out_specs=[pl.BlockSpec((16, cols), lambda i: (0, i))] * 8,
        scratch_shapes=[pltpu.VMEM((2 * QROWS, HD), F32), pltpu.VMEM((128, 512), BF)],
        compiler_params=pltpu.CompilerParams(vmem_limit_bytes=24 << 20),
        cost_estimate=pl.CostEstimate(flops=2 * 128 * 512 * width, bytes_accessed=8 << 20, transcendentals=4096),
        name="combine_project",
    )(head.reshape(1).astype(jnp.int32), own, *back, out_weight)
    total = parts[0].astype(F32)
    for k in (2, 6, 5, 7, 1, 3, 4):
        total = total + lax.ppermute(parts[k], "head", [(i, i ^ k) for i in range(8)]).astype(F32)
    return total.astype(BF)


def solution(mesh):
    in_specs = (
        P("rep", "head", None),
        P("rep", "head", None),
        P("rep", "head", None),
        P("rep", "head", None, None),
        P("rep", "head", None, None),
        P("rep"),
        P("rep", None),
        P("head", None),
    )
    out_specs = P(("rep", "head"), None)
    return jax.shard_map(
        on_device, mesh=mesh, in_specs=in_specs, out_specs=out_specs, check_vma=False
    )
```

```python
import functools
import math

import jax
import jax.numpy as jnp
from jax import lax
from jax.experimental import pallas as pl
from jax.experimental.pallas import tpu as pltpu
from jax.sharding import PartitionSpec as P

NEG = -1e30
Z = 8
GROUP = 4
LOCAL_PAGES = 4
TREE = 64
QROWS = 256
HD = 128
SESS = 8
C2 = (HD ** -0.5) * math.log2(math.e)
BF = jnp.bfloat16
F32 = jnp.float32

STREAMS = 4
NEAR = (-1, 1, -2, 2)
FAR = (-3, 3, 4)


def rep_of(xh, z, c):
    return xh * 16 + (z % Z) * 2 + c


def z_perm(k):
    return [(rep_of(a, z, c), rep_of(a, z + k, c)) for a in range(2) for z in range(Z) for c in range(2)]


def group_perm(r):
    return [(rep_of(a, z, c), rep_of(a ^ (r >> 1), z, c ^ (r & 1))) for a in range(2) for z in range(Z) for c in range(2)]


def pair_steps(entries, q_ref, kv, streams):
    at = [(e >> 8, e & 255) for e in entries]
    scores = [
        lax.dot_general(kv[k], q_ref[pl.ds(pl.multiple_of((s & (SESS - 1)) * QROWS, QROWS), QROWS), :], (((1,), (1,)), ((), ())), preferred_element_type=F32)
        for s, k in at
    ]
    olds = [m[s] for (s, _), (m, _, _) in zip(at, streams)]
    news = [jnp.maximum(o, jnp.max(x, axis=0, keepdims=True)) for o, x in zip(olds, scores)]
    probs = [jnp.exp2(x * C2 - n * C2) for x, n in zip(scores, news)]
    fixes = [jnp.exp2((o - n) * C2) for o, n in zip(olds, news)]
    parts = [
        lax.dot_general(
            kv[k + LOCAL_PAGES], p.astype(BF), (((0,), (0,)), ((), ())), preferred_element_type=F32
        )
        for (_, k), p in zip(at, probs)
    ]
    for (s, _), n, p, fix, part, (m_ref, l_ref, a_ref) in zip(at, news, probs, fixes, parts, streams):
        m_ref[s] = n
        l_ref[s] = l_ref[s] * fix + jnp.sum(p, axis=0, keepdims=True)
        a_ref[s] = a_ref[s] * fix + part


def all_pairs(entries, q_ref, kv, streams):
    ns = len(streams)

    @pl.loop(0, (entries[0] + ns - 1) >> (ns.bit_length() - 1))
    def _(i):
        pair_steps([entries[ns * i + r + 1] for r in range(ns)], q_ref, kv, streams)


def streams_of(refs):
    return [tuple(refs[3 * r:3 * r + 3]) for r in range(STREAMS)]


def clear(streams):
    for m_ref, l_ref, a_ref in streams:
        m_ref[...] = jnp.full(m_ref.shape, NEG, F32)
        l_ref[...] = jnp.zeros(l_ref.shape, F32)
        a_ref[...] = jnp.zeros(a_ref.shape, F32)


def merge(states):
    top = functools.reduce(jnp.maximum, [m for m, _, _ in states])
    ws = [jnp.exp2((m - top) * C2) for m, _, _ in states]
    total = sum(w * l for w, (_, l, _) in zip(ws, states))
    acc = sum(w * a for w, (_, _, a) in zip(ws, states))
    return top, total, acc


def pack_kernel(pk, pv, q, table, kv, sent, sems):
    copies = [
        pltpu.make_async_copy(pk, kv.at[pl.ds(0, LOCAL_PAGES)], sems.at[0]),
        pltpu.make_async_copy(pv, kv.at[pl.ds(LOCAL_PAGES, LOCAL_PAGES)], sems.at[1]),
        pltpu.make_async_copy(q, sent.at[pl.ds(0, 2 * QROWS)], sems.at[2]),
    ]
    for cp in copies:
        cp.start()
    ids = table[...].astype(F32)
    sent[pl.ds(2 * QROWS, 16), :] = jnp.zeros((16, 128), BF)
    row = lax.broadcasted_iota(jnp.int32, (16, 16), 0)
    sent[pl.ds(2 * QROWS, 16), :16] = jnp.where(
        row == 0, ids[0:1, :], jnp.where(row == 1, ids[1:2, :], 0.0)
    ).astype(BF)
    for cp in copies:
        cp.wait()


def own_kernel(
    map_own, map_near, map_far, parent, s0, s1, s2, s3, tk, tv, kv,
    q_out, list_near, list_far, m_out, l_out, a_out, *refs,
):
    tails, ids, tbl, list_own = refs[:4]
    streams = streams_of(refs[4:-1])
    sems = refs[-1]
    sents = (s0, s1, s2, s3)
    for r, x in enumerate(sents):
        tails[pl.ds(r * 16, 16), :] = x[pl.ds(2 * QROWS, 16), :]
    ids[...] = tails[...].astype(F32).astype(jnp.int32)
    to_scalar = pltpu.make_async_copy(ids, tbl, sems.at[0])
    to_scalar.start()
    for r, x in enumerate(sents):
        q_out[pl.ds(r * 2 * QROWS, 2 * QROWS), :] = x[pl.ds(0, 2 * QROWS), :]
    clear(streams)
    both = 2 * TREE
    row = lax.broadcasted_iota(jnp.int32, (both, both), 0)
    lane = lax.broadcasted_iota(jnp.int32, (both, both), 1)
    above = parent[...] + jnp.where(lax.broadcasted_iota(jnp.int32, (1, both), 1) >= TREE, TREE, 0)
    reach = jnp.minimum((row == lane).astype(F32) + (row == above).astype(F32), 1.0)
    for _ in range(7):
        half = reach.astype(BF)
        reach = jnp.minimum(jnp.dot(half, half, preferred_element_type=F32), 1.0)
    half = reach.astype(BF)
    tree_row = lax.broadcasted_iota(jnp.int32, (both, QROWS), 0)
    of_query = lax.shift_right_logical(lax.broadcasted_iota(jnp.int32, (both, QROWS), 1), 2)
    m0, l0, a0 = streams[0]
    for s in range(2):
        rows = pl.ds(s * TREE, TREE)
        widen = (tree_row == of_query + s * TREE).astype(BF)
        seen = jnp.dot(half[s * TREE:(s + 1) * TREE, :], widen, preferred_element_type=F32)
        scores = lax.dot_general(
            tk[rows, :], s0[pl.ds(s * QROWS, QROWS), :], (((1,), (1,)), ((), ())), preferred_element_type=F32
        )
        scores = jnp.where(seen > 0.5, scores, NEG)
        top = jnp.max(scores, axis=0, keepdims=True)
        probs = jnp.exp2(scores * C2 - top * C2)
        m0[s] = top
        l0[s] = jnp.sum(probs, axis=0, keepdims=True)
        a0[s] = lax.dot_general(
            tv[rows, :], probs.astype(BF), (((0,), (0,)), ((), ())), preferred_element_type=F32
        )
    to_scalar.wait()
    maps = (map_own, map_near, map_far)
    lists = (list_own, list_near, list_far)

    def scan(r, counts):
        counts = list(counts)
        for half in range(2):
            pages = [tbl[r * 16 + half, j] for j in range(16)]
            found = [[x[p >> 2] for x in maps] for p in pages]
            for p, at in zip(pages, found):
                entry = (r * 2 + half) * 256 + (p & 3)
                for i in range(3):
                    lists[i][counts[i] + 1] = entry + at[i]
                    counts[i] = counts[i] + (at[i] >= 0).astype(jnp.int32)
        return tuple(counts)

    counts = lax.fori_loop(0, GROUP, scan, (jnp.int32(0),) * 3)
    for i in range(3):
        lists[i][0] = counts[i]
        for r in range(STREAMS - 1):
            lists[i][counts[i] + 1 + r] = jnp.int32(SESS * 256)
    all_pairs(list_own, q_out, kv, streams)
    for s in range(SESS):
        top, total, acc = merge([(m[s], l[s], a[s]) for m, l, a in streams])
        m_out[s] = top
        l_out[s] = total
        a_out[s] = acc


def load_blocks(blocks, kv, sems):
    copies = [pltpu.make_async_copy(b, kv.at[pl.ds(i * 8, 8)], sems.at[i]) for i, b in enumerate(blocks)]
    for cp in copies:
        cp.start()
    return copies


def near_kernel(*refs):
    nb = len(NEAR)
    list_near, q_ref = refs[:2]
    blocks = refs[2:2 + nb]
    before = refs[2 + nb:5 + nb]
    m_out, l_out, a_out, kv, before_a = refs[5 + nb:10 + nb]
    streams = streams_of(refs[10 + nb:-1])
    copies = load_blocks(blocks, kv, refs[-1])
    load = pltpu.make_async_copy(before[2], before_a, refs[-1].at[nb])
    load.start()
    clear(streams)
    for cp in copies:
        cp.wait()
    all_pairs(list_near, q_ref, kv, streams)
    load.wait()
    before = (before[0], before[1], before_a)
    for s in range(SESS):
        top, total, acc = merge([(m[s], l[s], a[s]) for m, l, a in [before] + streams])
        m_out[s] = top
        l_out[s] = total
        a_out[s] = acc


def far_kernel(*refs):
    nb = len(FAR)
    list_far, q_ref = refs[:2]
    blocks = refs[2:2 + nb]
    before = refs[2 + nb:5 + nb]
    own = refs[5 + nb]
    outs = refs[6 + nb:9 + nb]
    kv, before_a = refs[9 + nb:11 + nb]
    streams = streams_of(refs[11 + nb:-1])
    copies = load_blocks(blocks, kv, refs[-1])
    load = pltpu.make_async_copy(before[2], before_a, refs[-1].at[nb])
    load.start()
    clear(streams)
    for cp in copies:
        cp.wait()
    all_pairs(list_far, q_ref, kv, streams)
    load.wait()
    before = (before[0], before[1], before_a)
    for s in range(SESS):
        top, total, acc = merge([(m[s], l[s], a[s]) for m, l, a in [before] + streams])
        some = total > 0.0
        safe = jnp.where(some, total, 1.0)
        acc = acc * (1.0 / safe)
        lse = jnp.where(some, top * C2 + jnp.log2(safe), NEG)
        lanes = pl.ds((s % 2) * QROWS, QROWS)
        if s < 2:
            own[pl.ds(0, HD), lanes] = acc
            own[pl.ds(HD, 8), lanes] = jnp.broadcast_to(lse, (8, QROWS))
        else:
            out = outs[s // 2 - 1]
            out[pl.ds(0, HD), lanes] = acc.astype(BF)
            hi = lse.astype(BF).astype(F32)
            mid = (lse - hi).astype(BF).astype(F32)
            low = lse - hi - mid
            row = lax.broadcasted_iota(jnp.int32, (16, QROWS), 0)
            parts = jnp.where(row == 0, hi, jnp.where(row == 1, mid, jnp.where(row == 2, low, 0.0)))
            out[pl.ds(HD, 16), lanes] = parts.astype(BF)


def combine_kernel(head_ref, own, p1, p2, p3, attn, rows_f32):
    lses = [own[HD:HD + 1, :]]
    vals = [own[:HD, :]]
    for p in (p1, p2, p3):
        tail = p[HD:HD + 16, :].astype(F32)
        lses.append(tail[0:1] + tail[1:2] + tail[2:3])
        vals.append(p[:HD, :].astype(F32))
    top = functools.reduce(jnp.maximum, lses)
    ws = [jnp.exp2(x - top) for x in lses]
    inv = 1.0 / sum(ws)
    mixed = sum(v * (w * inv) for v, w in zip(vals, ws))
    rows_f32[...] = mixed.T
    for k in range(8):
        first = (head_ref[0] ^ k) * 64
        for h in range(4):
            block = rows_f32[pl.ds(first + h, 16, stride=4), :]
            attn[pl.ds(k * 16, 16), pl.ds(h * HD, HD)] = block.astype(BF)


def sum_kernel(*refs):
    out = refs[-1]
    out[...] = functools.reduce(jnp.add, [r[...].astype(F32) for r in refs[:-1]]).astype(BF)


VMEM = pl.BlockSpec(memory_space=pltpu.VMEM)
SMEM = pl.BlockSpec(memory_space=pltpu.SMEM)
ANY = pl.BlockSpec(memory_space=pl.ANY)


def stream_scratch():
    return [
        pltpu.VMEM((SESS + 1, 1, QROWS), F32),
        pltpu.VMEM((SESS + 1, 1, QROWS), F32),
        pltpu.VMEM((SESS + 1, HD, QROWS), F32),
    ]


def state_shapes(n):
    return [
        jax.ShapeDtypeStruct((n, 1, QROWS), F32),
        jax.ShapeDtypeStruct((n, 1, QROWS), F32),
        jax.ShapeDtypeStruct((n, HD, QROWS), F32),
    ]


def lists(n):
    return [jax.ShapeDtypeStruct((160,), jnp.int32)] * n


def own_call(*args):
    return pl.pallas_call(
        own_kernel,
        out_shape=[jax.ShapeDtypeStruct((SESS * QROWS, HD), BF)] + lists(2) + state_shapes(SESS),
        in_specs=[SMEM] * 3 + [VMEM] * 8,
        out_specs=[VMEM, SMEM, SMEM, VMEM, VMEM, VMEM],
        scratch_shapes=[
            pltpu.VMEM((64, 128), BF),
            pltpu.VMEM((64, 128), jnp.int32),
            pltpu.SMEM((64, 128), jnp.int32),
            pltpu.SMEM((160,), jnp.int32),
        ]
        + stream_scratch() * STREAMS
        + [pltpu.SemaphoreType.DMA((1,))],
        compiler_params=pltpu.CompilerParams(vmem_limit_bytes=24 << 20),
        cost_estimate=pl.CostEstimate(flops=2 * 10**9, bytes_accessed=4 << 20, transcendentals=1 << 20),
        name="own_pages",
    )(*args)


def near_call(*args):
    nn = len(NEAR)
    return pl.pallas_call(
        near_kernel,
        out_shape=state_shapes(SESS),
        in_specs=[SMEM, VMEM] + [ANY] * nn + [VMEM, VMEM, ANY],
        out_specs=[VMEM, VMEM, VMEM],
        scratch_shapes=[pltpu.VMEM((8 * nn, 128, HD), BF), pltpu.VMEM((SESS, HD, QROWS), F32)]
        + stream_scratch() * STREAMS
        + [pltpu.SemaphoreType.DMA((nn + 1,))],
        compiler_params=pltpu.CompilerParams(vmem_limit_bytes=24 << 20),
        cost_estimate=pl.CostEstimate(flops=3 * 10**9, bytes_accessed=4 << 20, transcendentals=1 << 20),
        name="near_pages",
    )(*args)


def far_call(*args):
    nf = len(FAR)
    return pl.pallas_call(
        far_kernel,
        out_shape=[jax.ShapeDtypeStruct((HD + 8, 2 * QROWS), F32)]
        + [jax.ShapeDtypeStruct((HD + 16, 2 * QROWS), BF)] * 3,
        in_specs=[SMEM, VMEM] + [ANY] * nf + [VMEM, VMEM, ANY],
        out_specs=[VMEM] * 4,
        scratch_shapes=[pltpu.VMEM((8 * nf, 128, HD), BF), pltpu.VMEM((SESS, HD, QROWS), F32)]
        + stream_scratch() * STREAMS
        + [pltpu.SemaphoreType.DMA((nf + 1,))],
        compiler_params=pltpu.CompilerParams(vmem_limit_bytes=24 << 20),
        cost_estimate=pl.CostEstimate(flops=2 * 10**9, bytes_accessed=4 << 20, transcendentals=1 << 20),
        name="far_pages",
    )(*args)


def on_device(
    queries, tree_keys, tree_values, prefix_keys, prefix_values, tree_parent, page_table, out_weight
):
    rep = lax.axis_index("rep")
    head = lax.axis_index("head")
    q_own = queries.reshape(2 * QROWS, HD)
    kv, sent = pl.pallas_call(
        pack_kernel,
        out_shape=[
            jax.ShapeDtypeStruct((2 * LOCAL_PAGES, 128, HD), BF),
            jax.ShapeDtypeStruct((2 * QROWS + 16, HD), BF),
        ],
        in_specs=[ANY, ANY, ANY, VMEM],
        out_specs=[VMEM, VMEM],
        scratch_shapes=[pltpu.SemaphoreType.DMA((3,))],
        compiler_params=pltpu.CompilerParams(vmem_limit_bytes=59 << 20),
        name="pack",
    )(prefix_keys.reshape(LOCAL_PAGES, 128, HD), prefix_values.reshape(LOCAL_PAGES, 128, HD), q_own, page_table)
    up1 = lax.ppermute(kv, "rep", z_perm(1))
    dn1 = lax.ppermute(kv, "rep", z_perm(-1))
    up2 = lax.ppermute(kv, "rep", z_perm(2))
    dn2 = lax.ppermute(kv, "rep", z_perm(-2))
    sents = [sent] + [lax.ppermute(sent, "rep", group_perm(r)) for r in (1, 2, 3)]
    up3 = lax.ppermute(up2, "rep", z_perm(1))
    dn3 = lax.ppermute(dn2, "rep", z_perm(-1))
    up4 = lax.ppermute(up2, "rep", z_perm(2))
    reps = jnp.arange(32, dtype=jnp.int32)
    same = ((reps ^ rep) & 17) == 0
    step = ((reps >> 1) - (rep >> 1)) & 7

    def place(offsets):
        at = jnp.full((32,), -100000, jnp.int32)
        for i, k in enumerate(offsets):
            at = jnp.where(same & (step == k % Z), i * 8, at)
        return at

    q_all, list_near, list_far, *state = own_call(
        place((0,)), place(NEAR), place(FAR), tree_parent.reshape(1, -1), *sents,
        tree_keys.reshape(-1, HD), tree_values.reshape(-1, HD), kv,
    )
    state = near_call(list_near, q_all, up1, dn1, up2, dn2, *state)
    own, p1, p2, p3 = far_call(list_far, q_all, up3, dn3, up4, *state)
    back = [lax.ppermute(p, "rep", group_perm(r)) for r, p in ((1, p1), (2, p2), (3, p3))]
    width = out_weight.shape[1]
    attn = pl.pallas_call(
        combine_kernel,
        out_shape=jax.ShapeDtypeStruct((128, 512), BF),
        in_specs=[SMEM] + [VMEM] * 4,
        out_specs=VMEM,
        scratch_shapes=[pltpu.VMEM((2 * QROWS, HD), F32)],
        compiler_params=pltpu.CompilerParams(vmem_limit_bytes=24 << 20),
        cost_estimate=pl.CostEstimate(flops=10**6, bytes_accessed=1 << 20, transcendentals=4096),
        name="combine",
    )(head.reshape(1).astype(jnp.int32), own, *back)
    rows = jnp.dot(attn, out_weight, preferred_element_type=F32).astype(BF)
    parts = [rows[k * 16:(k + 1) * 16] for k in range(8)]
    terms = [lax.ppermute(parts[k], "head", [(i, i ^ k) for i in range(8)]) for k in (1, 3, 4, 2, 5, 7, 6)]
    return pl.pallas_call(
        sum_kernel,
        out_shape=jax.ShapeDtypeStruct((16, width), BF),
        in_specs=[VMEM] * 8,
        out_specs=VMEM,
        compiler_params=pltpu.CompilerParams(vmem_limit_bytes=24 << 20),
        name="sum_heads",
    )(parts[0], *terms)


def solution(mesh):
    in_specs = (
        P("rep", "head", None),
        P("rep", "head", None),
        P("rep", "head", None),
        P("rep", "head", None, None),
        P("rep", "head", None, None),
        P("rep"),
        P("rep", None),
        P("head", None),
    )
    out_specs = P(("rep", "head"), None)
    return jax.shard_map(
        on_device, mesh=mesh, in_specs=in_specs, out_specs=out_specs, check_vma=False
    )
```

```python
import functools
import math

import jax
import jax.numpy as jnp
from jax import lax
from jax.experimental import pallas as pl
from jax.experimental.pallas import tpu as pltpu
from jax.sharding import PartitionSpec as P

NEG = -1e30
Z = 8
GROUP = 4
LOCAL_PAGES = 4
TK_AT = 528
TV_AT = 656
TREE = 64
QROWS = 256
HD = 128
SESS = 8
C2 = (HD ** -0.5) * math.log2(math.e)
BF = jnp.bfloat16
F32 = jnp.float32

STREAMS = 4
GROUPS = ((0,), (-1, 1, -2, 2), (-3, 3), (4,))


def rep_of(xh, z, c):
    return xh * 16 + (z % Z) * 2 + c


def z_perm(k):
    return [(rep_of(a, z, c), rep_of(a, z + k, c)) for a in range(2) for z in range(Z) for c in range(2)]


def group_perm(r):
    return [(rep_of(a, z, c), rep_of(a ^ (r >> 1), z, c ^ (r & 1))) for a in range(2) for z in range(Z) for c in range(2)]


def pair_steps(entries, q_ref, kv, streams):
    at = [(e >> 8, e & 255) for e in entries]
    scores = [
        lax.dot_general(kv[k], q_ref[pl.ds(pl.multiple_of((s & (SESS - 1)) * QROWS, QROWS), QROWS), :], (((1,), (1,)), ((), ())), preferred_element_type=F32)
        for s, k in at
    ]
    olds = [m[s] for (s, _), (m, _, _) in zip(at, streams)]
    news = [jnp.maximum(o, jnp.max(x, axis=0, keepdims=True)) for o, x in zip(olds, scores)]
    probs = [jnp.exp2(x * C2 - n * C2) for x, n in zip(scores, news)]
    fixes = [jnp.exp2((o - n) * C2) for o, n in zip(olds, news)]
    parts = [
        lax.dot_general(
            kv[k + LOCAL_PAGES], p.astype(BF), (((0,), (0,)), ((), ())), preferred_element_type=F32
        )
        for (_, k), p in zip(at, probs)
    ]
    for (s, _), n, p, fix, part, (m_ref, l_ref, a_ref) in zip(at, news, probs, fixes, parts, streams):
        m_ref[s] = n
        l_ref[s] = l_ref[s] * fix + jnp.sum(p, axis=0, keepdims=True)
        a_ref[s] = a_ref[s] * fix + part


def all_pairs(entries, q_ref, kv, streams):
    ns = len(streams)

    @pl.loop(0, (entries[0] + ns - 1) >> (ns.bit_length() - 1))
    def _(i):
        pair_steps([entries[ns * i + r + 1] for r in range(ns)], q_ref, kv, streams)


def streams_of(refs):
    return [tuple(refs[3 * r:3 * r + 3]) for r in range(STREAMS)]


def clear(streams):
    for m_ref, l_ref, a_ref in streams:
        m_ref[...] = jnp.full(m_ref.shape, NEG, F32)
        l_ref[...] = jnp.zeros(l_ref.shape, F32)
        a_ref[...] = jnp.zeros(a_ref.shape, F32)


def merge(states):
    top = functools.reduce(jnp.maximum, [m for m, _, _ in states])
    ws = [jnp.exp2((m - top) * C2) for m, _, _ in states]
    total = sum(w * l for w, (_, l, _) in zip(ws, states))
    acc = sum(w * a for w, (_, _, a) in zip(ws, states))
    return top, total, acc


def pack_kernel(pk, pv, q, tk, tv, table, parent, kv, sent, local, tail, sems):
    copies = [
        pltpu.make_async_copy(pk, kv.at[pl.ds(0, LOCAL_PAGES)], sems.at[0]),
        pltpu.make_async_copy(pv, kv.at[pl.ds(LOCAL_PAGES, LOCAL_PAGES)], sems.at[1]),
        pltpu.make_async_copy(q, sent.at[pl.ds(0, 2 * QROWS)], sems.at[2]),
        pltpu.make_async_copy(q, local.at[pl.ds(0, 2 * QROWS)], sems.at[3]),
        pltpu.make_async_copy(tk, local.at[pl.ds(TK_AT, 128)], sems.at[4]),
        pltpu.make_async_copy(tv, local.at[pl.ds(TV_AT, 128)], sems.at[5]),
    ]
    for cp in copies:
        cp.start()
    ids = table[...].astype(F32)
    row = lax.broadcasted_iota(jnp.int32, (16, 128), 0)
    tail[...] = jnp.where(row == 2, parent[...].astype(F32), 0.0).astype(BF)
    row = row[:, :16]
    tail[:, :16] = jnp.where(
        row == 0, ids[0:1, :], jnp.where(row == 1, ids[1:2, :], jnp.where(row == 2, parent[:, :16].astype(F32), 0.0))
    ).astype(BF)
    last = [
        pltpu.make_async_copy(tail, sent.at[pl.ds(2 * QROWS, 16)], sems.at[6]),
        pltpu.make_async_copy(tail, local.at[pl.ds(2 * QROWS, 16)], sems.at[7]),
    ]
    for cp in last:
        cp.start()
    for cp in copies + last:
        cp.wait()


def own_kernel(maps, local, s1, s2, s3, kv, q_out, *refs):
    lists = refs[:3]
    m_out, l_out, a_out, tails, ids, tbl, list_own, found = refs[3:11]
    lists = (list_own,) + lists
    streams = streams_of(refs[11:-1])
    sems = refs[-1]
    sents = (local, s1, s2, s3)
    for r, x in enumerate(sents):
        tails[pl.ds(r * 16, 16), :] = x[pl.ds(2 * QROWS, 16), :]
    ids[...] = tails[...].astype(F32).astype(jnp.int32)
    to_scalar = pltpu.make_async_copy(ids, tbl, sems.at[0])
    to_scalar.start()
    for r, x in enumerate(sents):
        q_out[pl.ds(r * 2 * QROWS, 2 * QROWS), :] = x[pl.ds(0, 2 * QROWS), :]
    clear(streams)
    both = 2 * TREE
    row = lax.broadcasted_iota(jnp.int32, (both, both), 0)
    lane = lax.broadcasted_iota(jnp.int32, (both, both), 1)
    above = ids[2:3, :] + jnp.where(lax.broadcasted_iota(jnp.int32, (1, both), 1) >= TREE, TREE, 0)
    reach = jnp.minimum((row == lane).astype(F32) + (row == above).astype(F32), 1.0)
    for _ in range(7):
        half = reach.astype(BF)
        reach = jnp.minimum(jnp.dot(half, half, preferred_element_type=F32), 1.0)
    half = reach.astype(BF)
    tree_row = lax.broadcasted_iota(jnp.int32, (both, QROWS), 0)
    of_query = lax.shift_right_logical(lax.broadcasted_iota(jnp.int32, (both, QROWS), 1), 2)
    m0, l0, a0 = streams[0]
    for s in range(2):
        widen = (tree_row == of_query + s * TREE).astype(BF)
        seen = jnp.dot(half[s * TREE:(s + 1) * TREE, :], widen, preferred_element_type=F32)
        scores = lax.dot_general(
            local[pl.ds(TK_AT + s * TREE, TREE), :],
            local[pl.ds(s * QROWS, QROWS), :],
            (((1,), (1,)), ((), ())),
            preferred_element_type=F32,
        )
        scores = jnp.where(seen > 0.5, scores, NEG)
        top = jnp.max(scores, axis=0, keepdims=True)
        probs = jnp.exp2(scores * C2 - top * C2)
        m0[s] = top
        l0[s] = jnp.sum(probs, axis=0, keepdims=True)
        a0[s] = lax.dot_general(
            local[pl.ds(TV_AT + s * TREE, TREE), :],
            probs.astype(BF),
            (((0,), (0,)), ((), ())),
            preferred_element_type=F32,
        )
    to_scalar.wait()

    def scan(r, n):
        for half in range(2):
            pages = [tbl[r * 16 + half, j] for j in range(16)]
            at = [maps[p >> 2] for p in pages]
            for p, where in zip(pages, at):
                found[n] = (r * 2 + half) * 256 + (p & 3) + where
                n = n + (where >= 0).astype(jnp.int32)
        return n

    total = lax.fori_loop(0, GROUP, scan, jnp.int32(0))

    def sort(i, counts):
        entry = found[i]
        kind = entry >> 16
        out = []
        for k in range(4):
            lists[k][counts[k] + 1] = entry & 65535
            out.append(counts[k] + (kind == k).astype(jnp.int32))
        return tuple(out)

    counts = lax.fori_loop(0, total, sort, (jnp.int32(0),) * 4)
    for k in range(4):
        lists[k][0] = counts[k]
        for r in range(STREAMS - 1):
            lists[k][counts[k] + 1 + r] = jnp.int32(SESS * 256)
    all_pairs(list_own, q_out, kv, streams)
    for s in range(SESS):
        top, total, acc = merge([(m[s], l[s], a[s]) for m, l, a in streams])
        m_out[s] = top
        l_out[s] = total
        a_out[s] = acc


def load_blocks(blocks, kv, sems):
    copies = [pltpu.make_async_copy(b, kv.at[pl.ds(i * 8, 8)], sems.at[i]) for i, b in enumerate(blocks)]
    for cp in copies:
        cp.start()
    return copies


def near_kernel(nb, *refs):
    list_near, q_ref = refs[:2]
    blocks = refs[2:2 + nb]
    before = refs[2 + nb:5 + nb]
    m_out, l_out, a_out, kv = refs[5 + nb:9 + nb]
    streams = streams_of(refs[9 + nb:-1])
    copies = load_blocks(blocks, kv, refs[-1])
    clear(streams)
    for cp in copies:
        cp.wait()
    all_pairs(list_near, q_ref, kv, streams)
    for s in range(SESS):
        top, total, acc = merge([(m[s], l[s], a[s]) for m, l, a in [before] + streams])
        m_out[s] = top
        l_out[s] = total
        a_out[s] = acc


def far_kernel(nb, *refs):
    list_far, q_ref = refs[:2]
    blocks = refs[2:2 + nb]
    before = refs[2 + nb:5 + nb]
    own = refs[5 + nb]
    outs = refs[6 + nb:9 + nb]
    kv = refs[9 + nb]
    streams = streams_of(refs[10 + nb:-1])
    copies = load_blocks(blocks, kv, refs[-1])
    clear(streams)
    for cp in copies:
        cp.wait()
    all_pairs(list_far, q_ref, kv, streams)
    for s in range(SESS):
        top, total, acc = merge([(m[s], l[s], a[s]) for m, l, a in [before] + streams])
        some = total > 0.0
        safe = jnp.where(some, total, 1.0)
        acc = acc * (1.0 / safe)
        lse = jnp.where(some, top * C2 + jnp.log2(safe), NEG)
        lanes = pl.ds((s % 2) * QROWS, QROWS)
        if s < 2:
            own[pl.ds(0, HD), lanes] = acc
            own[pl.ds(HD, 8), lanes] = jnp.broadcast_to(lse, (8, QROWS))
        else:
            out = outs[s // 2 - 1]
            out[pl.ds(0, HD), lanes] = acc.astype(BF)
            hi = lse.astype(BF).astype(F32)
            mid = (lse - hi).astype(BF).astype(F32)
            low = lse - hi - mid
            row = lax.broadcasted_iota(jnp.int32, (16, QROWS), 0)
            parts = jnp.where(row == 0, hi, jnp.where(row == 1, mid, jnp.where(row == 2, low, 0.0)))
            out[pl.ds(HD, 16), lanes] = parts.astype(BF)


def combine_kernel(head_ref, own, p1, p2, p3, attn, rows_f32):
    lses = [own[HD:HD + 1, :]]
    vals = [own[:HD, :]]
    for p in (p1, p2, p3):
        tail = p[HD:HD + 16, :].astype(F32)
        lses.append(tail[0:1] + tail[1:2] + tail[2:3])
        vals.append(p[:HD, :].astype(F32))
    top = functools.reduce(jnp.maximum, lses)
    ws = [jnp.exp2(x - top) for x in lses]
    inv = 1.0 / sum(ws)
    mixed = sum(v * (w * inv) for v, w in zip(vals, ws))
    rows_f32[...] = mixed.T
    for k in range(8):
        first = (head_ref[0] ^ k) * 64
        for h in range(4):
            block = rows_f32[pl.ds(first + h, 16, stride=4), :]
            attn[pl.ds(k * 16, 16), pl.ds(h * HD, HD)] = block.astype(BF)


def sum_kernel(*refs):
    out = refs[-1]
    out[...] = functools.reduce(jnp.add, [r[...].astype(F32) for r in refs[:-1]]).astype(BF)


VMEM = pl.BlockSpec(memory_space=pltpu.VMEM)
SMEM = pl.BlockSpec(memory_space=pltpu.SMEM)
ANY = pl.BlockSpec(memory_space=pl.ANY)


def stream_scratch():
    return [
        pltpu.VMEM((SESS + 1, 1, QROWS), F32),
        pltpu.VMEM((SESS + 1, 1, QROWS), F32),
        pltpu.VMEM((SESS + 1, HD, QROWS), F32),
    ]


def state_shapes(n):
    return [
        jax.ShapeDtypeStruct((n, 1, QROWS), F32),
        jax.ShapeDtypeStruct((n, 1, QROWS), F32),
        jax.ShapeDtypeStruct((n, HD, QROWS), F32),
    ]


def lists(n):
    return [jax.ShapeDtypeStruct((160,), jnp.int32)] * n


def own_call(*args):
    return pl.pallas_call(
        own_kernel,
        out_shape=[jax.ShapeDtypeStruct((SESS * QROWS, HD), BF)] + lists(3) + state_shapes(SESS),
        in_specs=[SMEM] + [VMEM] * 5,
        out_specs=[VMEM] + [SMEM] * 3 + [VMEM] * 3,
        scratch_shapes=[
            pltpu.VMEM((64, 128), BF),
            pltpu.VMEM((64, 128), jnp.int32),
            pltpu.SMEM((64, 128), jnp.int32),
            pltpu.SMEM((160,), jnp.int32),
            pltpu.SMEM((160,), jnp.int32),
        ]
        + stream_scratch() * STREAMS
        + [pltpu.SemaphoreType.DMA((1,))],
        compiler_params=pltpu.CompilerParams(vmem_limit_bytes=24 << 20),
        cost_estimate=pl.CostEstimate(flops=2 * 10**9, bytes_accessed=4 << 20, transcendentals=1 << 20),
        name="own_pages",
    )(*args)


def block_scratch(nb):
    return (
        [pltpu.VMEM((8 * nb, 128, HD), BF)]
        + stream_scratch() * STREAMS
        + [pltpu.SemaphoreType.DMA((nb,))]
    )


def near_call(pages, q_all, blocks, state, name):
    nb = len(blocks)
    return pl.pallas_call(
        functools.partial(near_kernel, nb),
        out_shape=state_shapes(SESS),
        in_specs=[SMEM, VMEM] + [ANY] * nb + [VMEM] * 3,
        out_specs=[VMEM] * 3,
        scratch_shapes=block_scratch(nb),
        compiler_params=pltpu.CompilerParams(vmem_limit_bytes=24 << 20),
        cost_estimate=pl.CostEstimate(flops=10**9 * nb, bytes_accessed=4 << 20, transcendentals=1 << 20),
        name=name,
    )(pages, q_all, *blocks, *state)


def far_call(pages, q_all, blocks, state):
    nb = len(blocks)
    return pl.pallas_call(
        functools.partial(far_kernel, nb),
        out_shape=[jax.ShapeDtypeStruct((HD + 8, 2 * QROWS), F32)]
        + [jax.ShapeDtypeStruct((HD + 16, 2 * QROWS), BF)] * 3,
        in_specs=[SMEM, VMEM] + [ANY] * nb + [VMEM] * 3,
        out_specs=[VMEM] * 4,
        scratch_shapes=block_scratch(nb),
        compiler_params=pltpu.CompilerParams(vmem_limit_bytes=24 << 20),
        cost_estimate=pl.CostEstimate(flops=10**9, bytes_accessed=4 << 20, transcendentals=1 << 20),
        name="last_pages",
    )(pages, q_all, *blocks, *state)


def on_device(
    queries, tree_keys, tree_values, prefix_keys, prefix_values, tree_parent, page_table, out_weight
):
    rep = lax.axis_index("rep")
    head = lax.axis_index("head")
    q_own = queries.reshape(2 * QROWS, HD)
    kv, sent, local = pl.pallas_call(
        pack_kernel,
        out_shape=[
            jax.ShapeDtypeStruct((2 * LOCAL_PAGES, 128, HD), BF),
            jax.ShapeDtypeStruct((2 * QROWS + 16, HD), BF),
            jax.ShapeDtypeStruct((TV_AT + 128, HD), BF),
        ],
        in_specs=[ANY] * 5 + [VMEM] * 2,
        out_specs=[ANY] * 3,
        scratch_shapes=[pltpu.VMEM((16, 128), BF), pltpu.SemaphoreType.DMA((8,))],
        compiler_params=pltpu.CompilerParams(vmem_limit_bytes=59 << 20),
        name="pack",
    )(
        prefix_keys.reshape(LOCAL_PAGES, 128, HD), prefix_values.reshape(LOCAL_PAGES, 128, HD), q_own,
        tree_keys.reshape(-1, HD), tree_values.reshape(-1, HD), page_table, tree_parent.reshape(1, -1),
    )
    up1 = lax.ppermute(kv, "rep", z_perm(1))
    dn1 = lax.ppermute(kv, "rep", z_perm(-1))
    sents = [lax.ppermute(sent, "rep", group_perm(r)) for r in (1, 2, 3)]
    up2 = lax.ppermute(up1, "rep", z_perm(1))
    dn2 = lax.ppermute(dn1, "rep", z_perm(-1))
    up3 = lax.ppermute(up2, "rep", z_perm(1))
    dn3 = lax.ppermute(dn2, "rep", z_perm(-1))
    up4 = lax.ppermute(up3, "rep", z_perm(1))

    reps = jnp.arange(32, dtype=jnp.int32)
    same = ((reps ^ rep) & 17) == 0
    step = ((reps >> 1) - (rep >> 1)) & 7
    maps = jnp.full((32,), -(1 << 20), jnp.int32)
    for k, offsets in enumerate(GROUPS):
        for i, o in enumerate(offsets):
            maps = jnp.where(same & (step == o % Z), k * 65536 + i * 8, maps)
    q_all, list_1, list_2, list_3, *state = own_call(maps, local, *sents, kv)
    state = near_call(list_1, q_all, (up1, dn1, up2, dn2), state, "near_pages")
    state = near_call(list_2, q_all, (up3, dn3), state, "far_pages")
    own, p1, p2, p3 = far_call(list_3, q_all, (up4,), state)
    back = [lax.ppermute(p, "rep", group_perm(r)) for r, p in ((1, p1), (2, p2), (3, p3))]
    width = out_weight.shape[1]
    attn = pl.pallas_call(
        combine_kernel,
        out_shape=jax.ShapeDtypeStruct((128, 512), BF),
        in_specs=[SMEM] + [VMEM] * 4,
        out_specs=VMEM,
        scratch_shapes=[pltpu.VMEM((2 * QROWS, HD), F32)],
        compiler_params=pltpu.CompilerParams(vmem_limit_bytes=24 << 20),
        cost_estimate=pl.CostEstimate(flops=10**6, bytes_accessed=1 << 20, transcendentals=4096),
        name="combine",
    )(head.reshape(1).astype(jnp.int32), own, *back)
    rows = jnp.dot(attn, out_weight, preferred_element_type=F32).astype(BF)
    parts = [rows[k * 16:(k + 1) * 16] for k in range(8)]
    terms = [lax.ppermute(parts[k], "head", [(i, i ^ k) for i in range(8)]) for k in (1, 3, 4, 2, 5, 7, 6)]
    return pl.pallas_call(
        sum_kernel,
        out_shape=jax.ShapeDtypeStruct((16, width), BF),
        in_specs=[VMEM] * 8,
        out_specs=VMEM,
        compiler_params=pltpu.CompilerParams(vmem_limit_bytes=24 << 20),
        name="sum_heads",
    )(parts[0], *terms)


def solution(mesh):
    in_specs = (
        P("rep", "head", None),
        P("rep", "head", None),
        P("rep", "head", None),
        P("rep", "head", None, None),
        P("rep", "head", None, None),
        P("rep"),
        P("rep", None),
        P("head", None),
    )
    out_specs = P(("rep", "head"), None)
    return jax.shard_map(
        on_device, mesh=mesh, in_specs=in_specs, out_specs=out_specs, check_vma=False
    )
```

```python
import functools
import math

import jax
import jax.numpy as jnp
from jax import lax
from jax.experimental import pallas as pl
from jax.experimental.pallas import tpu as pltpu
from jax.sharding import PartitionSpec as P

NEG = -1e30
Z = 8
GROUP = 4
LOCAL_PAGES = 4
TK_AT = 528
TV_AT = 656
TREE = 64
QROWS = 256
HD = 128
SESS = 8
C2 = (HD ** -0.5) * math.log2(math.e)
BF = jnp.bfloat16
F32 = jnp.float32

STREAMS = 4
GROUPS = ((0,), (-1, 1, -2, 2), (-3, 3), (4,))


def rep_of(xh, z, c):
    return xh * 16 + (z % Z) * 2 + c


def z_perm(k):
    return [(rep_of(a, z, c), rep_of(a, z + k, c)) for a in range(2) for z in range(Z) for c in range(2)]


def group_perm(r):
    return [(rep_of(a, z, c), rep_of(a ^ (r >> 1), z, c ^ (r & 1))) for a in range(2) for z in range(Z) for c in range(2)]


def pair_steps(entries, q_ref, kv, streams):
    at = [(e >> 8, e & 255) for e in entries]
    scores = [
        lax.dot_general(kv[k], q_ref[pl.ds(pl.multiple_of((s & (SESS - 1)) * QROWS, QROWS), QROWS), :], (((1,), (1,)), ((), ())), preferred_element_type=F32)
        for s, k in at
    ]
    olds = [m[s] for (s, _), (m, _, _) in zip(at, streams)]
    news = [jnp.maximum(o, jnp.max(x, axis=0, keepdims=True)) for o, x in zip(olds, scores)]
    probs = [jnp.exp2(x * C2 - n * C2) for x, n in zip(scores, news)]
    fixes = [jnp.exp2((o - n) * C2) for o, n in zip(olds, news)]
    parts = [
        lax.dot_general(
            kv[k + LOCAL_PAGES], p.astype(BF), (((0,), (0,)), ((), ())), preferred_element_type=F32
        )
        for (_, k), p in zip(at, probs)
    ]
    for (s, _), n, p, fix, part, (m_ref, l_ref, a_ref) in zip(at, news, probs, fixes, parts, streams):
        m_ref[s] = n
        l_ref[s] = l_ref[s] * fix + jnp.sum(p, axis=0, keepdims=True)
        a_ref[s] = a_ref[s] * fix + part


def all_pairs(entries, q_ref, kv, streams):
    ns = len(streams)

    @pl.loop(0, (entries[0] + ns - 1) >> (ns.bit_length() - 1))
    def _(i):
        pair_steps([entries[ns * i + r + 1] for r in range(ns)], q_ref, kv, streams)


def streams_of(refs):
    return [tuple(refs[3 * r:3 * r + 3]) for r in range(STREAMS)]


def clear(streams):
    for m_ref, l_ref, a_ref in streams:
        m_ref[...] = jnp.full(m_ref.shape, NEG, F32)
        l_ref[...] = jnp.zeros(l_ref.shape, F32)
        a_ref[...] = jnp.zeros(a_ref.shape, F32)


def merge(states):
    top = functools.reduce(jnp.maximum, [m for m, _, _ in states])
    ws = [jnp.exp2((m - top) * C2) for m, _, _ in states]
    total = sum(w * l for w, (_, l, _) in zip(ws, states))
    acc = sum(w * a for w, (_, _, a) in zip(ws, states))
    return top, total, acc


def pack_kernel(q, tk, tv, table, parent, up1, dn1, sent, local, sems):
    del up1, dn1
    copies = [
        pltpu.make_async_copy(q, sent.at[pl.ds(0, 2 * QROWS)], sems.at[0]),
        pltpu.make_async_copy(q, local.at[pl.ds(0, 2 * QROWS)], sems.at[1]),
        pltpu.make_async_copy(tk, local.at[pl.ds(TK_AT, 128)], sems.at[2]),
        pltpu.make_async_copy(tv, local.at[pl.ds(TV_AT, 128)], sems.at[3]),
    ]
    for cp in copies:
        cp.start()
    ids = table[...].astype(F32)
    row = lax.broadcasted_iota(jnp.int32, (16, 128), 0)
    above = parent[...].astype(F32)
    tail = pl.ds(2 * QROWS, 16)
    sent[tail, :] = jnp.zeros((16, 128), BF)
    local[tail, :] = jnp.where(row == 2, above, 0.0).astype(BF)
    row = row[:, :16]
    pages = jnp.where(row == 0, ids[0:1, :], jnp.where(row == 1, ids[1:2, :], 0.0))
    sent[tail, :16] = pages.astype(BF)
    local[tail, :16] = jnp.where(row == 2, above[:, :16], pages).astype(BF)
    for cp in copies:
        cp.wait()


def own_kernel(maps, local, s1, s2, s3, kv, up2, dn2, q_out, *refs):
    del up2, dn2
    lists = refs[:3]
    m_out, l_out, a_out, tails, ids, tbl, list_own, found = refs[3:11]
    lists = (list_own,) + lists
    streams = streams_of(refs[11:-1])
    sems = refs[-1]
    sents = (local, s1, s2, s3)
    for r, x in enumerate(sents):
        tails[pl.ds(r * 16, 16), :] = x[pl.ds(2 * QROWS, 16), :]
    ids[...] = tails[...].astype(F32).astype(jnp.int32)
    to_scalar = pltpu.make_async_copy(ids, tbl, sems.at[0])
    to_scalar.start()
    for r, x in enumerate(sents):
        q_out[pl.ds(r * 2 * QROWS, 2 * QROWS), :] = x[pl.ds(0, 2 * QROWS), :]
    clear(streams)
    both = 2 * TREE
    row = lax.broadcasted_iota(jnp.int32, (both, both), 0)
    lane = lax.broadcasted_iota(jnp.int32, (both, both), 1)
    above = ids[2:3, :] + jnp.where(lax.broadcasted_iota(jnp.int32, (1, both), 1) >= TREE, TREE, 0)
    reach = jnp.minimum((row == lane).astype(F32) + (row == above).astype(F32), 1.0)
    for _ in range(7):
        half = reach.astype(BF)
        reach = jnp.minimum(jnp.dot(half, half, preferred_element_type=F32), 1.0)
    half = reach.astype(BF)
    tree_row = lax.broadcasted_iota(jnp.int32, (both, QROWS), 0)
    of_query = lax.shift_right_logical(lax.broadcasted_iota(jnp.int32, (both, QROWS), 1), 2)
    m0, l0, a0 = streams[0]
    for s in range(2):
        widen = (tree_row == of_query + s * TREE).astype(BF)
        seen = jnp.dot(half[s * TREE:(s + 1) * TREE, :], widen, preferred_element_type=F32)
        scores = lax.dot_general(
            local[pl.ds(TK_AT + s * TREE, TREE), :],
            local[pl.ds(s * QROWS, QROWS), :],
            (((1,), (1,)), ((), ())),
            preferred_element_type=F32,
        )
        scores = jnp.where(seen > 0.5, scores, NEG)
        top = jnp.max(scores, axis=0, keepdims=True)
        probs = jnp.exp2(scores * C2 - top * C2)
        m0[s] = top
        l0[s] = jnp.sum(probs, axis=0, keepdims=True)
        a0[s] = lax.dot_general(
            local[pl.ds(TV_AT + s * TREE, TREE), :],
            probs.astype(BF),
            (((0,), (0,)), ((), ())),
            preferred_element_type=F32,
        )
    to_scalar.wait()

    def scan(r, n):
        for half in range(2):
            pages = [tbl[r * 16 + half, j] for j in range(16)]
            at = [maps[p >> 2] for p in pages]
            for p, where in zip(pages, at):
                found[n] = (r * 2 + half) * 256 + (p & 3) + where
                n = n + (where >= 0).astype(jnp.int32)
        return n

    total = lax.fori_loop(0, GROUP, scan, jnp.int32(0))

    def sort(i, counts):
        entry = found[i]
        kind = entry >> 16
        out = []
        for k in range(4):
            lists[k][counts[k] + 1] = entry & 65535
            out.append(counts[k] + (kind == k).astype(jnp.int32))
        return tuple(out)

    counts = lax.fori_loop(0, total, sort, (jnp.int32(0),) * 4)
    for k in range(4):
        lists[k][0] = counts[k]
        for r in range(STREAMS - 1):
            lists[k][counts[k] + 1 + r] = jnp.int32(SESS * 256)
    all_pairs(list_own, q_out, kv, streams)
    for s in range(SESS):
        top, total, acc = merge([(m[s], l[s], a[s]) for m, l, a in streams])
        m_out[s] = top
        l_out[s] = total
        a_out[s] = acc


def load_blocks(blocks, kv, sems):
    copies = [pltpu.make_async_copy(b, kv.at[pl.ds(i * 8, 8)], sems.at[i]) for i, b in enumerate(blocks)]
    for cp in copies:
        cp.start()
    return copies


def near_kernel(nb, *refs):
    list_near, q_ref = refs[:2]
    blocks = refs[2:2 + nb]
    before = refs[2 + nb:5 + nb]
    m_out, l_out, a_out, kv = refs[5 + nb:9 + nb]
    streams = streams_of(refs[9 + nb:-1])
    copies = load_blocks(blocks, kv, refs[-1])
    clear(streams)
    for cp in copies:
        cp.wait()
    all_pairs(list_near, q_ref, kv, streams)
    for s in range(SESS):
        top, total, acc = merge([(m[s], l[s], a[s]) for m, l, a in [before] + streams])
        m_out[s] = top
        l_out[s] = total
        a_out[s] = acc


def far_kernel(nb, *refs):
    list_far, q_ref = refs[:2]
    blocks = refs[2:2 + nb]
    before = refs[2 + nb:5 + nb]
    own = refs[5 + nb]
    outs = refs[6 + nb:9 + nb]
    kv = refs[9 + nb]
    streams = streams_of(refs[10 + nb:-1])
    copies = load_blocks(blocks, kv, refs[-1])
    clear(streams)
    for cp in copies:
        cp.wait()
    all_pairs(list_far, q_ref, kv, streams)
    for s in range(SESS):
        top, total, acc = merge([(m[s], l[s], a[s]) for m, l, a in [before] + streams])
        some = total > 0.0
        safe = jnp.where(some, total, 1.0)
        acc = acc * (1.0 / safe)
        lse = jnp.where(some, top * C2 + jnp.log2(safe), NEG)
        lanes = pl.ds((s % 2) * QROWS, QROWS)
        if s < 2:
            own[pl.ds(0, HD), lanes] = acc
            own[pl.ds(HD, 8), lanes] = jnp.broadcast_to(lse, (8, QROWS))
        else:
            out = outs[s // 2 - 1]
            out[pl.ds(0, HD), lanes] = acc.astype(BF)
            hi = lse.astype(BF).astype(F32)
            mid = (lse - hi).astype(BF).astype(F32)
            low = lse - hi - mid
            row = lax.broadcasted_iota(jnp.int32, (16, QROWS), 0)
            parts = jnp.where(row == 0, hi, jnp.where(row == 1, mid, jnp.where(row == 2, low, 0.0)))
            out[pl.ds(HD, 16), lanes] = parts.astype(BF)


def combine_kernel(head_ref, own, p1, p2, p3, attn, rows_f32):
    lses = [own[HD:HD + 1, :]]
    vals = [own[:HD, :]]
    for p in (p1, p2, p3):
        tail = p[HD:HD + 16, :].astype(F32)
        lses.append(tail[0:1] + tail[1:2] + tail[2:3])
        vals.append(p[:HD, :].astype(F32))
    top = functools.reduce(jnp.maximum, lses)
    ws = [jnp.exp2(x - top) for x in lses]
    inv = 1.0 / sum(ws)
    mixed = sum(v * (w * inv) for v, w in zip(vals, ws))
    rows_f32[...] = mixed.T
    for k in range(8):
        first = (head_ref[0] ^ k) * 64
        for h in range(4):
            block = rows_f32[pl.ds(first + h, 16, stride=4), :]
            attn[pl.ds(k * 16, 16), pl.ds(h * HD, HD)] = block.astype(BF)


def sum_kernel(*refs):
    out = refs[-1]
    out[...] = functools.reduce(jnp.add, [r[...].astype(F32) for r in refs[:-1]]).astype(BF)


VMEM = pl.BlockSpec(memory_space=pltpu.VMEM)
SMEM = pl.BlockSpec(memory_space=pltpu.SMEM)
ANY = pl.BlockSpec(memory_space=pl.ANY)


def stream_scratch():
    return [
        pltpu.VMEM((SESS + 1, 1, QROWS), F32),
        pltpu.VMEM((SESS + 1, 1, QROWS), F32),
        pltpu.VMEM((SESS + 1, HD, QROWS), F32),
    ]


def state_shapes(n):
    return [
        jax.ShapeDtypeStruct((n, 1, QROWS), F32),
        jax.ShapeDtypeStruct((n, 1, QROWS), F32),
        jax.ShapeDtypeStruct((n, HD, QROWS), F32),
    ]


def lists(n):
    return [jax.ShapeDtypeStruct((160,), jnp.int32)] * n


def own_call(*args):
    return pl.pallas_call(
        own_kernel,
        out_shape=[jax.ShapeDtypeStruct((SESS * QROWS, HD), BF)] + lists(3) + state_shapes(SESS),
        in_specs=[SMEM] + [VMEM] * 5 + [ANY] * 2,
        out_specs=[VMEM] + [SMEM] * 3 + [VMEM] * 3,
        scratch_shapes=[
            pltpu.VMEM((64, 128), BF),
            pltpu.VMEM((64, 128), jnp.int32),
            pltpu.SMEM((64, 128), jnp.int32),
            pltpu.SMEM((160,), jnp.int32),
            pltpu.SMEM((160,), jnp.int32),
        ]
        + stream_scratch() * STREAMS
        + [pltpu.SemaphoreType.DMA((1,))],
        compiler_params=pltpu.CompilerParams(vmem_limit_bytes=24 << 20),
        cost_estimate=pl.CostEstimate(flops=2 * 10**9, bytes_accessed=4 << 20, transcendentals=1 << 20),
        name="own_pages",
    )(*args)


def block_scratch(nb):
    return (
        [pltpu.VMEM((8 * nb, 128, HD), BF)]
        + stream_scratch() * STREAMS
        + [pltpu.SemaphoreType.DMA((nb,))]
    )


def near_call(pages, q_all, blocks, state, name):
    nb = len(blocks)
    return pl.pallas_call(
        functools.partial(near_kernel, nb),
        out_shape=state_shapes(SESS),
        in_specs=[SMEM, VMEM] + [ANY] * nb + [VMEM] * 3,
        out_specs=[VMEM] * 3,
        scratch_shapes=block_scratch(nb),
        compiler_params=pltpu.CompilerParams(vmem_limit_bytes=24 << 20),
        cost_estimate=pl.CostEstimate(flops=10**9 * nb, bytes_accessed=4 << 20, transcendentals=1 << 20),
        name=name,
    )(pages, q_all, *blocks, *state)


def far_call(pages, q_all, blocks, state):
    nb = len(blocks)
    return pl.pallas_call(
        functools.partial(far_kernel, nb),
        out_shape=[jax.ShapeDtypeStruct((HD + 8, 2 * QROWS), F32)]
        + [jax.ShapeDtypeStruct((HD + 16, 2 * QROWS), BF)] * 3,
        in_specs=[SMEM, VMEM] + [ANY] * nb + [VMEM] * 3,
        out_specs=[VMEM] * 4,
        scratch_shapes=block_scratch(nb),
        compiler_params=pltpu.CompilerParams(vmem_limit_bytes=24 << 20),
        cost_estimate=pl.CostEstimate(flops=10**9, bytes_accessed=4 << 20, transcendentals=1 << 20),
        name="last_pages",
    )(pages, q_all, *blocks, *state)


def on_device(
    queries, tree_keys, tree_values, prefix_keys, prefix_values, tree_parent, page_table, out_weight
):
    rep = lax.axis_index("rep")
    head = lax.axis_index("head")
    q_own = queries.reshape(2 * QROWS, HD)
    kv = jnp.concatenate([prefix_keys, prefix_values], axis=0).reshape(2 * LOCAL_PAGES, 128, HD)
    up1 = lax.ppermute(kv, "rep", z_perm(1))
    dn1 = lax.ppermute(kv, "rep", z_perm(-1))
    up2 = lax.ppermute(up1, "rep", z_perm(1))
    dn2 = lax.ppermute(dn1, "rep", z_perm(-1))
    sent, local = pl.pallas_call(
        pack_kernel,
        out_shape=[
            jax.ShapeDtypeStruct((2 * QROWS + 16, HD), BF),
            jax.ShapeDtypeStruct((TV_AT + 128, HD), BF),
        ],
        in_specs=[ANY] * 3 + [VMEM] * 2 + [ANY] * 2,
        out_specs=[VMEM] * 2,
        scratch_shapes=[pltpu.SemaphoreType.DMA((4,))],
        compiler_params=pltpu.CompilerParams(vmem_limit_bytes=59 << 20),
        name="pack",
    )(
        q_own, tree_keys.reshape(-1, HD), tree_values.reshape(-1, HD), page_table, tree_parent.reshape(1, -1),
        up1, dn1,
    )
    sents = [lax.ppermute(sent, "rep", group_perm(r)) for r in (1, 2, 3)]
    up3 = lax.ppermute(up2, "rep", z_perm(1))
    dn3 = lax.ppermute(dn2, "rep", z_perm(-1))
    up4 = lax.ppermute(up3, "rep", z_perm(1))

    reps = jnp.arange(32, dtype=jnp.int32)
    same = ((reps ^ rep) & 17) == 0
    step = ((reps >> 1) - (rep >> 1)) & 7
    maps = jnp.full((32,), -(1 << 20), jnp.int32)
    for k, offsets in enumerate(GROUPS):
        for i, o in enumerate(offsets):
            maps = jnp.where(same & (step == o % Z), k * 65536 + i * 8, maps)
    q_all, list_1, list_2, list_3, *state = own_call(maps, local, *sents, kv, up2, dn2)
    state = near_call(list_1, q_all, (up1, dn1, up2, dn2), state, "near_pages")
    state = near_call(list_2, q_all, (up3, dn3), state, "far_pages")
    own, p1, p2, p3 = far_call(list_3, q_all, (up4,), state)
    back = [lax.ppermute(p, "rep", group_perm(r)) for r, p in ((1, p1), (2, p2), (3, p3))]
    width = out_weight.shape[1]
    attn = pl.pallas_call(
        combine_kernel,
        out_shape=jax.ShapeDtypeStruct((128, 512), BF),
        in_specs=[SMEM] + [VMEM] * 4,
        out_specs=VMEM,
        scratch_shapes=[pltpu.VMEM((2 * QROWS, HD), F32)],
        compiler_params=pltpu.CompilerParams(vmem_limit_bytes=24 << 20),
        cost_estimate=pl.CostEstimate(flops=10**6, bytes_accessed=1 << 20, transcendentals=4096),
        name="combine",
    )(head.reshape(1).astype(jnp.int32), own, *back)
    rows = jnp.dot(attn, out_weight, preferred_element_type=F32).astype(BF)
    parts = [rows[k * 16:(k + 1) * 16] for k in range(8)]
    terms = [lax.ppermute(parts[k], "head", [(i, i ^ k) for i in range(8)]) for k in (1, 3, 4, 2, 5, 7, 6)]
    return pl.pallas_call(
        sum_kernel,
        out_shape=jax.ShapeDtypeStruct((16, width), BF),
        in_specs=[VMEM] * 8,
        out_specs=VMEM,
        compiler_params=pltpu.CompilerParams(vmem_limit_bytes=24 << 20),
        name="sum_heads",
    )(parts[0], *terms)


def solution(mesh):
    in_specs = (
        P("rep", "head", None),
        P("rep", "head", None),
        P("rep", "head", None),
        P("rep", "head", None, None),
        P("rep", "head", None, None),
        P("rep"),
        P("rep", None),
        P("head", None),
    )
    out_specs = P(("rep", "head"), None)
    return jax.shard_map(
        on_device, mesh=mesh, in_specs=in_specs, out_specs=out_specs, check_vma=False
    )
```

```python
import functools
import math

import jax
import jax.numpy as jnp
from jax import lax
from jax.experimental import pallas as pl
from jax.experimental.pallas import tpu as pltpu
from jax.sharding import PartitionSpec as P

NEG = -1e30
Z = 8
GROUP = 4
LOCAL_PAGES = 4
TK_AT = 528
TV_AT = 656
PAGES_AT = 784
TREE = 64
QROWS = 256
HD = 128
SESS = 8
C2 = (HD ** -0.5) * math.log2(math.e)
BF = jnp.bfloat16
F32 = jnp.float32

STREAMS = 4
GROUPS = ((0,), (-1, 1, -2, 2), (-3, 3), (4,))


def rep_of(xh, z, c):
    return xh * 16 + (z % Z) * 2 + c


def z_perm(k):
    return [(rep_of(a, z, c), rep_of(a, z + k, c)) for a in range(2) for z in range(Z) for c in range(2)]


def group_perm(r):
    return [(rep_of(a, z, c), rep_of(a ^ (r >> 1), z, c ^ (r & 1))) for a in range(2) for z in range(Z) for c in range(2)]


def pair_steps(entries, q_ref, page, streams):
    at = [(e >> 8, e & 255) for e in entries]
    scores = [
        lax.dot_general(page(k), q_ref[pl.ds(pl.multiple_of((s & (SESS - 1)) * QROWS, QROWS), QROWS), :], (((1,), (1,)), ((), ())), preferred_element_type=F32)
        for s, k in at
    ]
    olds = [m[s] for (s, _), (m, _, _) in zip(at, streams)]
    news = [jnp.maximum(o, jnp.max(x, axis=0, keepdims=True)) for o, x in zip(olds, scores)]
    probs = [jnp.exp2(x * C2 - n * C2) for x, n in zip(scores, news)]
    fixes = [jnp.exp2((o - n) * C2) for o, n in zip(olds, news)]
    parts = [
        lax.dot_general(
            page(k + LOCAL_PAGES), p.astype(BF), (((0,), (0,)), ((), ())), preferred_element_type=F32
        )
        for (_, k), p in zip(at, probs)
    ]
    for (s, _), n, p, fix, part, (m_ref, l_ref, a_ref) in zip(at, news, probs, fixes, parts, streams):
        m_ref[s] = n
        l_ref[s] = l_ref[s] * fix + jnp.sum(p, axis=0, keepdims=True)
        a_ref[s] = a_ref[s] * fix + part


def all_pairs(entries, q_ref, page, streams):
    ns = len(streams)

    @pl.loop(0, (entries[0] + ns - 1) >> (ns.bit_length() - 1))
    def _(i):
        pair_steps([entries[ns * i + r + 1] for r in range(ns)], q_ref, page, streams)


def streams_of(refs):
    return [tuple(refs[3 * r:3 * r + 3]) for r in range(STREAMS)]


def clear(streams):
    for m_ref, l_ref, a_ref in streams:
        m_ref[...] = jnp.full(m_ref.shape, NEG, F32)
        l_ref[...] = jnp.zeros(l_ref.shape, F32)
        a_ref[...] = jnp.zeros(a_ref.shape, F32)


def merge(states):
    top = functools.reduce(jnp.maximum, [m for m, _, _ in states])
    ws = [jnp.exp2((m - top) * C2) for m, _, _ in states]
    total = sum(w * l for w, (_, l, _) in zip(ws, states))
    acc = sum(w * a for w, (_, _, a) in zip(ws, states))
    return top, total, acc


def pack_kernel(q, tk, tv, pk, pv, table, parent, kv, sent, local, sems):
    del kv
    copies = [
        pltpu.make_async_copy(q, sent.at[pl.ds(0, 2 * QROWS)], sems.at[0]),
        pltpu.make_async_copy(q, local.at[pl.ds(0, 2 * QROWS)], sems.at[1]),
        pltpu.make_async_copy(tk, local.at[pl.ds(TK_AT, 128)], sems.at[2]),
        pltpu.make_async_copy(tv, local.at[pl.ds(TV_AT, 128)], sems.at[3]),
        pltpu.make_async_copy(pk, local.at[pl.ds(PAGES_AT, LOCAL_PAGES * 128)], sems.at[4]),
        pltpu.make_async_copy(pv, local.at[pl.ds(PAGES_AT + LOCAL_PAGES * 128, LOCAL_PAGES * 128)], sems.at[5]),
    ]
    for cp in copies:
        cp.start()
    ids = table[...].astype(F32)
    row = lax.broadcasted_iota(jnp.int32, (16, 128), 0)
    above = parent[...].astype(F32)
    tail = pl.ds(2 * QROWS, 16)
    sent[tail, :] = jnp.zeros((16, 128), BF)
    local[tail, :] = jnp.where(row == 2, above, 0.0).astype(BF)
    row = row[:, :16]
    pages = jnp.where(row == 0, ids[0:1, :], jnp.where(row == 1, ids[1:2, :], 0.0))
    sent[tail, :16] = pages.astype(BF)
    local[tail, :16] = jnp.where(row == 2, above[:, :16], pages).astype(BF)
    for cp in copies:
        cp.wait()


def own_kernel(maps, local, s1, s2, s3, up1, dn1, q_out, *refs):
    del up1, dn1
    lists = refs[:3]
    m_out, l_out, a_out, tails, ids, tbl, list_own, found = refs[3:11]
    lists = (list_own,) + lists
    streams = streams_of(refs[11:-1])
    sems = refs[-1]
    sents = (local, s1, s2, s3)
    for r, x in enumerate(sents):
        tails[pl.ds(r * 16, 16), :] = x[pl.ds(2 * QROWS, 16), :]
    ids[...] = tails[...].astype(F32).astype(jnp.int32)
    to_scalar = pltpu.make_async_copy(ids, tbl, sems.at[0])
    to_scalar.start()
    for r, x in enumerate(sents):
        q_out[pl.ds(r * 2 * QROWS, 2 * QROWS), :] = x[pl.ds(0, 2 * QROWS), :]
    clear(streams)
    both = 2 * TREE
    row = lax.broadcasted_iota(jnp.int32, (both, both), 0)
    lane = lax.broadcasted_iota(jnp.int32, (both, both), 1)
    above = ids[2:3, :] + jnp.where(lax.broadcasted_iota(jnp.int32, (1, both), 1) >= TREE, TREE, 0)
    reach = jnp.minimum((row == lane).astype(F32) + (row == above).astype(F32), 1.0)
    for _ in range(7):
        half = reach.astype(BF)
        reach = jnp.minimum(jnp.dot(half, half, preferred_element_type=F32), 1.0)
    half = reach.astype(BF)
    tree_row = lax.broadcasted_iota(jnp.int32, (both, QROWS), 0)
    of_query = lax.shift_right_logical(lax.broadcasted_iota(jnp.int32, (both, QROWS), 1), 2)
    m0, l0, a0 = streams[0]
    for s in range(2):
        widen = (tree_row == of_query + s * TREE).astype(BF)
        seen = jnp.dot(half[s * TREE:(s + 1) * TREE, :], widen, preferred_element_type=F32)
        scores = lax.dot_general(
            local[pl.ds(TK_AT + s * TREE, TREE), :],
            local[pl.ds(s * QROWS, QROWS), :],
            (((1,), (1,)), ((), ())),
            preferred_element_type=F32,
        )
        scores = jnp.where(seen > 0.5, scores, NEG)
        top = jnp.max(scores, axis=0, keepdims=True)
        probs = jnp.exp2(scores * C2 - top * C2)
        m0[s] = top
        l0[s] = jnp.sum(probs, axis=0, keepdims=True)
        a0[s] = lax.dot_general(
            local[pl.ds(TV_AT + s * TREE, TREE), :],
            probs.astype(BF),
            (((0,), (0,)), ((), ())),
            preferred_element_type=F32,
        )
    to_scalar.wait()

    def scan(r, n):
        for half in range(2):
            pages = [tbl[r * 16 + half, j] for j in range(16)]
            at = [maps[p >> 2] for p in pages]
            for p, where in zip(pages, at):
                found[n] = (r * 2 + half) * 256 + (p & 3) + where
                n = n + (where >= 0).astype(jnp.int32)
        return n

    total = lax.fori_loop(0, GROUP, scan, jnp.int32(0))

    def sort(i, counts):
        entry = found[i]
        kind = entry >> 16
        out = []
        for k in range(4):
            lists[k][counts[k] + 1] = entry & 65535
            out.append(counts[k] + (kind == k).astype(jnp.int32))
        return tuple(out)

    counts = lax.fori_loop(0, total, sort, (jnp.int32(0),) * 4)
    for k in range(4):
        lists[k][0] = counts[k]
        for r in range(STREAMS - 1):
            lists[k][counts[k] + 1 + r] = jnp.int32(SESS * 256)
    all_pairs(
        list_own, q_out, lambda i: local[pl.ds(pl.multiple_of(PAGES_AT + i * 128, 16), 128), :], streams
    )
    for s in range(SESS):
        top, total, acc = merge([(m[s], l[s], a[s]) for m, l, a in streams])
        m_out[s] = top
        l_out[s] = total
        a_out[s] = acc


def load_blocks(blocks, kv, sems):
    copies = [pltpu.make_async_copy(b, kv.at[pl.ds(i * 8, 8)], sems.at[i]) for i, b in enumerate(blocks)]
    for cp in copies:
        cp.start()
    return copies


def near_kernel(nb, *refs):
    list_near, q_ref = refs[:2]
    blocks = refs[2:2 + nb]
    before = refs[2 + nb:5 + nb]
    m_out, l_out, a_out, kv = refs[5 + nb:9 + nb]
    streams = streams_of(refs[9 + nb:-1])
    copies = load_blocks(blocks, kv, refs[-1])
    clear(streams)
    for cp in copies:
        cp.wait()
    all_pairs(list_near, q_ref, lambda i: kv[i], streams)
    for s in range(SESS):
        top, total, acc = merge([(m[s], l[s], a[s]) for m, l, a in [before] + streams])
        m_out[s] = top
        l_out[s] = total
        a_out[s] = acc


def far_kernel(nb, *refs):
    list_far, q_ref = refs[:2]
    blocks = refs[2:2 + nb]
    before = refs[2 + nb:5 + nb]
    own = refs[5 + nb]
    outs = refs[6 + nb:9 + nb]
    kv = refs[9 + nb]
    streams = streams_of(refs[10 + nb:-1])
    copies = load_blocks(blocks, kv, refs[-1])
    clear(streams)
    for cp in copies:
        cp.wait()
    all_pairs(list_far, q_ref, lambda i: kv[i], streams)
    for s in range(SESS):
        top, total, acc = merge([(m[s], l[s], a[s]) for m, l, a in [before] + streams])
        some = total > 0.0
        safe = jnp.where(some, total, 1.0)
        acc = acc * (1.0 / safe)
        lse = jnp.where(some, top * C2 + jnp.log2(safe), NEG)
        lanes = pl.ds((s % 2) * QROWS, QROWS)
        if s < 2:
            own[pl.ds(0, HD), lanes] = acc
            own[pl.ds(HD, 8), lanes] = jnp.broadcast_to(lse, (8, QROWS))
        else:
            out = outs[s // 2 - 1]
            out[pl.ds(0, HD), lanes] = acc.astype(BF)
            hi = lse.astype(BF).astype(F32)
            mid = (lse - hi).astype(BF).astype(F32)
            low = lse - hi - mid
            row = lax.broadcasted_iota(jnp.int32, (16, QROWS), 0)
            parts = jnp.where(row == 0, hi, jnp.where(row == 1, mid, jnp.where(row == 2, low, 0.0)))
            out[pl.ds(HD, 16), lanes] = parts.astype(BF)


def combine_kernel(head_ref, own, p1, p2, p3, attn, rows_f32):
    lses = [own[HD:HD + 1, :]]
    vals = [own[:HD, :]]
    for p in (p1, p2, p3):
        tail = p[HD:HD + 16, :].astype(F32)
        lses.append(tail[0:1] + tail[1:2] + tail[2:3])
        vals.append(p[:HD, :].astype(F32))
    top = functools.reduce(jnp.maximum, lses)
    ws = [jnp.exp2(x - top) for x in lses]
    inv = 1.0 / sum(ws)
    mixed = sum(v * (w * inv) for v, w in zip(vals, ws))
    rows_f32[...] = mixed.T
    for k in range(8):
        first = (head_ref[0] ^ k) * 64
        for h in range(4):
            block = rows_f32[pl.ds(first + h, 16, stride=4), :]
            attn[pl.ds(k * 16, 16), pl.ds(h * HD, HD)] = block.astype(BF)


def sum_kernel(*refs):
    out = refs[-1]
    out[...] = functools.reduce(jnp.add, [r[...].astype(F32) for r in refs[:-1]]).astype(BF)


VMEM = pl.BlockSpec(memory_space=pltpu.VMEM)
SMEM = pl.BlockSpec(memory_space=pltpu.SMEM)
ANY = pl.BlockSpec(memory_space=pl.ANY)


def stream_scratch():
    return [
        pltpu.VMEM((SESS + 1, 1, QROWS), F32),
        pltpu.VMEM((SESS + 1, 1, QROWS), F32),
        pltpu.VMEM((SESS + 1, HD, QROWS), F32),
    ]


def state_shapes(n):
    return [
        jax.ShapeDtypeStruct((n, 1, QROWS), F32),
        jax.ShapeDtypeStruct((n, 1, QROWS), F32),
        jax.ShapeDtypeStruct((n, HD, QROWS), F32),
    ]


def lists(n):
    return [jax.ShapeDtypeStruct((160,), jnp.int32)] * n


def own_call(*args):
    return pl.pallas_call(
        own_kernel,
        out_shape=[jax.ShapeDtypeStruct((SESS * QROWS, HD), BF)] + lists(3) + state_shapes(SESS),
        in_specs=[SMEM] + [VMEM] * 4 + [ANY] * 2,
        out_specs=[VMEM] + [SMEM] * 3 + [VMEM] * 3,
        scratch_shapes=[
            pltpu.VMEM((64, 128), BF),
            pltpu.VMEM((64, 128), jnp.int32),
            pltpu.SMEM((64, 128), jnp.int32),
            pltpu.SMEM((160,), jnp.int32),
            pltpu.SMEM((160,), jnp.int32),
        ]
        + stream_scratch() * STREAMS
        + [pltpu.SemaphoreType.DMA((1,))],
        compiler_params=pltpu.CompilerParams(vmem_limit_bytes=24 << 20),
        cost_estimate=pl.CostEstimate(flops=2 * 10**9, bytes_accessed=4 << 20, transcendentals=1 << 20),
        name="own_pages",
    )(*args)


def block_scratch(nb):
    return (
        [pltpu.VMEM((8 * nb, 128, HD), BF)]
        + stream_scratch() * STREAMS
        + [pltpu.SemaphoreType.DMA((nb,))]
    )


def near_call(pages, q_all, blocks, state, name):
    nb = len(blocks)
    return pl.pallas_call(
        functools.partial(near_kernel, nb),
        out_shape=state_shapes(SESS),
        in_specs=[SMEM, VMEM] + [ANY] * nb + [VMEM] * 3,
        out_specs=[VMEM] * 3,
        scratch_shapes=block_scratch(nb),
        compiler_params=pltpu.CompilerParams(vmem_limit_bytes=24 << 20),
        cost_estimate=pl.CostEstimate(flops=10**9 * nb, bytes_accessed=4 << 20, transcendentals=1 << 20),
        name=name,
    )(pages, q_all, *blocks, *state)


def far_call(pages, q_all, blocks, state):
    nb = len(blocks)
    return pl.pallas_call(
        functools.partial(far_kernel, nb),
        out_shape=[jax.ShapeDtypeStruct((HD + 8, 2 * QROWS), F32)]
        + [jax.ShapeDtypeStruct((HD + 16, 2 * QROWS), BF)] * 3,
        in_specs=[SMEM, VMEM] + [ANY] * nb + [VMEM] * 3,
        out_specs=[VMEM] * 4,
        scratch_shapes=block_scratch(nb),
        compiler_params=pltpu.CompilerParams(vmem_limit_bytes=24 << 20),
        cost_estimate=pl.CostEstimate(flops=10**9, bytes_accessed=4 << 20, transcendentals=1 << 20),
        name="last_pages",
    )(pages, q_all, *blocks, *state)


def on_device(
    queries, tree_keys, tree_values, prefix_keys, prefix_values, tree_parent, page_table, out_weight
):
    rep = lax.axis_index("rep")
    head = lax.axis_index("head")
    q_own = queries.reshape(2 * QROWS, HD)
    kv = jnp.concatenate([prefix_keys, prefix_values], axis=0).reshape(2 * LOCAL_PAGES, 128, HD)
    up1 = lax.ppermute(kv, "rep", z_perm(1))
    dn1 = lax.ppermute(kv, "rep", z_perm(-1))
    up2 = lax.ppermute(up1, "rep", z_perm(1))
    dn2 = lax.ppermute(dn1, "rep", z_perm(-1))
    sent, local = pl.pallas_call(
        pack_kernel,
        out_shape=[
            jax.ShapeDtypeStruct((2 * QROWS + 16, HD), BF),
            jax.ShapeDtypeStruct((PAGES_AT + 2 * LOCAL_PAGES * 128, HD), BF),
        ],
        in_specs=[ANY] * 5 + [VMEM] * 2 + [ANY],
        out_specs=[VMEM] * 2,
        scratch_shapes=[pltpu.SemaphoreType.DMA((6,))],
        compiler_params=pltpu.CompilerParams(vmem_limit_bytes=59 << 20),
        name="pack",
    )(
        q_own, tree_keys.reshape(-1, HD), tree_values.reshape(-1, HD),
        prefix_keys.reshape(-1, HD), prefix_values.reshape(-1, HD), page_table, tree_parent.reshape(1, -1),
        kv,
    )
    sents = [lax.ppermute(sent, "rep", group_perm(r)) for r in (1, 2, 3)]
    up3 = lax.ppermute(up2, "rep", z_perm(1))
    dn3 = lax.ppermute(dn2, "rep", z_perm(-1))
    held = jnp.where((rep & 1) == 0, up2, dn2)
    opposite = lax.ppermute(
        held, "rep", [(rep_of(a, z, c), rep_of(a, z + 2 - 4 * c, c)) for a in range(2) for z in range(Z) for c in range(2)]
    )

    reps = jnp.arange(32, dtype=jnp.int32)
    same = ((reps ^ rep) & 17) == 0
    step = ((reps >> 1) - (rep >> 1)) & 7
    maps = jnp.full((32,), -(1 << 20), jnp.int32)
    for k, offsets in enumerate(GROUPS):
        for i, o in enumerate(offsets):
            maps = jnp.where(same & (step == o % Z), k * 65536 + i * 8, maps)
    q_all, list_1, list_2, list_3, *state = own_call(maps, local, *sents, up1, dn1)
    state = near_call(list_1, q_all, (up1, dn1, up2, dn2), state, "near_pages")
    state = near_call(list_2, q_all, (up3, dn3), state, "far_pages")
    own, p1, p2, p3 = far_call(list_3, q_all, (opposite,), state)
    back = [lax.ppermute(p, "rep", group_perm(r)) for r, p in ((3, p3), (2, p2), (1, p1))]
    width = out_weight.shape[1]
    attn = pl.pallas_call(
        combine_kernel,
        out_shape=jax.ShapeDtypeStruct((128, 512), BF),
        in_specs=[SMEM] + [VMEM] * 4,
        out_specs=VMEM,
        scratch_shapes=[pltpu.VMEM((2 * QROWS, HD), F32)],
        compiler_params=pltpu.CompilerParams(vmem_limit_bytes=24 << 20),
        cost_estimate=pl.CostEstimate(flops=10**6, bytes_accessed=1 << 20, transcendentals=4096),
        name="combine",
    )(head.reshape(1).astype(jnp.int32), own, *back)
    rows = jnp.dot(attn, out_weight, preferred_element_type=F32).astype(BF)
    parts = [rows[k * 16:(k + 1) * 16] for k in range(8)]
    terms = [lax.ppermute(parts[k], "head", [(i, i ^ k) for i in range(8)]) for k in (1, 3, 4, 2, 5, 7, 6)]
    return pl.pallas_call(
        sum_kernel,
        out_shape=jax.ShapeDtypeStruct((16, width), BF),
        in_specs=[VMEM] * 8,
        out_specs=VMEM,
        compiler_params=pltpu.CompilerParams(vmem_limit_bytes=24 << 20),
        name="sum_heads",
    )(parts[0], *terms)


def solution(mesh):
    in_specs = (
        P("rep", "head", None),
        P("rep", "head", None),
        P("rep", "head", None),
        P("rep", "head", None, None),
        P("rep", "head", None, None),
        P("rep"),
        P("rep", None),
        P("head", None),
    )
    out_specs = P(("rep", "head"), None)
    return jax.shard_map(
        on_device, mesh=mesh, in_specs=in_specs, out_specs=out_specs, check_vma=False
    )
```

```python
import functools
import math

import jax
import jax.numpy as jnp
from jax import lax
from jax.experimental import pallas as pl
from jax.experimental.pallas import tpu as pltpu
from jax.sharding import PartitionSpec as P

NEG = -1e30
Z = 8
GROUP = 4
LOCAL_PAGES = 4
TK_AT = 528
TV_AT = 656
BLOCK = 1024
PAGES_AT = 784
TREE = 64
QROWS = 256
HD = 128
SESS = 8
C2 = (HD ** -0.5) * math.log2(math.e)
BF = jnp.bfloat16
F32 = jnp.float32

STREAMS = 4
GROUPS = ((0, -1, 1, -2, 2), (-3, 3, 4))


def rep_of(xh, z, c):
    return xh * 16 + (z % Z) * 2 + c


def z_perm(k):
    return [(rep_of(a, z, c), rep_of(a, z + k, c)) for a in range(2) for z in range(Z) for c in range(2)]


def group_perm(r):
    return [(rep_of(a, z, c), rep_of(a ^ (r >> 1), z, c ^ (r & 1))) for a in range(2) for z in range(Z) for c in range(2)]


def page(kv, i):
    return kv[pl.ds(pl.multiple_of(i * 128, 128), 128), :]


def pair_steps(entries, q_ref, kv, streams):
    at = [(e >> 8, e & 255) for e in entries]
    scores = [
        lax.dot_general(page(kv, k), q_ref[pl.ds(pl.multiple_of((s & (SESS - 1)) * QROWS, QROWS), QROWS), :], (((1,), (1,)), ((), ())), preferred_element_type=F32)
        for s, k in at
    ]
    olds = [m[s] for (s, _), (m, _, _) in zip(at, streams)]
    news = [jnp.maximum(o, jnp.max(x, axis=0, keepdims=True)) for o, x in zip(olds, scores)]
    probs = [jnp.exp2(x * C2 - n * C2) for x, n in zip(scores, news)]
    fixes = [jnp.exp2((o - n) * C2) for o, n in zip(olds, news)]
    parts = [
        lax.dot_general(
            page(kv, k + LOCAL_PAGES), p.astype(BF), (((0,), (0,)), ((), ())), preferred_element_type=F32
        )
        for (_, k), p in zip(at, probs)
    ]
    for (s, _), n, p, fix, part, (m_ref, l_ref, a_ref) in zip(at, news, probs, fixes, parts, streams):
        m_ref[s] = n
        l_ref[s] = l_ref[s] * fix + jnp.sum(p, axis=0, keepdims=True)
        a_ref[s] = a_ref[s] * fix + part


def all_pairs(entries, q_ref, kv, streams):
    ns = len(streams)

    @pl.loop(0, (entries[0] + ns - 1) >> (ns.bit_length() - 1))
    def _(i):
        pair_steps([entries[ns * i + r + 1] for r in range(ns)], q_ref, kv, streams)


def streams_of(refs):
    return [tuple(refs[3 * r:3 * r + 3]) for r in range(STREAMS)]


def clear(streams):
    for m_ref, l_ref, a_ref in streams:
        m_ref[...] = jnp.full(m_ref.shape, NEG, F32)
        l_ref[...] = jnp.zeros(l_ref.shape, F32)
        a_ref[...] = jnp.zeros(a_ref.shape, F32)


def merge(states):
    top = functools.reduce(jnp.maximum, [m for m, _, _ in states])
    ws = [jnp.exp2((m - top) * C2) for m, _, _ in states]
    total = sum(w * l for w, (_, l, _) in zip(ws, states))
    acc = sum(w * a for w, (_, _, a) in zip(ws, states))
    return top, total, acc


def pack_kernel(q, tk, tv, pk, pv, table, parent, kv, sent, local, sems):
    del kv
    copies = [
        pltpu.make_async_copy(q, sent.at[pl.ds(0, 2 * QROWS)], sems.at[0]),
        pltpu.make_async_copy(q, local.at[pl.ds(0, 2 * QROWS)], sems.at[1]),
        pltpu.make_async_copy(tk, local.at[pl.ds(TK_AT, 128)], sems.at[2]),
        pltpu.make_async_copy(tv, local.at[pl.ds(TV_AT, 128)], sems.at[3]),
        pltpu.make_async_copy(pk, local.at[pl.ds(PAGES_AT, LOCAL_PAGES * 128)], sems.at[4]),
        pltpu.make_async_copy(pv, local.at[pl.ds(PAGES_AT + LOCAL_PAGES * 128, LOCAL_PAGES * 128)], sems.at[5]),
    ]
    for cp in copies:
        cp.start()
    ids = table[...].astype(F32)
    row = lax.broadcasted_iota(jnp.int32, (16, 128), 0)
    above = parent[...].astype(F32)
    tail = pl.ds(2 * QROWS, 16)
    sent[tail, :] = jnp.zeros((16, 128), BF)
    local[tail, :] = jnp.where(row == 2, above, 0.0).astype(BF)
    row = row[:, :16]
    pages = jnp.where(row == 0, ids[0:1, :], jnp.where(row == 1, ids[1:2, :], 0.0))
    sent[tail, :16] = pages.astype(BF)
    local[tail, :16] = jnp.where(row == 2, above[:, :16], pages).astype(BF)
    for cp in copies:
        cp.wait()


def near_kernel(maps, local, s1, s2, s3, up1, dn1, up2, dn2, q_out, list_far, *refs):
    m_out, l_out, a_out, tails, ids, tbl, list_near, found, kv = refs[:9]
    lists = (list_near, list_far)
    streams = streams_of(refs[9:-1])
    sems = refs[-1]
    sents = (local, s1, s2, s3)
    for r, x in enumerate(sents):
        tails[pl.ds(r * 16, 16), :] = x[pl.ds(2 * QROWS, 16), :]
    ids[...] = tails[...].astype(F32).astype(jnp.int32)
    to_scalar = pltpu.make_async_copy(ids, tbl, sems.at[0])
    to_scalar.start()
    copies = load_blocks(
        [local.at[pl.ds(PAGES_AT, BLOCK)], up1, dn1, up2, dn2], kv, [sems.at[i + 1] for i in range(5)]
    )
    for r, x in enumerate(sents):
        q_out[pl.ds(r * 2 * QROWS, 2 * QROWS), :] = x[pl.ds(0, 2 * QROWS), :]
    clear(streams)
    both = 2 * TREE
    row = lax.broadcasted_iota(jnp.int32, (both, both), 0)
    lane = lax.broadcasted_iota(jnp.int32, (both, both), 1)
    above = ids[2:3, :] + jnp.where(lax.broadcasted_iota(jnp.int32, (1, both), 1) >= TREE, TREE, 0)
    reach = jnp.minimum((row == lane).astype(F32) + (row == above).astype(F32), 1.0)
    for _ in range(7):
        half = reach.astype(BF)
        reach = jnp.minimum(jnp.dot(half, half, preferred_element_type=F32), 1.0)
    half = reach.astype(BF)
    tree_row = lax.broadcasted_iota(jnp.int32, (both, QROWS), 0)
    of_query = lax.shift_right_logical(lax.broadcasted_iota(jnp.int32, (both, QROWS), 1), 2)
    m0, l0, a0 = streams[0]
    for s in range(2):
        widen = (tree_row == of_query + s * TREE).astype(BF)
        seen = jnp.dot(half[s * TREE:(s + 1) * TREE, :], widen, preferred_element_type=F32)
        scores = lax.dot_general(
            local[pl.ds(TK_AT + s * TREE, TREE), :],
            local[pl.ds(s * QROWS, QROWS), :],
            (((1,), (1,)), ((), ())),
            preferred_element_type=F32,
        )
        scores = jnp.where(seen > 0.5, scores, NEG)
        top = jnp.max(scores, axis=0, keepdims=True)
        probs = jnp.exp2(scores * C2 - top * C2)
        m0[s] = top
        l0[s] = jnp.sum(probs, axis=0, keepdims=True)
        a0[s] = lax.dot_general(
            local[pl.ds(TV_AT + s * TREE, TREE), :],
            probs.astype(BF),
            (((0,), (0,)), ((), ())),
            preferred_element_type=F32,
        )
    to_scalar.wait()

    def scan(r, n):
        for half in range(2):
            pages = [tbl[r * 16 + half, j] for j in range(16)]
            at = [maps[p >> 2] for p in pages]
            for p, where in zip(pages, at):
                found[n] = (r * 2 + half) * 256 + (p & 3) + where
                n = n + (where >= 0).astype(jnp.int32)
        return n

    total = lax.fori_loop(0, GROUP, scan, jnp.int32(0))

    def sort(i, counts):
        entry = found[i]
        kind = entry >> 16
        out = []
        for k in range(2):
            lists[k][counts[k] + 1] = entry & 65535
            out.append(counts[k] + (kind == k).astype(jnp.int32))
        return tuple(out)

    counts = lax.fori_loop(0, total, sort, (jnp.int32(0),) * 2)
    for k in range(2):
        lists[k][0] = counts[k]
        for r in range(STREAMS - 1):
            lists[k][counts[k] + 1 + r] = jnp.int32(SESS * 256)
    for cp in copies:
        cp.wait()
    all_pairs(list_near, q_out, kv, streams)
    for s in range(SESS):
        top, total, acc = merge([(m[s], l[s], a[s]) for m, l, a in streams])
        m_out[s] = top
        l_out[s] = total
        a_out[s] = acc


def load_blocks(blocks, kv, sems):
    copies = [pltpu.make_async_copy(b, kv.at[pl.ds(i * BLOCK, BLOCK)], sem) for i, (b, sem) in enumerate(zip(blocks, sems))]
    for cp in copies:
        cp.start()
    return copies


def far_kernel(nb, *refs):
    list_far, q_ref = refs[:2]
    blocks = refs[2:2 + nb]
    before = refs[2 + nb:5 + nb]
    own = refs[5 + nb]
    outs = refs[6 + nb:9 + nb]
    kv = refs[9 + nb]
    streams = streams_of(refs[10 + nb:-1])
    copies = load_blocks(blocks, kv, [refs[-1].at[i] for i in range(nb)])
    clear(streams)
    for cp in copies:
        cp.wait()
    all_pairs(list_far, q_ref, kv, streams)
    for s in range(SESS):
        top, total, acc = merge([(m[s], l[s], a[s]) for m, l, a in [before] + streams])
        some = total > 0.0
        safe = jnp.where(some, total, 1.0)
        acc = acc * (1.0 / safe)
        lse = jnp.where(some, top * C2 + jnp.log2(safe), NEG)
        lanes = pl.ds((s % 2) * QROWS, QROWS)
        if s < 2:
            own[pl.ds(0, HD), lanes] = acc
            own[pl.ds(HD, 8), lanes] = jnp.broadcast_to(lse, (8, QROWS))
        else:
            out = outs[s // 2 - 1]
            out[pl.ds(0, HD), lanes] = acc.astype(BF)
            hi = lse.astype(BF).astype(F32)
            mid = (lse - hi).astype(BF).astype(F32)
            low = lse - hi - mid
            row = lax.broadcasted_iota(jnp.int32, (16, QROWS), 0)
            parts = jnp.where(row == 0, hi, jnp.where(row == 1, mid, jnp.where(row == 2, low, 0.0)))
            out[pl.ds(HD, 16), lanes] = parts.astype(BF)


def combine_kernel(head_ref, own, p1, p2, p3, attn, rows_f32):
    lses = [own[HD:HD + 1, :]]
    vals = [own[:HD, :]]
    for p in (p1, p2, p3):
        tail = p[HD:HD + 16, :].astype(F32)
        lses.append(tail[0:1] + tail[1:2] + tail[2:3])
        vals.append(p[:HD, :].astype(F32))
    top = functools.reduce(jnp.maximum, lses)
    ws = [jnp.exp2(x - top) for x in lses]
    inv = 1.0 / sum(ws)
    mixed = sum(v * (w * inv) for v, w in zip(vals, ws))
    rows_f32[...] = mixed.T
    for k in range(8):
        first = (head_ref[0] ^ k) * 64
        for h in range(4):
            block = rows_f32[pl.ds(first + h, 16, stride=4), :]
            attn[pl.ds(k * 16, 16), pl.ds(h * HD, HD)] = block.astype(BF)


def sum_kernel(*refs):
    out = refs[-1]
    out[...] = functools.reduce(jnp.add, [r[...].astype(F32) for r in refs[:-1]]).astype(BF)


VMEM = pl.BlockSpec(memory_space=pltpu.VMEM)
SMEM = pl.BlockSpec(memory_space=pltpu.SMEM)
ANY = pl.BlockSpec(memory_space=pl.ANY)


def stream_scratch():
    return [
        pltpu.VMEM((SESS + 1, 1, QROWS), F32),
        pltpu.VMEM((SESS + 1, 1, QROWS), F32),
        pltpu.VMEM((SESS + 1, HD, QROWS), F32),
    ]


def state_shapes(n):
    return [
        jax.ShapeDtypeStruct((n, 1, QROWS), F32),
        jax.ShapeDtypeStruct((n, 1, QROWS), F32),
        jax.ShapeDtypeStruct((n, HD, QROWS), F32),
    ]


def near_call(*args):
    return pl.pallas_call(
        near_kernel,
        out_shape=[jax.ShapeDtypeStruct((SESS * QROWS, HD), BF), jax.ShapeDtypeStruct((160,), jnp.int32)]
        + state_shapes(SESS),
        in_specs=[SMEM] + [VMEM] * 4 + [ANY] * 4,
        out_specs=[VMEM, SMEM] + [VMEM] * 3,
        scratch_shapes=[
            pltpu.VMEM((64, 128), BF),
            pltpu.VMEM((64, 128), jnp.int32),
            pltpu.SMEM((64, 128), jnp.int32),
            pltpu.SMEM((160,), jnp.int32),
            pltpu.SMEM((160,), jnp.int32),
            pltpu.VMEM((5 * BLOCK, HD), BF),
        ]
        + stream_scratch() * STREAMS
        + [pltpu.SemaphoreType.DMA((6,))],
        compiler_params=pltpu.CompilerParams(vmem_limit_bytes=24 << 20),
        cost_estimate=pl.CostEstimate(flops=4 * 10**9, bytes_accessed=4 << 20, transcendentals=1 << 20),
        name="near_pages",
    )(*args)


def far_call(pages, q_all, blocks, state):
    nb = len(blocks)
    return pl.pallas_call(
        functools.partial(far_kernel, nb),
        out_shape=[jax.ShapeDtypeStruct((HD + 8, 2 * QROWS), F32)]
        + [jax.ShapeDtypeStruct((HD + 16, 2 * QROWS), BF)] * 3,
        in_specs=[SMEM, VMEM] + [ANY] * nb + [VMEM] * 3,
        out_specs=[VMEM] * 4,
        scratch_shapes=[pltpu.VMEM((nb * BLOCK, HD), BF)]
        + stream_scratch() * STREAMS
        + [pltpu.SemaphoreType.DMA((nb,))],
        compiler_params=pltpu.CompilerParams(vmem_limit_bytes=24 << 20),
        cost_estimate=pl.CostEstimate(flops=10**9, bytes_accessed=4 << 20, transcendentals=1 << 20),
        name="far_pages",
    )(pages, q_all, *blocks, *state)


def on_device(
    queries, tree_keys, tree_values, prefix_keys, prefix_values, tree_parent, page_table, out_weight
):
    rep = lax.axis_index("rep")
    head = lax.axis_index("head")
    q_own = queries.reshape(2 * QROWS, HD)
    kv = jnp.concatenate([prefix_keys, prefix_values], axis=0).reshape(BLOCK, HD)
    up1 = lax.ppermute(kv, "rep", z_perm(1))
    dn1 = lax.ppermute(kv, "rep", z_perm(-1))
    up2 = lax.ppermute(up1, "rep", z_perm(1))
    dn2 = lax.ppermute(dn1, "rep", z_perm(-1))
    sent, local = pl.pallas_call(
        pack_kernel,
        out_shape=[
            jax.ShapeDtypeStruct((2 * QROWS + 16, HD), BF),
            jax.ShapeDtypeStruct((PAGES_AT + 2 * LOCAL_PAGES * 128, HD), BF),
        ],
        in_specs=[ANY] * 5 + [VMEM] * 2 + [ANY],
        out_specs=[VMEM] * 2,
        scratch_shapes=[pltpu.SemaphoreType.DMA((6,))],
        compiler_params=pltpu.CompilerParams(vmem_limit_bytes=59 << 20),
        name="pack",
    )(
        q_own, tree_keys.reshape(-1, HD), tree_values.reshape(-1, HD),
        prefix_keys.reshape(-1, HD), prefix_values.reshape(-1, HD), page_table, tree_parent.reshape(1, -1),
        kv,
    )
    sents = [lax.ppermute(sent, "rep", group_perm(r)) for r in (1, 2, 3)]
    up3 = lax.ppermute(up2, "rep", z_perm(1))
    dn3 = lax.ppermute(dn2, "rep", z_perm(-1))
    held = jnp.where((rep & 1) == 0, up2, dn2)
    opposite = lax.ppermute(
        held, "rep", [(rep_of(a, z, c), rep_of(a, z + 2 - 4 * c, c)) for a in range(2) for z in range(Z) for c in range(2)]
    )

    reps = jnp.arange(32, dtype=jnp.int32)
    same = ((reps ^ rep) & 17) == 0
    step = ((reps >> 1) - (rep >> 1)) & 7
    maps = jnp.full((32,), -(1 << 20), jnp.int32)
    for k, offsets in enumerate(GROUPS):
        for i, o in enumerate(offsets):
            maps = jnp.where(same & (step == o % Z), k * 65536 + i * 8, maps)
    q_all, list_far, *state = near_call(maps, local, *sents, up1, dn1, up2, dn2)
    own, p1, p2, p3 = far_call(list_far, q_all, (up3, dn3, opposite), state)
    back = [lax.ppermute(p, "rep", group_perm(r)) for r, p in ((3, p3), (2, p2), (1, p1))]
    width = out_weight.shape[1]
    attn = pl.pallas_call(
        combine_kernel,
        out_shape=jax.ShapeDtypeStruct((128, 512), BF),
        in_specs=[SMEM] + [VMEM] * 4,
        out_specs=VMEM,
        scratch_shapes=[pltpu.VMEM((2 * QROWS, HD), F32)],
        compiler_params=pltpu.CompilerParams(vmem_limit_bytes=24 << 20),
        cost_estimate=pl.CostEstimate(flops=10**6, bytes_accessed=1 << 20, transcendentals=4096),
        name="combine",
    )(head.reshape(1).astype(jnp.int32), own, *back)
    rows = jnp.dot(attn, out_weight, preferred_element_type=F32).astype(BF)
    parts = [rows[k * 16:(k + 1) * 16] for k in range(8)]
    terms = [lax.ppermute(parts[k], "head", [(i, i ^ k) for i in range(8)]) for k in (1, 3, 4, 2, 5, 7, 6)]
    return pl.pallas_call(
        sum_kernel,
        out_shape=jax.ShapeDtypeStruct((16, width), BF),
        in_specs=[VMEM] * 8,
        out_specs=VMEM,
        compiler_params=pltpu.CompilerParams(vmem_limit_bytes=24 << 20),
        name="sum_heads",
    )(parts[0], *terms)


def solution(mesh):
    in_specs = (
        P("rep", "head", None),
        P("rep", "head", None),
        P("rep", "head", None),
        P("rep", "head", None, None),
        P("rep", "head", None, None),
        P("rep"),
        P("rep", None),
        P("head", None),
    )
    out_specs = P(("rep", "head"), None)
    return jax.shard_map(
        on_device, mesh=mesh, in_specs=in_specs, out_specs=out_specs, check_vma=False
    )
```

```python
import functools
import math

import jax
import jax.numpy as jnp
from jax import lax
from jax.experimental import pallas as pl
from jax.experimental.pallas import tpu as pltpu
from jax.sharding import PartitionSpec as P

NEG = -1e30
Z = 8
GROUP = 4
LOCAL_PAGES = 4
TK_AT = 528
TV_AT = 656
BLOCK = 1024
PAGES_AT = 784
TREE = 64
QROWS = 256
HD = 128
SESS = 8
C2 = (HD ** -0.5) * math.log2(math.e)
BF = jnp.bfloat16
F32 = jnp.float32

STREAMS = 4
GROUPS = ((0, -1, 1, -2, 2), (-3, 3, 4))


HEADS = ((0, 0), (0, 1), (0, 3), (0, 2), (1, 0), (1, 1), (1, 3), (1, 2))


def rep_of(xh, z, c):
    return xh * 16 + (z % Z) * 2 + c


def z_perm(k):
    return [(rep_of(a, z, c), rep_of(a, z + k, c)) for a in range(2) for z in range(Z) for c in range(2)]


def group_perm(r):
    return [(rep_of(a, z, c), rep_of(a ^ (r >> 1), z, c ^ (r & 1))) for a in range(2) for z in range(Z) for c in range(2)]


def page(kv, i):
    return kv[pl.ds(pl.multiple_of(i * 128, 128), 128), :]


def pair_steps(entries, q_ref, kv, streams):
    at = [(e >> 8, e & 255) for e in entries]
    scores = [
        lax.dot_general(page(kv, k), q_ref[pl.ds(pl.multiple_of((s & (SESS - 1)) * QROWS, QROWS), QROWS), :], (((1,), (1,)), ((), ())), preferred_element_type=F32)
        for s, k in at
    ]
    olds = [m[s] for (s, _), (m, _, _) in zip(at, streams)]
    news = [jnp.maximum(o, jnp.max(x, axis=0, keepdims=True)) for o, x in zip(olds, scores)]
    probs = [jnp.exp2(x * C2 - n * C2) for x, n in zip(scores, news)]
    fixes = [jnp.exp2((o - n) * C2) for o, n in zip(olds, news)]
    parts = [
        lax.dot_general(
            page(kv, k + LOCAL_PAGES), p.astype(BF), (((0,), (0,)), ((), ())), preferred_element_type=F32
        )
        for (_, k), p in zip(at, probs)
    ]
    for (s, _), n, p, fix, part, (m_ref, l_ref, a_ref) in zip(at, news, probs, fixes, parts, streams):
        m_ref[s] = n
        l_ref[s] = l_ref[s] * fix + jnp.sum(p, axis=0, keepdims=True)
        a_ref[s] = a_ref[s] * fix + part


def all_pairs(entries, q_ref, kv, streams):
    ns = len(streams)

    @pl.loop(0, (entries[0] + ns - 1) >> (ns.bit_length() - 1))
    def _(i):
        pair_steps([entries[ns * i + r + 1] for r in range(ns)], q_ref, kv, streams)


def streams_of(refs):
    return [tuple(refs[3 * r:3 * r + 3]) for r in range(STREAMS)]


def clear(streams):
    for m_ref, l_ref, a_ref in streams:
        m_ref[...] = jnp.full(m_ref.shape, NEG, F32)
        l_ref[...] = jnp.zeros(l_ref.shape, F32)
        a_ref[...] = jnp.zeros(a_ref.shape, F32)


def merge(states):
    top = functools.reduce(jnp.maximum, [m for m, _, _ in states])
    ws = [jnp.exp2((m - top) * C2) for m, _, _ in states]
    total = sum(w * l for w, (_, l, _) in zip(ws, states))
    acc = sum(w * a for w, (_, _, a) in zip(ws, states))
    return top, total, acc


def pack_kernel(q, tk, tv, pk, pv, table, parent, kv, sent, local, sems):
    del kv
    copies = [
        pltpu.make_async_copy(q, sent.at[pl.ds(0, 2 * QROWS)], sems.at[0]),
        pltpu.make_async_copy(q, local.at[pl.ds(0, 2 * QROWS)], sems.at[1]),
        pltpu.make_async_copy(tk, local.at[pl.ds(TK_AT, 128)], sems.at[2]),
        pltpu.make_async_copy(tv, local.at[pl.ds(TV_AT, 128)], sems.at[3]),
        pltpu.make_async_copy(pk, local.at[pl.ds(PAGES_AT, LOCAL_PAGES * 128)], sems.at[4]),
        pltpu.make_async_copy(pv, local.at[pl.ds(PAGES_AT + LOCAL_PAGES * 128, LOCAL_PAGES * 128)], sems.at[5]),
    ]
    for cp in copies:
        cp.start()
    ids = table[...].astype(F32)
    row = lax.broadcasted_iota(jnp.int32, (16, 128), 0)
    above = parent[...].astype(F32)
    tail = pl.ds(2 * QROWS, 16)
    sent[tail, :] = jnp.zeros((16, 128), BF)
    local[tail, :] = jnp.where(row == 2, above, 0.0).astype(BF)
    row = row[:, :16]
    pages = jnp.where(row == 0, ids[0:1, :], jnp.where(row == 1, ids[1:2, :], 0.0))
    sent[tail, :16] = pages.astype(BF)
    local[tail, :16] = jnp.where(row == 2, above[:, :16], pages).astype(BF)
    for cp in copies:
        cp.wait()


def near_kernel(maps, local, s1, s2, s3, up1, dn1, up2, dn2, q_out, list_far, *refs):
    m_out, l_out, a_out, tails, ids, tbl, list_near, found, kv = refs[:9]
    lists = (list_near, list_far)
    streams = streams_of(refs[9:-1])
    sems = refs[-1]
    sents = (local, s1, s2, s3)
    for r, x in enumerate(sents):
        tails[pl.ds(r * 16, 16), :] = x[pl.ds(2 * QROWS, 16), :]
    ids[...] = tails[...].astype(F32).astype(jnp.int32)
    to_scalar = pltpu.make_async_copy(ids, tbl, sems.at[0])
    to_scalar.start()
    copies = load_blocks(
        [local.at[pl.ds(PAGES_AT, BLOCK)], up1, dn1, up2, dn2], kv, [sems.at[i + 1] for i in range(5)]
    )
    for r, x in enumerate(sents):
        q_out[pl.ds(r * 2 * QROWS, 2 * QROWS), :] = x[pl.ds(0, 2 * QROWS), :]
    clear(streams)
    both = 2 * TREE
    row = lax.broadcasted_iota(jnp.int32, (both, both), 0)
    lane = lax.broadcasted_iota(jnp.int32, (both, both), 1)
    above = ids[2:3, :] + jnp.where(lax.broadcasted_iota(jnp.int32, (1, both), 1) >= TREE, TREE, 0)
    reach = jnp.minimum((row == lane).astype(F32) + (row == above).astype(F32), 1.0)
    for _ in range(7):
        half = reach.astype(BF)
        reach = jnp.minimum(jnp.dot(half, half, preferred_element_type=F32), 1.0)
    half = reach.astype(BF)
    tree_row = lax.broadcasted_iota(jnp.int32, (both, QROWS), 0)
    of_query = lax.shift_right_logical(lax.broadcasted_iota(jnp.int32, (both, QROWS), 1), 2)
    m0, l0, a0 = streams[0]
    for s in range(2):
        widen = (tree_row == of_query + s * TREE).astype(BF)
        seen = jnp.dot(half[s * TREE:(s + 1) * TREE, :], widen, preferred_element_type=F32)
        scores = lax.dot_general(
            local[pl.ds(TK_AT + s * TREE, TREE), :],
            local[pl.ds(s * QROWS, QROWS), :],
            (((1,), (1,)), ((), ())),
            preferred_element_type=F32,
        )
        scores = jnp.where(seen > 0.5, scores, NEG)
        top = jnp.max(scores, axis=0, keepdims=True)
        probs = jnp.exp2(scores * C2 - top * C2)
        m0[s] = top
        l0[s] = jnp.sum(probs, axis=0, keepdims=True)
        a0[s] = lax.dot_general(
            local[pl.ds(TV_AT + s * TREE, TREE), :],
            probs.astype(BF),
            (((0,), (0,)), ((), ())),
            preferred_element_type=F32,
        )
    to_scalar.wait()

    def scan(r, n):
        for half in range(2):
            pages = [tbl[r * 16 + half, j] for j in range(16)]
            at = [maps[p >> 2] for p in pages]
            for p, where in zip(pages, at):
                found[n] = (r * 2 + half) * 256 + (p & 3) + where
                n = n + (where >= 0).astype(jnp.int32)
        return n

    total = lax.fori_loop(0, GROUP, scan, jnp.int32(0))

    def sort(i, counts):
        entry = found[i]
        kind = entry >> 16
        out = []
        for k in range(2):
            lists[k][counts[k] + 1] = entry & 65535
            out.append(counts[k] + (kind == k).astype(jnp.int32))
        return tuple(out)

    counts = lax.fori_loop(0, total, sort, (jnp.int32(0),) * 2)
    for k in range(2):
        lists[k][0] = counts[k]
        for r in range(STREAMS - 1):
            lists[k][counts[k] + 1 + r] = jnp.int32(SESS * 256)
    for cp in copies:
        cp.wait()
    all_pairs(list_near, q_out, kv, streams)
    for s in range(SESS):
        top, total, acc = merge([(m[s], l[s], a[s]) for m, l, a in streams])
        m_out[s] = top
        l_out[s] = total
        a_out[s] = acc


def load_blocks(blocks, kv, sems):
    copies = [pltpu.make_async_copy(b, kv.at[pl.ds(i * BLOCK, BLOCK)], sem) for i, (b, sem) in enumerate(zip(blocks, sems))]
    for cp in copies:
        cp.start()
    return copies


def far_kernel(nb, *refs):
    list_far, q_ref = refs[:2]
    blocks = refs[2:2 + nb]
    before = refs[2 + nb:5 + nb]
    own = refs[5 + nb]
    outs = refs[6 + nb:9 + nb]
    kv = refs[9 + nb]
    streams = streams_of(refs[10 + nb:-1])
    copies = load_blocks(blocks, kv, [refs[-1].at[i] for i in range(nb)])
    clear(streams)
    for cp in copies:
        cp.wait()
    all_pairs(list_far, q_ref, kv, streams)
    for s in range(SESS):
        top, total, acc = merge([(m[s], l[s], a[s]) for m, l, a in [before] + streams])
        some = total > 0.0
        safe = jnp.where(some, total, 1.0)
        acc = acc * (1.0 / safe)
        lse = jnp.where(some, top * C2 + jnp.log2(safe), NEG)
        lanes = pl.ds((s % 2) * QROWS, QROWS)
        if s < 2:
            own[pl.ds(0, HD), lanes] = acc
            own[pl.ds(HD, 8), lanes] = jnp.broadcast_to(lse, (8, QROWS))
        else:
            out = outs[s // 2 - 1]
            out[pl.ds(0, HD), lanes] = acc.astype(BF)
            hi = lse.astype(BF).astype(F32)
            mid = (lse - hi).astype(BF).astype(F32)
            low = lse - hi - mid
            row = lax.broadcasted_iota(jnp.int32, (16, QROWS), 0)
            parts = jnp.where(row == 0, hi, jnp.where(row == 1, mid, jnp.where(row == 2, low, 0.0)))
            out[pl.ds(HD, 16), lanes] = parts.astype(BF)


def combine_kernel(head_ref, own, p1, p2, p3, attn, rows_f32):
    lses = [own[HD:HD + 1, :]]
    vals = [own[:HD, :]]
    for p in (p1, p2, p3):
        tail = p[HD:HD + 16, :].astype(F32)
        lses.append(tail[0:1] + tail[1:2] + tail[2:3])
        vals.append(p[:HD, :].astype(F32))
    top = functools.reduce(jnp.maximum, lses)
    ws = [jnp.exp2(x - top) for x in lses]
    inv = 1.0 / sum(ws)
    mixed = sum(v * (w * inv) for v, w in zip(vals, ws))
    rows_f32[...] = mixed.T
    for k, (dx, dy) in enumerate(HEADS):
        first = ((head_ref[0] & 4) ^ (dx * 4)) * 64 + ((head_ref[0] + dy) & 3) * 64
        for h in range(4):
            block = rows_f32[pl.ds(first + h, 16, stride=4), :]
            attn[pl.ds(k * 16, 16), pl.ds(h * HD, HD)] = block.astype(BF)


def sum_kernel(*refs):
    out = refs[-1]
    out[...] = functools.reduce(jnp.add, [r[...].astype(F32) for r in refs[:-1]]).astype(BF)


VMEM = pl.BlockSpec(memory_space=pltpu.VMEM)
SMEM = pl.BlockSpec(memory_space=pltpu.SMEM)
ANY = pl.BlockSpec(memory_space=pl.ANY)


def stream_scratch():
    return [
        pltpu.VMEM((SESS + 1, 1, QROWS), F32),
        pltpu.VMEM((SESS + 1, 1, QROWS), F32),
        pltpu.VMEM((SESS + 1, HD, QROWS), F32),
    ]


def state_shapes(n):
    return [
        jax.ShapeDtypeStruct((n, 1, QROWS), F32),
        jax.ShapeDtypeStruct((n, 1, QROWS), F32),
        jax.ShapeDtypeStruct((n, HD, QROWS), F32),
    ]


def near_call(*args):
    return pl.pallas_call(
        near_kernel,
        out_shape=[jax.ShapeDtypeStruct((SESS * QROWS, HD), BF), jax.ShapeDtypeStruct((160,), jnp.int32)]
        + state_shapes(SESS),
        in_specs=[SMEM] + [VMEM] * 4 + [ANY] * 4,
        out_specs=[VMEM, SMEM] + [VMEM] * 3,
        scratch_shapes=[
            pltpu.VMEM((64, 128), BF),
            pltpu.VMEM((64, 128), jnp.int32),
            pltpu.SMEM((64, 128), jnp.int32),
            pltpu.SMEM((160,), jnp.int32),
            pltpu.SMEM((160,), jnp.int32),
            pltpu.VMEM((5 * BLOCK, HD), BF),
        ]
        + stream_scratch() * STREAMS
        + [pltpu.SemaphoreType.DMA((6,))],
        compiler_params=pltpu.CompilerParams(vmem_limit_bytes=24 << 20),
        cost_estimate=pl.CostEstimate(flops=4 * 10**9, bytes_accessed=4 << 20, transcendentals=1 << 20),
        name="near_pages",
    )(*args)


def far_call(pages, q_all, blocks, state):
    nb = len(blocks)
    return pl.pallas_call(
        functools.partial(far_kernel, nb),
        out_shape=[jax.ShapeDtypeStruct((HD + 8, 2 * QROWS), F32)]
        + [jax.ShapeDtypeStruct((HD + 16, 2 * QROWS), BF)] * 3,
        in_specs=[SMEM, VMEM] + [ANY] * nb + [VMEM] * 3,
        out_specs=[VMEM] * 4,
        scratch_shapes=[pltpu.VMEM((nb * BLOCK, HD), BF)]
        + stream_scratch() * STREAMS
        + [pltpu.SemaphoreType.DMA((nb,))],
        compiler_params=pltpu.CompilerParams(vmem_limit_bytes=24 << 20),
        cost_estimate=pl.CostEstimate(flops=10**9, bytes_accessed=4 << 20, transcendentals=1 << 20),
        name="far_pages",
    )(pages, q_all, *blocks, *state)


def on_device(
    queries, tree_keys, tree_values, prefix_keys, prefix_values, tree_parent, page_table, out_weight
):
    rep = lax.axis_index("rep")
    head = lax.axis_index("head")
    q_own = queries.reshape(2 * QROWS, HD)
    kv = jnp.concatenate([prefix_keys, prefix_values], axis=0).reshape(BLOCK, HD)
    up1 = lax.ppermute(kv, "rep", z_perm(1))
    dn1 = lax.ppermute(kv, "rep", z_perm(-1))
    up2 = lax.ppermute(up1, "rep", z_perm(1))
    dn2 = lax.ppermute(dn1, "rep", z_perm(-1))
    sent, local = pl.pallas_call(
        pack_kernel,
        out_shape=[
            jax.ShapeDtypeStruct((2 * QROWS + 16, HD), BF),
            jax.ShapeDtypeStruct((PAGES_AT + 2 * LOCAL_PAGES * 128, HD), BF),
        ],
        in_specs=[ANY] * 5 + [VMEM] * 2 + [ANY],
        out_specs=[VMEM] * 2,
        scratch_shapes=[pltpu.SemaphoreType.DMA((6,))],
        compiler_params=pltpu.CompilerParams(vmem_limit_bytes=59 << 20),
        name="pack",
    )(
        q_own, tree_keys.reshape(-1, HD), tree_values.reshape(-1, HD),
        prefix_keys.reshape(-1, HD), prefix_values.reshape(-1, HD), page_table, tree_parent.reshape(1, -1),
        kv,
    )
    sents = [lax.ppermute(sent, "rep", group_perm(r)) for r in (1, 2, 3)]
    up3 = lax.ppermute(up2, "rep", z_perm(1))
    dn3 = lax.ppermute(dn2, "rep", z_perm(-1))
    held = jnp.where((rep & 1) == 0, up2, dn2)
    opposite = lax.ppermute(
        held, "rep", [(rep_of(a, z, c), rep_of(a, z + 2 - 4 * c, c)) for a in range(2) for z in range(Z) for c in range(2)]
    )

    reps = jnp.arange(32, dtype=jnp.int32)
    same = ((reps ^ rep) & 17) == 0
    step = ((reps >> 1) - (rep >> 1)) & 7
    maps = jnp.full((32,), -(1 << 20), jnp.int32)
    for k, offsets in enumerate(GROUPS):
        for i, o in enumerate(offsets):
            maps = jnp.where(same & (step == o % Z), k * 65536 + i * 8, maps)
    q_all, list_far, *state = near_call(maps, local, *sents, up1, dn1, up2, dn2)
    own, p1, p2, p3 = far_call(list_far, q_all, (up3, dn3, opposite), state)
    back = [lax.ppermute(p, "rep", group_perm(r)) for r, p in ((3, p3), (2, p2), (1, p1))]
    width = out_weight.shape[1]
    attn = pl.pallas_call(
        combine_kernel,
        out_shape=jax.ShapeDtypeStruct((128, 512), BF),
        in_specs=[SMEM] + [VMEM] * 4,
        out_specs=VMEM,
        scratch_shapes=[pltpu.VMEM((2 * QROWS, HD), F32)],
        compiler_params=pltpu.CompilerParams(vmem_limit_bytes=24 << 20),
        cost_estimate=pl.CostEstimate(flops=10**6, bytes_accessed=1 << 20, transcendentals=4096),
        name="combine",
    )(head.reshape(1).astype(jnp.int32), own, *back)
    rows = jnp.dot(attn, out_weight, preferred_element_type=F32).astype(BF)
    parts = [rows[k * 16:(k + 1) * 16] for k in range(8)]
    terms = [
        lax.ppermute(part, "head", [(i, ((i & 4) ^ (dx * 4)) + ((i + dy) & 3)) for i in range(8)])
        for part, (dx, dy) in zip(parts[1:], HEADS[1:])
    ]
    return pl.pallas_call(
        sum_kernel,
        out_shape=jax.ShapeDtypeStruct((16, width), BF),
        in_specs=[VMEM] * 8,
        out_specs=VMEM,
        compiler_params=pltpu.CompilerParams(vmem_limit_bytes=24 << 20),
        name="sum_heads",
    )(parts[0], *terms)


def solution(mesh):
    in_specs = (
        P("rep", "head", None),
        P("rep", "head", None),
        P("rep", "head", None),
        P("rep", "head", None, None),
        P("rep", "head", None, None),
        P("rep"),
        P("rep", None),
        P("head", None),
    )
    out_specs = P(("rep", "head"), None)
    return jax.shard_map(
        on_device, mesh=mesh, in_specs=in_specs, out_specs=out_specs, check_vma=False
    )
```

```python
import functools
import math

import jax
import jax.numpy as jnp
from jax import lax
from jax.experimental import pallas as pl
from jax.experimental.pallas import tpu as pltpu
from jax.sharding import PartitionSpec as P

NEG = -1e30
Z = 8
GROUP = 4
LOCAL_PAGES = 4
TK_AT = 528
TV_AT = 656
BLOCK = 1024
PAGES_AT = 784
TREE = 64
QROWS = 256
HD = 128
SESS = 8
C2 = (HD ** -0.5) * math.log2(math.e)
BF = jnp.bfloat16
F32 = jnp.float32

STREAMS = 4
GROUPS = ((0, -1, 1, -2, 2), (-3, 3, 4))


HEADS = ((0, 0), (0, 1), (0, 3), (0, 2), (1, 0), (1, 1), (1, 3), (1, 2))


def rep_of(xh, z, c):
    return xh * 16 + (z % Z) * 2 + c


def z_perm(k):
    return [(rep_of(a, z, c), rep_of(a, z + k, c)) for a in range(2) for z in range(Z) for c in range(2)]


def group_perm(r):
    return [(rep_of(a, z, c), rep_of(a ^ (r >> 1), z, c ^ (r & 1))) for a in range(2) for z in range(Z) for c in range(2)]


def page(kv, i):
    return kv[pl.ds(pl.multiple_of(i * 128, 128), 128), :]


def pair_steps(entries, q_ref, kv, streams):
    at = [(e >> 8, e & 255) for e in entries]
    scores = [
        lax.dot_general(page(kv, k), q_ref[pl.ds(pl.multiple_of((s & (SESS - 1)) * QROWS, QROWS), QROWS), :], (((1,), (1,)), ((), ())), preferred_element_type=F32)
        for s, k in at
    ]
    olds = [m[s] for (s, _), (m, _, _) in zip(at, streams)]
    news = [jnp.maximum(o, jnp.max(x, axis=0, keepdims=True)) for o, x in zip(olds, scores)]
    probs = [jnp.exp2(x * C2 - n * C2) for x, n in zip(scores, news)]
    fixes = [jnp.exp2((o - n) * C2) for o, n in zip(olds, news)]
    parts = [
        lax.dot_general(
            page(kv, k + LOCAL_PAGES), p.astype(BF), (((0,), (0,)), ((), ())), preferred_element_type=F32
        )
        for (_, k), p in zip(at, probs)
    ]
    for (s, _), n, p, fix, part, (m_ref, l_ref, a_ref) in zip(at, news, probs, fixes, parts, streams):
        m_ref[s] = n
        l_ref[s] = l_ref[s] * fix + jnp.sum(p, axis=0, keepdims=True)
        a_ref[s] = a_ref[s] * fix + part


def all_pairs(entries, q_ref, kv, streams):
    ns = len(streams)

    @pl.loop(0, (entries[0] + ns - 1) >> (ns.bit_length() - 1))
    def _(i):
        pair_steps([entries[ns * i + r + 1] for r in range(ns)], q_ref, kv, streams)


def streams_of(refs):
    return [tuple(refs[3 * r:3 * r + 3]) for r in range(STREAMS)]


def clear(streams):
    for m_ref, l_ref, a_ref in streams:
        m_ref[...] = jnp.full(m_ref.shape, NEG, F32)
        l_ref[...] = jnp.zeros(l_ref.shape, F32)
        a_ref[...] = jnp.zeros(a_ref.shape, F32)


def merge(states):
    top = functools.reduce(jnp.maximum, [m for m, _, _ in states])
    ws = [jnp.exp2((m - top) * C2) for m, _, _ in states]
    total = sum(w * l for w, (_, l, _) in zip(ws, states))
    acc = sum(w * a for w, (_, _, a) in zip(ws, states))
    return top, total, acc


def pack_kernel(q, tk, tv, pk, pv, table, parent, kv, sent, local, sems):
    del kv
    copies = [
        pltpu.make_async_copy(q, sent.at[pl.ds(0, 2 * QROWS)], sems.at[0]),
        pltpu.make_async_copy(q, local.at[pl.ds(0, 2 * QROWS)], sems.at[1]),
        pltpu.make_async_copy(tk, local.at[pl.ds(TK_AT, 128)], sems.at[2]),
        pltpu.make_async_copy(tv, local.at[pl.ds(TV_AT, 128)], sems.at[3]),
        pltpu.make_async_copy(pk, local.at[pl.ds(PAGES_AT, LOCAL_PAGES * 128)], sems.at[4]),
        pltpu.make_async_copy(pv, local.at[pl.ds(PAGES_AT + LOCAL_PAGES * 128, LOCAL_PAGES * 128)], sems.at[5]),
    ]
    for cp in copies:
        cp.start()
    ids = table[...].astype(F32)
    row = lax.broadcasted_iota(jnp.int32, (16, 128), 0)
    above = parent[...].astype(F32)
    tail = pl.ds(2 * QROWS, 16)
    sent[tail, :] = jnp.zeros((16, 128), BF)
    local[tail, :] = jnp.where(row == 2, above, 0.0).astype(BF)
    row = row[:, :16]
    pages = jnp.where(row == 0, ids[0:1, :], jnp.where(row == 1, ids[1:2, :], 0.0))
    sent[tail, :16] = pages.astype(BF)
    local[tail, :16] = jnp.where(row == 2, above[:, :16], pages).astype(BF)
    for cp in copies:
        cp.wait()


def near_kernel(maps, local, s1, s2, s3, up1, dn1, up2, dn2, q_out, list_far, *refs):
    m_out, l_out, a_out, tails, ids, tbl, list_near, found, kv = refs[:9]
    lists = (list_near, list_far)
    streams = streams_of(refs[9:-1])
    sems = refs[-1]
    sents = (local, s1, s2, s3)
    for r, x in enumerate(sents):
        tails[pl.ds(r * 16, 16), :] = x[pl.ds(2 * QROWS, 16), :]
    ids[...] = tails[...].astype(F32).astype(jnp.int32)
    to_scalar = pltpu.make_async_copy(ids, tbl, sems.at[0])
    to_scalar.start()
    copies = load_blocks(
        [local.at[pl.ds(PAGES_AT, BLOCK)], up1, dn1, up2, dn2], kv, [sems.at[i + 1] for i in range(5)]
    )
    for r, x in enumerate(sents):
        q_out[pl.ds(r * 2 * QROWS, 2 * QROWS), :] = x[pl.ds(0, 2 * QROWS), :]
    clear(streams)
    both = 2 * TREE
    row = lax.broadcasted_iota(jnp.int32, (both, both), 0)
    lane = lax.broadcasted_iota(jnp.int32, (both, both), 1)
    above = ids[2:3, :] + jnp.where(lax.broadcasted_iota(jnp.int32, (1, both), 1) >= TREE, TREE, 0)
    reach = jnp.minimum((row == lane).astype(F32) + (row == above).astype(F32), 1.0)
    for _ in range(7):
        half = reach.astype(BF)
        reach = jnp.minimum(jnp.dot(half, half, preferred_element_type=F32), 1.0)
    half = reach.astype(BF)
    tree_row = lax.broadcasted_iota(jnp.int32, (both, QROWS), 0)
    of_query = lax.shift_right_logical(lax.broadcasted_iota(jnp.int32, (both, QROWS), 1), 2)
    m0, l0, a0 = streams[0]
    for s in range(2):
        widen = (tree_row == of_query + s * TREE).astype(BF)
        seen = jnp.dot(half[s * TREE:(s + 1) * TREE, :], widen, preferred_element_type=F32)
        scores = lax.dot_general(
            local[pl.ds(TK_AT + s * TREE, TREE), :],
            local[pl.ds(s * QROWS, QROWS), :],
            (((1,), (1,)), ((), ())),
            preferred_element_type=F32,
        )
        scores = jnp.where(seen > 0.5, scores, NEG)
        top = jnp.max(scores, axis=0, keepdims=True)
        probs = jnp.exp2(scores * C2 - top * C2)
        m0[s] = top
        l0[s] = jnp.sum(probs, axis=0, keepdims=True)
        a0[s] = lax.dot_general(
            local[pl.ds(TV_AT + s * TREE, TREE), :],
            probs.astype(BF),
            (((0,), (0,)), ((), ())),
            preferred_element_type=F32,
        )
    to_scalar.wait()

    def scan(r, n):
        for half in range(2):
            pages = [tbl[r * 16 + half, j] for j in range(16)]
            at = [maps[p >> 2] for p in pages]
            for p, where in zip(pages, at):
                found[n] = (r * 2 + half) * 256 + (p & 3) + where
                n = n + (where >= 0).astype(jnp.int32)
        return n

    total = lax.fori_loop(0, GROUP, scan, jnp.int32(0))

    def sort(i, counts):
        entry = found[i]
        kind = entry >> 16
        out = []
        for k in range(2):
            lists[k][counts[k] + 1] = entry & 65535
            out.append(counts[k] + (kind == k).astype(jnp.int32))
        return tuple(out)

    counts = lax.fori_loop(0, total, sort, (jnp.int32(0),) * 2)
    for k in range(2):
        lists[k][0] = counts[k]
        for r in range(STREAMS - 1):
            lists[k][counts[k] + 1 + r] = jnp.int32(SESS * 256)
    for cp in copies:
        cp.wait()
    all_pairs(list_near, q_out, kv, streams)
    for s in range(SESS):
        top, total, acc = merge([(m[s], l[s], a[s]) for m, l, a in streams])
        m_out[s] = top
        l_out[s] = total
        a_out[s] = acc


def load_blocks(blocks, kv, sems):
    copies = [pltpu.make_async_copy(b, kv.at[pl.ds(i * BLOCK, BLOCK)], sem) for i, (b, sem) in enumerate(zip(blocks, sems))]
    for cp in copies:
        cp.start()
    return copies


def far_kernel(nb, *refs):
    list_far, q_ref = refs[:2]
    blocks = refs[2:2 + nb]
    before = refs[2 + nb:5 + nb]
    own = refs[5 + nb]
    outs = refs[6 + nb:9 + nb]
    kv = refs[9 + nb]
    streams = streams_of(refs[10 + nb:-1])
    copies = load_blocks(blocks, kv, [refs[-1].at[i] for i in range(nb)])
    clear(streams)
    for cp in copies:
        cp.wait()
    all_pairs(list_far, q_ref, kv, streams)
    for s in range(SESS):
        top, total, acc = merge([(m[s], l[s], a[s]) for m, l, a in [before] + streams])
        some = total > 0.0
        safe = jnp.where(some, total, 1.0)
        acc = acc * (1.0 / safe)
        lse = jnp.where(some, top * C2 + jnp.log2(safe), NEG)
        lanes = pl.ds((s % 2) * QROWS, QROWS)
        if s < 2:
            own[pl.ds(0, HD), lanes] = acc
            own[pl.ds(HD, 8), lanes] = jnp.broadcast_to(lse, (8, QROWS))
        else:
            out = outs[s // 2 - 1]
            out[pl.ds(0, HD), lanes] = acc.astype(BF)
            hi = lse.astype(BF).astype(F32)
            mid = (lse - hi).astype(BF).astype(F32)
            low = lse - hi - mid
            row = lax.broadcasted_iota(jnp.int32, (16, QROWS), 0)
            parts = jnp.where(row == 0, hi, jnp.where(row == 1, mid, jnp.where(row == 2, low, 0.0)))
            out[pl.ds(HD, 16), lanes] = parts.astype(BF)


def combine_kernel(head_ref, own, p1, p2, p3, attn, rows_f32):
    lses = [own[HD:HD + 1, :]]
    vals = [own[:HD, :]]
    for p in (p1, p2, p3):
        tail = p[HD:HD + 16, :].astype(F32)
        lses.append(tail[0:1] + tail[1:2] + tail[2:3])
        vals.append(p[:HD, :].astype(F32))
    top = functools.reduce(jnp.maximum, lses)
    ws = [jnp.exp2(x - top) for x in lses]
    inv = 1.0 / sum(ws)
    mixed = sum(v * (w * inv) for v, w in zip(vals, ws))
    rows_f32[...] = mixed.T
    for k, (dx, dy) in enumerate(HEADS):
        first = ((head_ref[0] & 4) ^ (dx * 4)) * 64 + ((head_ref[0] + dy) & 3) * 64
        for h in range(4):
            block = rows_f32[pl.ds(first + h, 16, stride=4), :]
            attn[pl.ds(k * 16, 16), pl.ds(h * HD, HD)] = block.astype(BF)


def sum_kernel(*refs):
    out = refs[-1]
    out[...] = functools.reduce(jnp.add, [r[...].astype(F32) for r in refs[:-1]]).astype(BF)


VMEM = pl.BlockSpec(memory_space=pltpu.VMEM)
SMEM = pl.BlockSpec(memory_space=pltpu.SMEM)
ANY = pl.BlockSpec(memory_space=pl.ANY)


def stream_scratch():
    return [
        pltpu.VMEM((SESS + 1, 1, QROWS), F32),
        pltpu.VMEM((SESS + 1, 1, QROWS), F32),
        pltpu.VMEM((SESS + 1, HD, QROWS), F32),
    ]


def state_shapes(n):
    return [
        jax.ShapeDtypeStruct((n, 1, QROWS), F32),
        jax.ShapeDtypeStruct((n, 1, QROWS), F32),
        jax.ShapeDtypeStruct((n, HD, QROWS), F32),
    ]


def near_call(*args):
    return pl.pallas_call(
        near_kernel,
        out_shape=[jax.ShapeDtypeStruct((SESS * QROWS, HD), BF), jax.ShapeDtypeStruct((160,), jnp.int32)]
        + state_shapes(SESS),
        in_specs=[SMEM] + [VMEM] * 4 + [ANY] * 4,
        out_specs=[VMEM, SMEM] + [VMEM] * 3,
        scratch_shapes=[
            pltpu.VMEM((64, 128), BF),
            pltpu.VMEM((64, 128), jnp.int32),
            pltpu.SMEM((64, 128), jnp.int32),
            pltpu.SMEM((160,), jnp.int32),
            pltpu.SMEM((160,), jnp.int32),
            pltpu.VMEM((5 * BLOCK, HD), BF),
        ]
        + stream_scratch() * STREAMS
        + [pltpu.SemaphoreType.DMA((6,))],
        compiler_params=pltpu.CompilerParams(vmem_limit_bytes=24 << 20),
        cost_estimate=pl.CostEstimate(flops=4 * 10**9, bytes_accessed=4 << 20, transcendentals=1 << 20),
        name="near_pages",
    )(*args)


def far_call(pages, q_all, blocks, state):
    nb = len(blocks)
    return pl.pallas_call(
        functools.partial(far_kernel, nb),
        out_shape=[jax.ShapeDtypeStruct((HD + 8, 2 * QROWS), F32)]
        + [jax.ShapeDtypeStruct((HD + 16, 2 * QROWS), BF)] * 3,
        in_specs=[SMEM, VMEM] + [ANY] * nb + [VMEM] * 3,
        out_specs=[VMEM] * 4,
        scratch_shapes=[pltpu.VMEM((nb * BLOCK, HD), BF)]
        + stream_scratch() * STREAMS
        + [pltpu.SemaphoreType.DMA((nb,))],
        compiler_params=pltpu.CompilerParams(vmem_limit_bytes=24 << 20),
        cost_estimate=pl.CostEstimate(flops=10**9, bytes_accessed=4 << 20, transcendentals=1 << 20),
        name="far_pages",
    )(pages, q_all, *blocks, *state)


def on_device(
    queries, tree_keys, tree_values, prefix_keys, prefix_values, tree_parent, page_table, out_weight
):
    rep = lax.axis_index("rep")
    head = lax.axis_index("head")
    q_own = queries.reshape(2 * QROWS, HD)
    kv = jnp.concatenate([prefix_keys, prefix_values], axis=0).reshape(BLOCK, HD)
    up1 = lax.ppermute(kv, "rep", z_perm(1))
    dn1 = lax.ppermute(kv, "rep", z_perm(-1))
    sent, local = pl.pallas_call(
        pack_kernel,
        out_shape=[
            jax.ShapeDtypeStruct((2 * QROWS + 16, HD), BF),
            jax.ShapeDtypeStruct((PAGES_AT + 2 * LOCAL_PAGES * 128, HD), BF),
        ],
        in_specs=[ANY] * 5 + [VMEM] * 2 + [ANY],
        out_specs=[VMEM] * 2,
        scratch_shapes=[pltpu.SemaphoreType.DMA((6,))],
        compiler_params=pltpu.CompilerParams(vmem_limit_bytes=59 << 20),
        name="pack",
    )(
        q_own, tree_keys.reshape(-1, HD), tree_values.reshape(-1, HD),
        prefix_keys.reshape(-1, HD), prefix_values.reshape(-1, HD), page_table, tree_parent.reshape(1, -1),
        kv,
    )
    up1, dn1, sent = lax.optimization_barrier((up1, dn1, sent))
    up2 = lax.ppermute(up1, "rep", z_perm(1))
    dn2 = lax.ppermute(dn1, "rep", z_perm(-1))
    sents = [lax.ppermute(sent, "rep", group_perm(r)) for r in (1, 2, 3)]
    up3 = lax.ppermute(up2, "rep", z_perm(1))
    dn3 = lax.ppermute(dn2, "rep", z_perm(-1))
    held = jnp.where((rep & 1) == 0, up2, dn2)
    opposite = lax.ppermute(
        held, "rep", [(rep_of(a, z, c), rep_of(a, z + 2 - 4 * c, c)) for a in range(2) for z in range(Z) for c in range(2)]
    )

    reps = jnp.arange(32, dtype=jnp.int32)
    same = ((reps ^ rep) & 17) == 0
    step = ((reps >> 1) - (rep >> 1)) & 7
    maps = jnp.full((32,), -(1 << 20), jnp.int32)
    for k, offsets in enumerate(GROUPS):
        for i, o in enumerate(offsets):
            maps = jnp.where(same & (step == o % Z), k * 65536 + i * 8, maps)
    q_all, list_far, *state = near_call(maps, local, *sents, up1, dn1, up2, dn2)
    own, p1, p2, p3 = far_call(list_far, q_all, (up3, dn3, opposite), state)
    back = [lax.ppermute(p, "rep", group_perm(r)) for r, p in ((3, p3), (2, p2), (1, p1))]
    width = out_weight.shape[1]
    attn = pl.pallas_call(
        combine_kernel,
        out_shape=jax.ShapeDtypeStruct((128, 512), BF),
        in_specs=[SMEM] + [VMEM] * 4,
        out_specs=VMEM,
        scratch_shapes=[pltpu.VMEM((2 * QROWS, HD), F32)],
        compiler_params=pltpu.CompilerParams(vmem_limit_bytes=24 << 20),
        cost_estimate=pl.CostEstimate(flops=10**6, bytes_accessed=1 << 20, transcendentals=4096),
        name="combine",
    )(head.reshape(1).astype(jnp.int32), own, *back)
    rows = jnp.dot(attn, out_weight, preferred_element_type=F32).astype(BF)
    parts = [rows[k * 16:(k + 1) * 16] for k in range(8)]
    terms = [
        lax.ppermute(part, "head", [(i, ((i & 4) ^ (dx * 4)) + ((i + dy) & 3)) for i in range(8)])
        for part, (dx, dy) in zip(parts[1:], HEADS[1:])
    ]
    return pl.pallas_call(
        sum_kernel,
        out_shape=jax.ShapeDtypeStruct((16, width), BF),
        in_specs=[VMEM] * 8,
        out_specs=VMEM,
        compiler_params=pltpu.CompilerParams(vmem_limit_bytes=24 << 20),
        name="sum_heads",
    )(parts[0], *terms)


def solution(mesh):
    in_specs = (
        P("rep", "head", None),
        P("rep", "head", None),
        P("rep", "head", None),
        P("rep", "head", None, None),
        P("rep", "head", None, None),
        P("rep"),
        P("rep", None),
        P("head", None),
    )
    out_specs = P(("rep", "head"), None)
    return jax.shard_map(
        on_device, mesh=mesh, in_specs=in_specs, out_specs=out_specs, check_vma=False
    )
```

```python
import functools
import math

import jax
import jax.numpy as jnp
from jax import lax
from jax.experimental import pallas as pl
from jax.experimental.pallas import tpu as pltpu
from jax.sharding import PartitionSpec as P

NEG = -1e30
Z = 8
GROUP = 4
LOCAL_PAGES = 4
TK_AT = 528
TV_AT = 656
BLOCK = 1024
PAGES_AT = 784
TREE = 64
QROWS = 256
HD = 128
SESS = 8
C2 = (HD ** -0.5) * math.log2(math.e)
BF = jnp.bfloat16
F32 = jnp.float32

STREAMS = 4
GROUPS = ((0, -1, 1, -2, 2), (-3, 3, 4))


HEADS = ((0, 0), (1, 0), (0, 2), (1, 2), (0, 1), (1, 1), (0, 3), (1, 3))


def rep_of(xh, z, c):
    return xh * 16 + (z % Z) * 2 + c


def z_perm(k):
    return [(rep_of(a, z, c), rep_of(a, z + k, c)) for a in range(2) for z in range(Z) for c in range(2)]


def group_perm(r):
    return [(rep_of(a, z, c), rep_of(a ^ (r >> 1), z, c ^ (r & 1))) for a in range(2) for z in range(Z) for c in range(2)]


def page(kv, i):
    return kv[pl.ds(pl.multiple_of(i * 128, 128), 128), :]


def pair_steps(entries, q_ref, kv, streams):
    at = [(e >> 8, e & 255) for e in entries]
    scores = [
        lax.dot_general(page(kv, k), q_ref[pl.ds(pl.multiple_of((s & (SESS - 1)) * QROWS, QROWS), QROWS), :], (((1,), (1,)), ((), ())), preferred_element_type=F32)
        for s, k in at
    ]
    olds = [m[s] for (s, _), (m, _, _) in zip(at, streams)]
    news = [jnp.maximum(o, jnp.max(x, axis=0, keepdims=True)) for o, x in zip(olds, scores)]
    probs = [jnp.exp2(x * C2 - n * C2) for x, n in zip(scores, news)]
    fixes = [jnp.exp2((o - n) * C2) for o, n in zip(olds, news)]
    parts = [
        lax.dot_general(
            page(kv, k + LOCAL_PAGES), p.astype(BF), (((0,), (0,)), ((), ())), preferred_element_type=F32
        )
        for (_, k), p in zip(at, probs)
    ]
    for (s, _), n, p, fix, part, (m_ref, l_ref, a_ref) in zip(at, news, probs, fixes, parts, streams):
        m_ref[s] = n
        l_ref[s] = l_ref[s] * fix + jnp.sum(p, axis=0, keepdims=True)
        a_ref[s] = a_ref[s] * fix + part


def all_pairs(entries, q_ref, kv, streams):
    ns = len(streams)

    @pl.loop(0, (entries[0] + ns - 1) >> (ns.bit_length() - 1))
    def _(i):
        pair_steps([entries[ns * i + r + 1] for r in range(ns)], q_ref, kv, streams)


def streams_of(refs):
    return [tuple(refs[3 * r:3 * r + 3]) for r in range(STREAMS)]


def clear(streams):
    for m_ref, l_ref, a_ref in streams:
        m_ref[...] = jnp.full(m_ref.shape, NEG, F32)
        l_ref[...] = jnp.zeros(l_ref.shape, F32)
        a_ref[...] = jnp.zeros(a_ref.shape, F32)


def merge(states):
    top = functools.reduce(jnp.maximum, [m for m, _, _ in states])
    ws = [jnp.exp2((m - top) * C2) for m, _, _ in states]
    total = sum(w * l for w, (_, l, _) in zip(ws, states))
    acc = sum(w * a for w, (_, _, a) in zip(ws, states))
    return top, total, acc


def pack_kernel(q, tk, tv, pk, pv, table, parent, kv, sent, local, sems):
    del kv
    copies = [
        pltpu.make_async_copy(q, sent.at[pl.ds(0, 2 * QROWS)], sems.at[0]),
        pltpu.make_async_copy(q, local.at[pl.ds(0, 2 * QROWS)], sems.at[1]),
        pltpu.make_async_copy(tk, local.at[pl.ds(TK_AT, 128)], sems.at[2]),
        pltpu.make_async_copy(tv, local.at[pl.ds(TV_AT, 128)], sems.at[3]),
        pltpu.make_async_copy(pk, local.at[pl.ds(PAGES_AT, LOCAL_PAGES * 128)], sems.at[4]),
        pltpu.make_async_copy(pv, local.at[pl.ds(PAGES_AT + LOCAL_PAGES * 128, LOCAL_PAGES * 128)], sems.at[5]),
    ]
    for cp in copies:
        cp.start()
    ids = table[...].astype(F32)
    row = lax.broadcasted_iota(jnp.int32, (16, 128), 0)
    above = parent[...].astype(F32)
    tail = pl.ds(2 * QROWS, 16)
    sent[tail, :] = jnp.zeros((16, 128), BF)
    local[tail, :] = jnp.where(row == 2, above, 0.0).astype(BF)
    row = row[:, :16]
    pages = jnp.where(row == 0, ids[0:1, :], jnp.where(row == 1, ids[1:2, :], 0.0))
    sent[tail, :16] = pages.astype(BF)
    local[tail, :16] = jnp.where(row == 2, above[:, :16], pages).astype(BF)
    for cp in copies:
        cp.wait()


def near_kernel(maps, local, s1, s2, s3, up1, dn1, up2, dn2, q_out, list_far, *refs):
    m_out, l_out, a_out, tails, ids, tbl, list_near, found, kv = refs[:9]
    lists = (list_near, list_far)
    streams = streams_of(refs[9:-1])
    sems = refs[-1]
    sents = (local, s1, s2, s3)
    for r, x in enumerate(sents):
        tails[pl.ds(r * 16, 16), :] = x[pl.ds(2 * QROWS, 16), :]
    ids[...] = tails[...].astype(F32).astype(jnp.int32)
    to_scalar = pltpu.make_async_copy(ids, tbl, sems.at[0])
    to_scalar.start()
    copies = load_blocks(
        [local.at[pl.ds(PAGES_AT, BLOCK)], up1, dn1, up2, dn2], kv, [sems.at[i + 1] for i in range(5)]
    )
    for r, x in enumerate(sents):
        q_out[pl.ds(r * 2 * QROWS, 2 * QROWS), :] = x[pl.ds(0, 2 * QROWS), :]
    clear(streams)
    both = 2 * TREE
    row = lax.broadcasted_iota(jnp.int32, (both, both), 0)
    lane = lax.broadcasted_iota(jnp.int32, (both, both), 1)
    above = ids[2:3, :] + jnp.where(lax.broadcasted_iota(jnp.int32, (1, both), 1) >= TREE, TREE, 0)
    reach = jnp.minimum((row == lane).astype(F32) + (row == above).astype(F32), 1.0)
    for _ in range(7):
        half = reach.astype(BF)
        reach = jnp.minimum(jnp.dot(half, half, preferred_element_type=F32), 1.0)
    half = reach.astype(BF)
    tree_row = lax.broadcasted_iota(jnp.int32, (both, QROWS), 0)
    of_query = lax.shift_right_logical(lax.broadcasted_iota(jnp.int32, (both, QROWS), 1), 2)
    m0, l0, a0 = streams[0]
    for s in range(2):
        widen = (tree_row == of_query + s * TREE).astype(BF)
        seen = jnp.dot(half[s * TREE:(s + 1) * TREE, :], widen, preferred_element_type=F32)
        scores = lax.dot_general(
            local[pl.ds(TK_AT + s * TREE, TREE), :],
            local[pl.ds(s * QROWS, QROWS), :],
            (((1,), (1,)), ((), ())),
            preferred_element_type=F32,
        )
        scores = jnp.where(seen > 0.5, scores, NEG)
        top = jnp.max(scores, axis=0, keepdims=True)
        probs = jnp.exp2(scores * C2 - top * C2)
        m0[s] = top
        l0[s] = jnp.sum(probs, axis=0, keepdims=True)
        a0[s] = lax.dot_general(
            local[pl.ds(TV_AT + s * TREE, TREE), :],
            probs.astype(BF),
            (((0,), (0,)), ((), ())),
            preferred_element_type=F32,
        )
    to_scalar.wait()

    def scan(r, n):
        for half in range(2):
            pages = [tbl[r * 16 + half, j] for j in range(16)]
            at = [maps[p >> 2] for p in pages]
            for p, where in zip(pages, at):
                found[n] = (r * 2 + half) * 256 + (p & 3) + where
                n = n + (where >= 0).astype(jnp.int32)
        return n

    total = lax.fori_loop(0, GROUP, scan, jnp.int32(0))

    def sort(i, counts):
        entry = found[i]
        kind = entry >> 16
        out = []
        for k in range(2):
            lists[k][counts[k] + 1] = entry & 65535
            out.append(counts[k] + (kind == k).astype(jnp.int32))
        return tuple(out)

    counts = lax.fori_loop(0, total, sort, (jnp.int32(0),) * 2)
    for k in range(2):
        lists[k][0] = counts[k]
        for r in range(STREAMS - 1):
            lists[k][counts[k] + 1 + r] = jnp.int32(SESS * 256)
    for cp in copies:
        cp.wait()
    all_pairs(list_near, q_out, kv, streams)
    for s in range(SESS):
        top, total, acc = merge([(m[s], l[s], a[s]) for m, l, a in streams])
        m_out[s] = top
        l_out[s] = total
        a_out[s] = acc


def load_blocks(blocks, kv, sems):
    copies = [pltpu.make_async_copy(b, kv.at[pl.ds(i * BLOCK, BLOCK)], sem) for i, (b, sem) in enumerate(zip(blocks, sems))]
    for cp in copies:
        cp.start()
    return copies


def far_kernel(nb, *refs):
    list_far, q_ref = refs[:2]
    blocks = refs[2:2 + nb]
    before = refs[2 + nb:5 + nb]
    own = refs[5 + nb]
    outs = refs[6 + nb:9 + nb]
    kv = refs[9 + nb]
    streams = streams_of(refs[10 + nb:-1])
    copies = load_blocks(blocks, kv, [refs[-1].at[i] for i in range(nb)])
    clear(streams)
    for cp in copies:
        cp.wait()
    all_pairs(list_far, q_ref, kv, streams)
    for s in range(SESS):
        top, total, acc = merge([(m[s], l[s], a[s]) for m, l, a in [before] + streams])
        some = total > 0.0
        safe = jnp.where(some, total, 1.0)
        acc = acc * (1.0 / safe)
        lse = jnp.where(some, top * C2 + jnp.log2(safe), NEG)
        lanes = pl.ds((s % 2) * QROWS, QROWS)
        if s < 2:
            own[pl.ds(0, HD), lanes] = acc
            own[pl.ds(HD, 8), lanes] = jnp.broadcast_to(lse, (8, QROWS))
        else:
            out = outs[s // 2 - 1]
            out[pl.ds(0, HD), lanes] = acc.astype(BF)
            hi = lse.astype(BF).astype(F32)
            mid = (lse - hi).astype(BF).astype(F32)
            low = lse - hi - mid
            row = lax.broadcasted_iota(jnp.int32, (16, QROWS), 0)
            parts = jnp.where(row == 0, hi, jnp.where(row == 1, mid, jnp.where(row == 2, low, 0.0)))
            out[pl.ds(HD, 16), lanes] = parts.astype(BF)


def combine_kernel(head_ref, own, p1, p2, p3, attn, rows_f32):
    lses = [own[HD:HD + 1, :]]
    vals = [own[:HD, :]]
    for p in (p1, p2, p3):
        tail = p[HD:HD + 16, :].astype(F32)
        lses.append(tail[0:1] + tail[1:2] + tail[2:3])
        vals.append(p[:HD, :].astype(F32))
    top = functools.reduce(jnp.maximum, lses)
    ws = [jnp.exp2(x - top) for x in lses]
    inv = 1.0 / sum(ws)
    mixed = sum(v * (w * inv) for v, w in zip(vals, ws))
    rows_f32[...] = mixed.T
    for k, (dx, dy) in enumerate(HEADS):
        first = ((head_ref[0] & 4) ^ (dx * 4)) * 64 + ((head_ref[0] + dy) & 3) * 64
        for h in range(4):
            block = rows_f32[pl.ds(first + h, 16, stride=4), :]
            attn[pl.ds(k * 16, 16), pl.ds(h * HD, HD)] = block.astype(BF)


def sum_y_kernel(p0, p1, p2, p3, mine, other):
    total = functools.reduce(jnp.add, [r[...].astype(F32) for r in (p0, p1, p2, p3)])
    mine[...] = total[:16]
    other[...] = total[16:].astype(BF)


def sum_x_kernel(mine, got, out):
    out[...] = (mine[...] + got[...].astype(F32)).astype(BF)


VMEM = pl.BlockSpec(memory_space=pltpu.VMEM)
SMEM = pl.BlockSpec(memory_space=pltpu.SMEM)
ANY = pl.BlockSpec(memory_space=pl.ANY)


def stream_scratch():
    return [
        pltpu.VMEM((SESS + 1, 1, QROWS), F32),
        pltpu.VMEM((SESS + 1, 1, QROWS), F32),
        pltpu.VMEM((SESS + 1, HD, QROWS), F32),
    ]


def state_shapes(n):
    return [
        jax.ShapeDtypeStruct((n, 1, QROWS), F32),
        jax.ShapeDtypeStruct((n, 1, QROWS), F32),
        jax.ShapeDtypeStruct((n, HD, QROWS), F32),
    ]


def near_call(*args):
    return pl.pallas_call(
        near_kernel,
        out_shape=[jax.ShapeDtypeStruct((SESS * QROWS, HD), BF), jax.ShapeDtypeStruct((160,), jnp.int32)]
        + state_shapes(SESS),
        in_specs=[SMEM] + [VMEM] * 4 + [ANY] * 4,
        out_specs=[VMEM, SMEM] + [VMEM] * 3,
        scratch_shapes=[
            pltpu.VMEM((64, 128), BF),
            pltpu.VMEM((64, 128), jnp.int32),
            pltpu.SMEM((64, 128), jnp.int32),
            pltpu.SMEM((160,), jnp.int32),
            pltpu.SMEM((160,), jnp.int32),
            pltpu.VMEM((5 * BLOCK, HD), BF),
        ]
        + stream_scratch() * STREAMS
        + [pltpu.SemaphoreType.DMA((6,))],
        compiler_params=pltpu.CompilerParams(vmem_limit_bytes=24 << 20),
        cost_estimate=pl.CostEstimate(flops=4 * 10**9, bytes_accessed=4 << 20, transcendentals=1 << 20),
        name="near_pages",
    )(*args)


def far_call(pages, q_all, blocks, state):
    nb = len(blocks)
    return pl.pallas_call(
        functools.partial(far_kernel, nb),
        out_shape=[jax.ShapeDtypeStruct((HD + 8, 2 * QROWS), F32)]
        + [jax.ShapeDtypeStruct((HD + 16, 2 * QROWS), BF)] * 3,
        in_specs=[SMEM, VMEM] + [ANY] * nb + [VMEM] * 3,
        out_specs=[VMEM] * 4,
        scratch_shapes=[pltpu.VMEM((nb * BLOCK, HD), BF)]
        + stream_scratch() * STREAMS
        + [pltpu.SemaphoreType.DMA((nb,))],
        compiler_params=pltpu.CompilerParams(vmem_limit_bytes=24 << 20),
        cost_estimate=pl.CostEstimate(flops=10**9, bytes_accessed=4 << 20, transcendentals=1 << 20),
        name="far_pages",
    )(pages, q_all, *blocks, *state)


def on_device(
    queries, tree_keys, tree_values, prefix_keys, prefix_values, tree_parent, page_table, out_weight
):
    rep = lax.axis_index("rep")
    head = lax.axis_index("head")
    q_own = queries.reshape(2 * QROWS, HD)
    kv = jnp.concatenate([prefix_keys, prefix_values], axis=0).reshape(BLOCK, HD)
    up1 = lax.ppermute(kv, "rep", z_perm(1))
    dn1 = lax.ppermute(kv, "rep", z_perm(-1))
    sent, local = pl.pallas_call(
        pack_kernel,
        out_shape=[
            jax.ShapeDtypeStruct((2 * QROWS + 16, HD), BF),
            jax.ShapeDtypeStruct((PAGES_AT + 2 * LOCAL_PAGES * 128, HD), BF),
        ],
        in_specs=[ANY] * 5 + [VMEM] * 2 + [ANY],
        out_specs=[VMEM] * 2,
        scratch_shapes=[pltpu.SemaphoreType.DMA((6,))],
        compiler_params=pltpu.CompilerParams(vmem_limit_bytes=59 << 20),
        name="pack",
    )(
        q_own, tree_keys.reshape(-1, HD), tree_values.reshape(-1, HD),
        prefix_keys.reshape(-1, HD), prefix_values.reshape(-1, HD), page_table, tree_parent.reshape(1, -1),
        kv,
    )
    up1, dn1, sent = lax.optimization_barrier((up1, dn1, sent))
    up2 = lax.ppermute(up1, "rep", z_perm(1))
    dn2 = lax.ppermute(dn1, "rep", z_perm(-1))
    sents = [lax.ppermute(sent, "rep", group_perm(r)) for r in (1, 2, 3)]
    up3 = lax.ppermute(up2, "rep", z_perm(1))
    dn3 = lax.ppermute(dn2, "rep", z_perm(-1))
    held = jnp.where((rep & 1) == 0, up2, dn2)
    opposite = lax.ppermute(
        held, "rep", [(rep_of(a, z, c), rep_of(a, z + 2 - 4 * c, c)) for a in range(2) for z in range(Z) for c in range(2)]
    )

    reps = jnp.arange(32, dtype=jnp.int32)
    same = ((reps ^ rep) & 17) == 0
    step = ((reps >> 1) - (rep >> 1)) & 7
    maps = jnp.full((32,), -(1 << 20), jnp.int32)
    for k, offsets in enumerate(GROUPS):
        for i, o in enumerate(offsets):
            maps = jnp.where(same & (step == o % Z), k * 65536 + i * 8, maps)
    q_all, list_far, *state = near_call(maps, local, *sents, up1, dn1, up2, dn2)
    own, p1, p2, p3 = far_call(list_far, q_all, (up3, dn3, opposite), state)
    back = [lax.ppermute(p, "rep", group_perm(r)) for r, p in ((3, p3), (2, p2), (1, p1))]
    width = out_weight.shape[1]
    attn = pl.pallas_call(
        combine_kernel,
        out_shape=jax.ShapeDtypeStruct((128, 512), BF),
        in_specs=[SMEM] + [VMEM] * 4,
        out_specs=VMEM,
        scratch_shapes=[pltpu.VMEM((2 * QROWS, HD), F32)],
        compiler_params=pltpu.CompilerParams(vmem_limit_bytes=24 << 20),
        cost_estimate=pl.CostEstimate(flops=10**6, bytes_accessed=1 << 20, transcendentals=4096),
        name="combine",
    )(head.reshape(1).astype(jnp.int32), own, *back)
    rows = jnp.dot(attn, out_weight, preferred_element_type=F32).astype(BF)
    parts = [rows[k * 32:(k + 1) * 32] for k in range(4)]
    terms = [
        lax.ppermute(part, "head", [(i, (i & 4) + ((i + dy) & 3)) for i in range(8)])
        for part, (_, dy) in zip(parts[1:], HEADS[2::2])
    ]
    mine, other = pl.pallas_call(
        sum_y_kernel,
        out_shape=[jax.ShapeDtypeStruct((16, width), F32), jax.ShapeDtypeStruct((16, width), BF)],
        in_specs=[VMEM] * 4,
        out_specs=[VMEM] * 2,
        compiler_params=pltpu.CompilerParams(vmem_limit_bytes=16 << 20),
        name="sum_along_y",
    )(parts[0], *terms)
    got = lax.ppermute(other, "head", [(i, i ^ 4) for i in range(8)])
    return pl.pallas_call(
        sum_x_kernel,
        out_shape=jax.ShapeDtypeStruct((16, width), BF),
        in_specs=[VMEM] * 2,
        out_specs=VMEM,
        compiler_params=pltpu.CompilerParams(vmem_limit_bytes=16 << 20),
        name="sum_along_x",
    )(mine, got)


def solution(mesh):
    in_specs = (
        P("rep", "head", None),
        P("rep", "head", None),
        P("rep", "head", None),
        P("rep", "head", None, None),
        P("rep", "head", None, None),
        P("rep"),
        P("rep", None),
        P("head", None),
    )
    out_specs = P(("rep", "head"), None)
    return jax.shard_map(
        on_device, mesh=mesh, in_specs=in_specs, out_specs=out_specs, check_vma=False
    )
```

```python
import functools
import math

import jax
import jax.numpy as jnp
from jax import lax
from jax.experimental import pallas as pl
from jax.experimental.pallas import tpu as pltpu
from jax.sharding import PartitionSpec as P

NEG = -1e30
Z = 8
GROUP = 4
LOCAL_PAGES = 4
TK_AT = 528
TV_AT = 656
BLOCK = 1024
PAGES_AT = 784
TREE = 64
QROWS = 256
HD = 128
SESS = 8
C2 = (HD ** -0.5) * math.log2(math.e)
BF = jnp.bfloat16
F32 = jnp.float32

STREAMS = 4
GROUPS = ((0, -1, 1, -2, 2), (-3, 3, 4))


HEADS = ((0, 0), (0, 1), (0, 3), (0, 2), (1, 0), (1, 1), (1, 3), (1, 2))


def rep_of(xh, z, c):
    return xh * 16 + (z % Z) * 2 + c


def z_perm(k):
    return [(rep_of(a, z, c), rep_of(a, z + k, c)) for a in range(2) for z in range(Z) for c in range(2)]


def group_perm(r):
    return [(rep_of(a, z, c), rep_of(a ^ (r >> 1), z, c ^ (r & 1))) for a in range(2) for z in range(Z) for c in range(2)]


def page(kv, i):
    return kv[pl.ds(pl.multiple_of(i * 128, 128), 128), :]


def pair_steps(entries, q_ref, kv, streams):
    at = [(e >> 8, e & 255) for e in entries]
    scores = [
        lax.dot_general(page(kv, k), q_ref[pl.ds(pl.multiple_of((s & (SESS - 1)) * QROWS, QROWS), QROWS), :], (((1,), (1,)), ((), ())), preferred_element_type=F32)
        for s, k in at
    ]
    olds = [m[s] for (s, _), (m, _, _) in zip(at, streams)]
    news = [jnp.maximum(o, jnp.max(x, axis=0, keepdims=True)) for o, x in zip(olds, scores)]
    probs = [jnp.exp2(x * C2 - n * C2) for x, n in zip(scores, news)]
    fixes = [jnp.exp2((o - n) * C2) for o, n in zip(olds, news)]
    parts = [
        lax.dot_general(
            page(kv, k + LOCAL_PAGES), p.astype(BF), (((0,), (0,)), ((), ())), preferred_element_type=F32
        )
        for (_, k), p in zip(at, probs)
    ]
    for (s, _), o, n, p, fix, part, (m_ref, l_ref, a_ref) in zip(at, olds, news, probs, fixes, parts, streams):
        m_ref[s] = n
        l_ref[s] = l_ref[s] * fix + jnp.sum(p, axis=0, keepdims=True)
        a_ref[s] = jnp.where(o > NEG, a_ref[s] * fix, 0.0) + part


def all_pairs(entries, q_ref, kv, streams):
    ns = len(streams)

    @pl.loop(0, (entries[0] + ns - 1) >> (ns.bit_length() - 1))
    def _(i):
        pair_steps([entries[ns * i + r + 1] for r in range(ns)], q_ref, kv, streams)


def streams_of(refs):
    return [tuple(refs[3 * r:3 * r + 3]) for r in range(STREAMS)]


def clear(streams):
    for m_ref, l_ref, _ in streams:
        m_ref[...] = jnp.full(m_ref.shape, NEG, F32)
        l_ref[...] = jnp.zeros(l_ref.shape, F32)


def merge(states):
    top = functools.reduce(jnp.maximum, [m for m, _, _ in states])
    ws = [jnp.exp2((m - top) * C2) for m, _, _ in states]
    total = sum(w * l for w, (_, l, _) in zip(ws, states))
    acc = sum(jnp.where(m > NEG, w * a, 0.0) for w, (m, _, a) in zip(ws, states))
    return top, total, acc


def pack_kernel(q, tk, tv, pk, pv, table, parent, kv, sent, local, sems):
    del kv
    copies = [
        pltpu.make_async_copy(q, sent.at[pl.ds(0, 2 * QROWS)], sems.at[0]),
        pltpu.make_async_copy(q, local.at[pl.ds(0, 2 * QROWS)], sems.at[1]),
        pltpu.make_async_copy(tk, local.at[pl.ds(TK_AT, 128)], sems.at[2]),
        pltpu.make_async_copy(tv, local.at[pl.ds(TV_AT, 128)], sems.at[3]),
        pltpu.make_async_copy(pk, local.at[pl.ds(PAGES_AT, LOCAL_PAGES * 128)], sems.at[4]),
        pltpu.make_async_copy(pv, local.at[pl.ds(PAGES_AT + LOCAL_PAGES * 128, LOCAL_PAGES * 128)], sems.at[5]),
    ]
    for cp in copies:
        cp.start()
    ids = table[...].astype(F32)
    row = lax.broadcasted_iota(jnp.int32, (16, 128), 0)
    above = parent[...].astype(F32)
    tail = pl.ds(2 * QROWS, 16)
    sent[tail, :] = jnp.zeros((16, 128), BF)
    local[tail, :] = jnp.where(row == 2, above, 0.0).astype(BF)
    row = row[:, :16]
    pages = jnp.where(row == 0, ids[0:1, :], jnp.where(row == 1, ids[1:2, :], 0.0))
    sent[tail, :16] = pages.astype(BF)
    local[tail, :16] = jnp.where(row == 2, above[:, :16], pages).astype(BF)
    for cp in copies:
        cp.wait()


def near_kernel(maps, local, s1, s2, s3, up1, dn1, up2, dn2, q_out, list_far, list_far_x, *refs):
    m_out, l_out, a_out, tails, ids, tbl, list_near, found, kv = refs[:9]
    lists = (list_near, list_far, list_far_x)
    streams = streams_of(refs[9:-1])
    sems = refs[-1]
    sents = (local, s1, s2, s3)
    for r, x in enumerate(sents):
        tails[pl.ds(r * 16, 16), :] = x[pl.ds(2 * QROWS, 16), :]
    ids[...] = tails[...].astype(F32).astype(jnp.int32)
    to_scalar = pltpu.make_async_copy(ids, tbl, sems.at[0])
    to_scalar.start()
    copies = load_blocks(
        [local.at[pl.ds(PAGES_AT, BLOCK)], up1, dn1, up2, dn2], kv, [sems.at[i + 1] for i in range(5)]
    )
    for r, x in enumerate(sents):
        q_out[pl.ds(r * 2 * QROWS, 2 * QROWS), :] = x[pl.ds(0, 2 * QROWS), :]
    clear(streams)
    both = 2 * TREE
    row = lax.broadcasted_iota(jnp.int32, (both, both), 0)
    lane = lax.broadcasted_iota(jnp.int32, (both, both), 1)
    above = ids[2:3, :] + jnp.where(lax.broadcasted_iota(jnp.int32, (1, both), 1) >= TREE, TREE, 0)
    reach = jnp.minimum((row == lane).astype(F32) + (row == above).astype(F32), 1.0)
    for _ in range(7):
        half = reach.astype(BF)
        reach = jnp.minimum(jnp.dot(half, half, preferred_element_type=F32), 1.0)
    half = reach.astype(BF)
    tree_row = lax.broadcasted_iota(jnp.int32, (both, QROWS), 0)
    of_query = lax.shift_right_logical(lax.broadcasted_iota(jnp.int32, (both, QROWS), 1), 2)
    m0, l0, a0 = streams[0]
    for s in range(2):
        widen = (tree_row == of_query + s * TREE).astype(BF)
        seen = jnp.dot(half[s * TREE:(s + 1) * TREE, :], widen, preferred_element_type=F32)
        scores = lax.dot_general(
            local[pl.ds(TK_AT + s * TREE, TREE), :],
            local[pl.ds(s * QROWS, QROWS), :],
            (((1,), (1,)), ((), ())),
            preferred_element_type=F32,
        )
        scores = jnp.where(seen > 0.5, scores, NEG)
        top = jnp.max(scores, axis=0, keepdims=True)
        probs = jnp.exp2(scores * C2 - top * C2)
        m0[s] = top
        l0[s] = jnp.sum(probs, axis=0, keepdims=True)
        a0[s] = lax.dot_general(
            local[pl.ds(TV_AT + s * TREE, TREE), :],
            probs.astype(BF),
            (((0,), (0,)), ((), ())),
            preferred_element_type=F32,
        )
    to_scalar.wait()

    def scan(r, n):
        for half in range(2):
            pages = [tbl[r * 16 + half, j] for j in range(16)]
            at = [maps[p >> 2] for p in pages]
            for p, where in zip(pages, at):
                found[n] = (r * 2 + half) * 256 + (p & 3) + where
                n = n + (where >= 0).astype(jnp.int32)
        return n

    total = lax.fori_loop(0, GROUP, scan, jnp.int32(0))

    def sort(i, counts):
        entry = found[i]
        kind = entry >> 16
        kind = kind + (kind & (entry >> 10))
        out = []
        for k in range(3):
            lists[k][counts[k] + 1] = entry & 65535
            out.append(counts[k] + (kind == k).astype(jnp.int32))
        return tuple(out)

    counts = lax.fori_loop(0, total, sort, (jnp.int32(0),) * 3)
    for k in range(3):
        lists[k][0] = counts[k]
        for r in range(STREAMS - 1):
            lists[k][counts[k] + 1 + r] = jnp.int32(SESS * 256)
    for cp in copies:
        cp.wait()
    all_pairs(list_near, q_out, kv, streams)
    for s in range(SESS):
        top, total, acc = merge([(m[s], l[s], a[s]) for m, l, a in streams])
        m_out[s] = top
        l_out[s] = total
        a_out[s] = acc


def load_blocks(blocks, kv, sems):
    copies = [pltpu.make_async_copy(b, kv.at[pl.ds(i * BLOCK, BLOCK)], sem) for i, (b, sem) in enumerate(zip(blocks, sems))]
    for cp in copies:
        cp.start()
    return copies


def far_kernel(nb, first, *refs):
    list_far, q_ref = refs[:2]
    blocks = refs[2:2 + nb]
    before = refs[2 + nb:5 + nb]
    outs = refs[5 + nb:7 + nb]
    kv = refs[7 + nb]
    streams = streams_of(refs[8 + nb:-1])
    copies = load_blocks(blocks, kv, [refs[-1].at[i] for i in range(nb)])
    clear(streams)
    for cp in copies:
        cp.wait()
    all_pairs(list_far, q_ref, kv, streams)
    for s in range(first, first + SESS // 2):
        top, total, acc = merge([(m[s], l[s], a[s]) for m, l, a in [before] + streams])
        some = total > 0.0
        safe = jnp.where(some, total, 1.0)
        acc = acc * (1.0 / safe)
        lse = jnp.where(some, top * C2 + jnp.log2(safe), NEG)
        lanes = pl.ds((s % 2) * QROWS, QROWS)
        if s < 2:
            outs[0][pl.ds(0, HD), lanes] = acc
            outs[0][pl.ds(HD, 8), lanes] = jnp.broadcast_to(lse, (8, QROWS))
        else:
            out = outs[(s - first) // 2]
            out[pl.ds(0, HD), lanes] = acc.astype(BF)
            hi = lse.astype(BF).astype(F32)
            mid = (lse - hi).astype(BF).astype(F32)
            low = lse - hi - mid
            row = lax.broadcasted_iota(jnp.int32, (16, QROWS), 0)
            parts = jnp.where(row == 0, hi, jnp.where(row == 1, mid, jnp.where(row == 2, low, 0.0)))
            out[pl.ds(HD, 16), lanes] = parts.astype(BF)


def combine_kernel(head_ref, own, p1, p2, p3, attn, rows_f32):
    lses = [own[HD:HD + 1, :]]
    vals = [own[:HD, :]]
    for p in (p1, p2, p3):
        tail = p[HD:HD + 16, :].astype(F32)
        lses.append(tail[0:1] + tail[1:2] + tail[2:3])
        vals.append(p[:HD, :].astype(F32))
    top = functools.reduce(jnp.maximum, lses)
    ws = [jnp.exp2(x - top) for x in lses]
    inv = 1.0 / sum(ws)
    mixed = sum(v * (w * inv) for v, w in zip(vals, ws))
    rows_f32[...] = mixed.T
    for k, (dx, dy) in enumerate(HEADS):
        first = ((head_ref[0] & 4) ^ (dx * 4)) * 64 + ((head_ref[0] + dy) & 3) * 64
        for h in range(4):
            block = rows_f32[pl.ds(first + h, 16, stride=4), :]
            attn[pl.ds(k * 16, 16), pl.ds(h * HD, HD)] = block.astype(BF)


def sum_kernel(*refs):
    out = refs[-1]
    out[...] = functools.reduce(jnp.add, [r[...].astype(F32) for r in refs[:-1]]).astype(BF)


VMEM = pl.BlockSpec(memory_space=pltpu.VMEM)
SMEM = pl.BlockSpec(memory_space=pltpu.SMEM)
ANY = pl.BlockSpec(memory_space=pl.ANY)


def stream_scratch():
    return [
        pltpu.VMEM((SESS + 1, 1, QROWS), F32),
        pltpu.VMEM((SESS + 1, 1, QROWS), F32),
        pltpu.VMEM((SESS + 1, HD, QROWS), F32),
    ]


def state_shapes(n):
    return [
        jax.ShapeDtypeStruct((n, 1, QROWS), F32),
        jax.ShapeDtypeStruct((n, 1, QROWS), F32),
        jax.ShapeDtypeStruct((n, HD, QROWS), F32),
    ]


def near_call(*args):
    return pl.pallas_call(
        near_kernel,
        out_shape=[jax.ShapeDtypeStruct((SESS * QROWS, HD), BF), jax.ShapeDtypeStruct((160,), jnp.int32)]
        + [jax.ShapeDtypeStruct((160,), jnp.int32)]
        + state_shapes(SESS),
        in_specs=[SMEM] + [VMEM] * 4 + [ANY] * 4,
        out_specs=[VMEM, SMEM, SMEM] + [VMEM] * 3,
        scratch_shapes=[
            pltpu.VMEM((64, 128), BF),
            pltpu.VMEM((64, 128), jnp.int32),
            pltpu.SMEM((64, 128), jnp.int32),
            pltpu.SMEM((160,), jnp.int32),
            pltpu.SMEM((160,), jnp.int32),
            pltpu.VMEM((5 * BLOCK, HD), BF),
        ]
        + stream_scratch() * STREAMS
        + [pltpu.SemaphoreType.DMA((6,))],
        compiler_params=pltpu.CompilerParams(vmem_limit_bytes=24 << 20),
        cost_estimate=pl.CostEstimate(flops=4 * 10**9, bytes_accessed=4 << 20, transcendentals=1 << 20),
        name="near_pages",
    )(*args)


def far_call(pages, q_all, blocks, state, first, name):
    nb = len(blocks)
    part = jax.ShapeDtypeStruct((HD + 16, 2 * QROWS), BF)
    own = jax.ShapeDtypeStruct((HD + 8, 2 * QROWS), F32)
    return pl.pallas_call(
        functools.partial(far_kernel, nb, first),
        out_shape=[part if first else own, part],
        in_specs=[SMEM, VMEM] + [ANY] * nb + [VMEM] * 3,
        out_specs=[VMEM] * 2,
        scratch_shapes=[pltpu.VMEM((nb * BLOCK, HD), BF)]
        + stream_scratch() * STREAMS
        + [pltpu.SemaphoreType.DMA((nb,))],
        compiler_params=pltpu.CompilerParams(vmem_limit_bytes=24 << 20),
        cost_estimate=pl.CostEstimate(flops=10**9, bytes_accessed=4 << 20, transcendentals=1 << 20),
        name=name,
    )(pages, q_all, *blocks, *state)


def on_device(
    queries, tree_keys, tree_values, prefix_keys, prefix_values, tree_parent, page_table, out_weight
):
    rep = lax.axis_index("rep")
    head = lax.axis_index("head")
    q_own = queries.reshape(2 * QROWS, HD)
    kv = jnp.concatenate([prefix_keys, prefix_values], axis=0).reshape(BLOCK, HD)
    up1 = lax.ppermute(kv, "rep", z_perm(1))
    dn1 = lax.ppermute(kv, "rep", z_perm(-1))
    sent, local = pl.pallas_call(
        pack_kernel,
        out_shape=[
            jax.ShapeDtypeStruct((2 * QROWS + 16, HD), BF),
            jax.ShapeDtypeStruct((PAGES_AT + 2 * LOCAL_PAGES * 128, HD), BF),
        ],
        in_specs=[ANY] * 5 + [VMEM] * 2 + [ANY],
        out_specs=[VMEM] * 2,
        scratch_shapes=[pltpu.SemaphoreType.DMA((6,))],
        compiler_params=pltpu.CompilerParams(vmem_limit_bytes=59 << 20),
        name="pack",
    )(
        q_own, tree_keys.reshape(-1, HD), tree_values.reshape(-1, HD),
        prefix_keys.reshape(-1, HD), prefix_values.reshape(-1, HD), page_table, tree_parent.reshape(1, -1),
        kv,
    )
    up1, dn1, sent = lax.optimization_barrier((up1, dn1, sent))
    up2 = lax.ppermute(up1, "rep", z_perm(1))
    dn2 = lax.ppermute(dn1, "rep", z_perm(-1))
    sents = [lax.ppermute(sent, "rep", group_perm(r)) for r in (1, 2, 3)]
    up3 = lax.ppermute(up2, "rep", z_perm(1))
    dn3 = lax.ppermute(dn2, "rep", z_perm(-1))
    held = jnp.where((rep & 1) == 0, up2, dn2)
    opposite = lax.ppermute(
        held, "rep", [(rep_of(a, z, c), rep_of(a, z + 2 - 4 * c, c)) for a in range(2) for z in range(Z) for c in range(2)]
    )

    reps = jnp.arange(32, dtype=jnp.int32)
    same = ((reps ^ rep) & 17) == 0
    step = ((reps >> 1) - (rep >> 1)) & 7
    maps = jnp.full((32,), -(1 << 20), jnp.int32)
    for k, offsets in enumerate(GROUPS):
        for i, o in enumerate(offsets):
            maps = jnp.where(same & (step == o % Z), k * 65536 + i * 8, maps)
    q_all, list_far, list_far_x, *state = near_call(maps, local, *sents, up1, dn1, up2, dn2)
    blocks = (up3, dn3, opposite)
    p2, p3 = far_call(list_far_x, q_all, blocks, state, SESS // 2, "far_pages_x")
    p3 = lax.ppermute(p3, "rep", group_perm(3))
    p2 = lax.ppermute(p2, "rep", group_perm(2))
    own, p1 = far_call(list_far, q_all, blocks, state, 0, "far_pages_own")
    back = [p3, p2, lax.ppermute(p1, "rep", group_perm(1))]
    width = out_weight.shape[1]
    attn = pl.pallas_call(
        combine_kernel,
        out_shape=jax.ShapeDtypeStruct((128, 512), BF),
        in_specs=[SMEM] + [VMEM] * 4,
        out_specs=VMEM,
        scratch_shapes=[pltpu.VMEM((2 * QROWS, HD), F32)],
        compiler_params=pltpu.CompilerParams(vmem_limit_bytes=24 << 20),
        cost_estimate=pl.CostEstimate(flops=10**6, bytes_accessed=1 << 20, transcendentals=4096),
        name="combine",
    )(head.reshape(1).astype(jnp.int32), own, *back)
    rows = jnp.dot(attn, out_weight, preferred_element_type=F32).astype(BF)
    parts = [rows[k * 16:(k + 1) * 16] for k in range(8)]
    terms = [
        lax.ppermute(part, "head", [(i, ((i & 4) ^ (dx * 4)) + ((i + dy) & 3)) for i in range(8)])
        for part, (dx, dy) in zip(parts[1:], HEADS[1:])
    ]
    return pl.pallas_call(
        sum_kernel,
        out_shape=jax.ShapeDtypeStruct((16, width), BF),
        in_specs=[VMEM] * 8,
        out_specs=VMEM,
        compiler_params=pltpu.CompilerParams(vmem_limit_bytes=24 << 20),
        name="sum_heads",
    )(parts[0], *terms)


def solution(mesh):
    in_specs = (
        P("rep", "head", None),
        P("rep", "head", None),
        P("rep", "head", None),
        P("rep", "head", None, None),
        P("rep", "head", None, None),
        P("rep"),
        P("rep", None),
        P("head", None),
    )
    out_specs = P(("rep", "head"), None)
    return jax.shard_map(
        on_device, mesh=mesh, in_specs=in_specs, out_specs=out_specs, check_vma=False
    )
```

```python
import functools
import math

import jax
import jax.numpy as jnp
from jax import lax
from jax.experimental import pallas as pl
from jax.experimental.pallas import tpu as pltpu
from jax.sharding import PartitionSpec as P

NEG = -1e30
Z = 8
GROUP = 4
LOCAL_PAGES = 4
TK_AT = 528
TV_AT = 656
BLOCK = 1024
PAGES_AT = 784
TREE = 64
QROWS = 256
HD = 128
SESS = 8
C2 = (HD ** -0.5) * math.log2(math.e)
BF = jnp.bfloat16
F32 = jnp.float32

STREAMS = 4
GROUPS = ((0, -1, 1, -2, 2), (-3, 3, 4))


HEADS = ((0, 0), (0, 1), (0, 3), (0, 2), (1, 0), (1, 1), (1, 3), (1, 2))


def rep_of(xh, z, c):
    return xh * 16 + (z % Z) * 2 + c


def z_perm(k):
    return [(rep_of(a, z, c), rep_of(a, z + k, c)) for a in range(2) for z in range(Z) for c in range(2)]


def group_perm(r):
    return [(rep_of(a, z, c), rep_of(a ^ (r >> 1), z, c ^ (r & 1))) for a in range(2) for z in range(Z) for c in range(2)]


def page(kv, i):
    return kv[pl.ds(pl.multiple_of(i * 128, 128), 128), :]


def pair_steps(entries, q_ref, kv, streams):
    at = [(e >> 8, e & 255) for e in entries]
    scores = [
        lax.dot_general(page(kv, k), q_ref[pl.ds(pl.multiple_of((s & (SESS - 1)) * QROWS, QROWS), QROWS), :], (((1,), (1,)), ((), ())), preferred_element_type=F32)
        for s, k in at
    ]
    olds = [m[s] for (s, _), (m, _, _) in zip(at, streams)]
    news = [jnp.maximum(o, jnp.max(x, axis=0, keepdims=True)) for o, x in zip(olds, scores)]
    probs = [jnp.exp2(x * C2 - n * C2) for x, n in zip(scores, news)]
    fixes = [jnp.exp2((o - n) * C2) for o, n in zip(olds, news)]
    parts = [
        lax.dot_general(
            page(kv, k + LOCAL_PAGES), p.astype(BF), (((0,), (0,)), ((), ())), preferred_element_type=F32
        )
        for (_, k), p in zip(at, probs)
    ]
    for (s, _), o, n, p, fix, part, (m_ref, l_ref, a_ref) in zip(at, olds, news, probs, fixes, parts, streams):
        m_ref[s] = n
        l_ref[s] = l_ref[s] * fix + jnp.sum(p, axis=0, keepdims=True)
        a_ref[s] = jnp.where(o > NEG, a_ref[s] * fix, 0.0) + part


def all_pairs(entries, q_ref, kv, streams):
    ns = len(streams)

    @pl.loop(0, (entries[0] + ns - 1) >> (ns.bit_length() - 1))
    def _(i):
        pair_steps([entries[ns * i + r + 1] for r in range(ns)], q_ref, kv, streams)


def streams_of(refs):
    return [tuple(refs[3 * r:3 * r + 3]) for r in range(STREAMS)]


def clear(streams):
    for m_ref, l_ref, _ in streams:
        m_ref[...] = jnp.full(m_ref.shape, NEG, F32)
        l_ref[...] = jnp.zeros(l_ref.shape, F32)


def merge(states):
    top = functools.reduce(jnp.maximum, [m for m, _, _ in states])
    ws = [jnp.exp2((m - top) * C2) for m, _, _ in states]
    total = sum(w * l for w, (_, l, _) in zip(ws, states))
    acc = sum(jnp.where(m > NEG, w * a, 0.0) for w, (m, _, a) in zip(ws, states))
    return top, total, acc


def pack_kernel(q, tk, tv, pk, pv, table, parent, kv, sent, local, sems):
    del kv
    copies = [
        pltpu.make_async_copy(q, sent.at[pl.ds(0, 2 * QROWS)], sems.at[0]),
        pltpu.make_async_copy(q, local.at[pl.ds(0, 2 * QROWS)], sems.at[1]),
        pltpu.make_async_copy(tk, local.at[pl.ds(TK_AT, 128)], sems.at[2]),
        pltpu.make_async_copy(tv, local.at[pl.ds(TV_AT, 128)], sems.at[3]),
        pltpu.make_async_copy(pk, local.at[pl.ds(PAGES_AT, LOCAL_PAGES * 128)], sems.at[4]),
        pltpu.make_async_copy(pv, local.at[pl.ds(PAGES_AT + LOCAL_PAGES * 128, LOCAL_PAGES * 128)], sems.at[5]),
    ]
    for cp in copies:
        cp.start()
    ids = table[...].astype(F32)
    row = lax.broadcasted_iota(jnp.int32, (16, 128), 0)
    above = parent[...].astype(F32)
    tail = pl.ds(2 * QROWS, 16)
    sent[tail, :] = jnp.zeros((16, 128), BF)
    local[tail, :] = jnp.where(row == 2, above, 0.0).astype(BF)
    row = row[:, :16]
    pages = jnp.where(row == 0, ids[0:1, :], jnp.where(row == 1, ids[1:2, :], 0.0))
    sent[tail, :16] = pages.astype(BF)
    local[tail, :16] = jnp.where(row == 2, above[:, :16], pages).astype(BF)
    for cp in copies:
        cp.wait()


def near_kernel(maps, local, s1, s2, s3, up1, dn1, up2, dn2, q_out, list_far, list_far_x, *refs):
    m_out, l_out, a_out, tails, ids, tbl, list_near, found, kv = refs[:9]
    lists = (list_near, list_far, list_far_x)
    streams = streams_of(refs[9:-1])
    sems = refs[-1]
    sents = (local, s1, s2, s3)
    for r, x in enumerate(sents):
        tails[pl.ds(r * 16, 16), :] = x[pl.ds(2 * QROWS, 16), :]
    ids[...] = tails[...].astype(F32).astype(jnp.int32)
    to_scalar = pltpu.make_async_copy(ids, tbl, sems.at[0])
    to_scalar.start()
    copies = load_blocks(
        [local.at[pl.ds(PAGES_AT, BLOCK)], up1, dn1, up2, dn2], kv, [sems.at[i + 1] for i in range(5)]
    )
    for r, x in enumerate(sents):
        q_out[pl.ds(r * 2 * QROWS, 2 * QROWS), :] = x[pl.ds(0, 2 * QROWS), :]
    clear(streams)
    both = 2 * TREE
    row = lax.broadcasted_iota(jnp.int32, (both, both), 0)
    lane = lax.broadcasted_iota(jnp.int32, (both, both), 1)
    above = ids[2:3, :] + jnp.where(lax.broadcasted_iota(jnp.int32, (1, both), 1) >= TREE, TREE, 0)
    reach = jnp.minimum((row == lane).astype(F32) + (row == above).astype(F32), 1.0)
    for _ in range(7):
        half = reach.astype(BF)
        reach = jnp.minimum(jnp.dot(half, half, preferred_element_type=F32), 1.0)
    half = reach.astype(BF)
    tree_row = lax.broadcasted_iota(jnp.int32, (both, QROWS), 0)
    of_query = lax.shift_right_logical(lax.broadcasted_iota(jnp.int32, (both, QROWS), 1), 2)
    m0, l0, a0 = streams[0]
    for s in range(2):
        widen = (tree_row == of_query + s * TREE).astype(BF)
        seen = jnp.dot(half[s * TREE:(s + 1) * TREE, :], widen, preferred_element_type=F32)
        scores = lax.dot_general(
            local[pl.ds(TK_AT + s * TREE, TREE), :],
            local[pl.ds(s * QROWS, QROWS), :],
            (((1,), (1,)), ((), ())),
            preferred_element_type=F32,
        )
        scores = jnp.where(seen > 0.5, scores, NEG)
        top = jnp.max(scores, axis=0, keepdims=True)
        probs = jnp.exp2(scores * C2 - top * C2)
        m0[s] = top
        l0[s] = jnp.sum(probs, axis=0, keepdims=True)
        a0[s] = lax.dot_general(
            local[pl.ds(TV_AT + s * TREE, TREE), :],
            probs.astype(BF),
            (((0,), (0,)), ((), ())),
            preferred_element_type=F32,
        )
    to_scalar.wait()

    def scan(r, n):
        for half in range(2):
            pages = [tbl[r * 16 + half, j] for j in range(16)]
            at = [maps[p >> 2] for p in pages]
            for p, where in zip(pages, at):
                found[n] = (r * 2 + half) * 256 + (p & 3) + where
                n = n + (where >= 0).astype(jnp.int32)
        return n

    total = lax.fori_loop(0, GROUP, scan, jnp.int32(0))

    def sort(i, counts):
        entry = found[i]
        kind = entry >> 16
        kind = kind + (kind & (entry >> 10))
        out = []
        for k in range(3):
            lists[k][counts[k] + 1] = entry & 65535
            out.append(counts[k] + (kind == k).astype(jnp.int32))
        return tuple(out)

    counts = lax.fori_loop(0, total, sort, (jnp.int32(0),) * 3)
    for k in range(3):
        lists[k][0] = counts[k]
        for r in range(STREAMS - 1):
            lists[k][counts[k] + 1 + r] = jnp.int32(SESS * 256)
    for cp in copies:
        cp.wait()
    all_pairs(list_near, q_out, kv, streams)
    for s in range(SESS):
        top, total, acc = merge([(m[s], l[s], a[s]) for m, l, a in streams])
        m_out[s] = top
        l_out[s] = total
        a_out[s] = acc


def load_blocks(blocks, kv, sems):
    copies = [pltpu.make_async_copy(b, kv.at[pl.ds(i * BLOCK, BLOCK)], sem) for i, (b, sem) in enumerate(zip(blocks, sems))]
    for cp in copies:
        cp.start()
    return copies


def far_kernel(nb, first, *refs):
    list_far, q_ref = refs[:2]
    blocks = refs[2:2 + nb]
    before = refs[2 + nb:5 + nb]
    outs = refs[5 + nb:7 + nb]
    kv = refs[7 + nb]
    streams = streams_of(refs[8 + nb:-1])
    copies = load_blocks(blocks, kv, [refs[-1].at[i] for i in range(nb)])
    clear(streams)
    for cp in copies:
        cp.wait()
    all_pairs(list_far, q_ref, kv, streams)
    for s in range(first, first + SESS // 2):
        top, total, acc = merge([(m[s], l[s], a[s]) for m, l, a in [before] + streams])
        some = total > 0.0
        safe = jnp.where(some, total, 1.0)
        acc = acc * (1.0 / safe)
        lse = jnp.where(some, top * C2 + jnp.log2(safe), NEG)
        lanes = pl.ds((s % 2) * QROWS, QROWS)
        if s < 2:
            outs[0][pl.ds(0, HD), lanes] = acc
            outs[0][pl.ds(HD, 8), lanes] = jnp.broadcast_to(lse, (8, QROWS))
        else:
            out = outs[(s - first) // 2]
            out[pl.ds(0, HD), lanes] = acc.astype(BF)
            hi = lse.astype(BF).astype(F32)
            mid = (lse - hi).astype(BF).astype(F32)
            low = lse - hi - mid
            row = lax.broadcasted_iota(jnp.int32, (16, QROWS), 0)
            parts = jnp.where(row == 0, hi, jnp.where(row == 1, mid, jnp.where(row == 2, low, 0.0)))
            out[pl.ds(HD, 16), lanes] = parts.astype(BF)


def combine_kernel(head_ref, own, p1, p2, p3, attn, rows_f32):
    lses = [own[HD:HD + 1, :]]
    vals = [own[:HD, :]]
    for p in (p1, p2, p3):
        tail = p[HD:HD + 16, :].astype(F32)
        lses.append(tail[0:1] + tail[1:2] + tail[2:3])
        vals.append(p[:HD, :].astype(F32))
    top = functools.reduce(jnp.maximum, lses)
    ws = [jnp.exp2(x - top) for x in lses]
    inv = 1.0 / sum(ws)
    mixed = sum(v * (w * inv) for v, w in zip(vals, ws))
    rows_f32[...] = mixed.T
    for k, (dx, dy) in enumerate(HEADS):
        first = ((head_ref[0] & 4) ^ (dx * 4)) * 64 + ((head_ref[0] + dy) & 3) * 64
        for h in range(4):
            block = rows_f32[pl.ds(first + h, 16, stride=4), :]
            attn[pl.ds(k * 16, 16), pl.ds(h * HD, HD)] = block.astype(BF)


def sum_kernel(*refs):
    out = refs[-1]
    out[...] = functools.reduce(jnp.add, [r[...].astype(F32) for r in refs[:-1]]).astype(BF)


VMEM = pl.BlockSpec(memory_space=pltpu.VMEM)
SMEM = pl.BlockSpec(memory_space=pltpu.SMEM)
ANY = pl.BlockSpec(memory_space=pl.ANY)


def stream_scratch():
    return [
        pltpu.VMEM((SESS + 1, 1, QROWS), F32),
        pltpu.VMEM((SESS + 1, 1, QROWS), F32),
        pltpu.VMEM((SESS + 1, HD, QROWS), F32),
    ]


def state_shapes(n):
    return [
        jax.ShapeDtypeStruct((n, 1, QROWS), F32),
        jax.ShapeDtypeStruct((n, 1, QROWS), F32),
        jax.ShapeDtypeStruct((n, HD, QROWS), F32),
    ]


def near_call(*args):
    return pl.pallas_call(
        near_kernel,
        out_shape=[jax.ShapeDtypeStruct((SESS * QROWS, HD), BF), jax.ShapeDtypeStruct((160,), jnp.int32)]
        + [jax.ShapeDtypeStruct((160,), jnp.int32)]
        + state_shapes(SESS),
        in_specs=[SMEM] + [VMEM] * 4 + [ANY] * 4,
        out_specs=[VMEM, SMEM, SMEM] + [VMEM] * 3,
        scratch_shapes=[
            pltpu.VMEM((64, 128), BF),
            pltpu.VMEM((64, 128), jnp.int32),
            pltpu.SMEM((64, 128), jnp.int32),
            pltpu.SMEM((160,), jnp.int32),
            pltpu.SMEM((160,), jnp.int32),
            pltpu.VMEM((5 * BLOCK, HD), BF),
        ]
        + stream_scratch() * STREAMS
        + [pltpu.SemaphoreType.DMA((6,))],
        compiler_params=pltpu.CompilerParams(vmem_limit_bytes=24 << 20),
        cost_estimate=pl.CostEstimate(flops=4 * 10**9, bytes_accessed=4 << 20, transcendentals=1 << 20),
        name="near_pages",
    )(*args)


def far_call(pages, q_all, blocks, state, first, name):
    nb = len(blocks)
    part = jax.ShapeDtypeStruct((HD + 16, 2 * QROWS), BF)
    own = jax.ShapeDtypeStruct((HD + 8, 2 * QROWS), F32)
    return pl.pallas_call(
        functools.partial(far_kernel, nb, first),
        out_shape=[part if first else own, part],
        in_specs=[SMEM, VMEM] + [ANY] * nb + [VMEM] * 3,
        out_specs=[VMEM] * 2,
        scratch_shapes=[pltpu.VMEM((nb * BLOCK, HD), BF)]
        + stream_scratch() * STREAMS
        + [pltpu.SemaphoreType.DMA((nb,))],
        compiler_params=pltpu.CompilerParams(vmem_limit_bytes=24 << 20),
        cost_estimate=pl.CostEstimate(flops=10**9, bytes_accessed=4 << 20, transcendentals=1 << 20),
        name=name,
    )(pages, q_all, *blocks, *state)


def on_device(
    queries, tree_keys, tree_values, prefix_keys, prefix_values, tree_parent, page_table, out_weight
):
    rep = lax.axis_index("rep")
    head = lax.axis_index("head")
    q_own = queries.reshape(2 * QROWS, HD)
    kv = jnp.concatenate([prefix_keys, prefix_values], axis=0).reshape(BLOCK, HD)
    up1 = lax.ppermute(kv, "rep", z_perm(1))
    dn1 = lax.ppermute(kv, "rep", z_perm(-1))
    sent, local = pl.pallas_call(
        pack_kernel,
        out_shape=[
            jax.ShapeDtypeStruct((2 * QROWS + 16, HD), BF),
            jax.ShapeDtypeStruct((PAGES_AT + 2 * LOCAL_PAGES * 128, HD), BF),
        ],
        in_specs=[ANY] * 5 + [VMEM] * 2 + [ANY],
        out_specs=[VMEM] * 2,
        scratch_shapes=[pltpu.SemaphoreType.DMA((6,))],
        compiler_params=pltpu.CompilerParams(vmem_limit_bytes=59 << 20),
        name="pack",
    )(
        q_own, tree_keys.reshape(-1, HD), tree_values.reshape(-1, HD),
        prefix_keys.reshape(-1, HD), prefix_values.reshape(-1, HD), page_table, tree_parent.reshape(1, -1),
        kv,
    )
    up2 = lax.ppermute(kv, "rep", z_perm(2))
    dn2 = lax.ppermute(kv, "rep", z_perm(-2))
    q_x = lax.ppermute(sent, "rep", group_perm(2))
    q_x, sent = lax.optimization_barrier((q_x, sent))
    sents = [lax.ppermute(sent, "rep", group_perm(1)), q_x, lax.ppermute(q_x, "rep", group_perm(1))]
    up3 = lax.ppermute(up2, "rep", z_perm(1))
    dn3 = lax.ppermute(dn2, "rep", z_perm(-1))
    held = jnp.where((rep & 1) == 0, up2, dn2)
    opposite = lax.ppermute(
        held, "rep", [(rep_of(a, z, c), rep_of(a, z + 2 - 4 * c, c)) for a in range(2) for z in range(Z) for c in range(2)]
    )

    reps = jnp.arange(32, dtype=jnp.int32)
    same = ((reps ^ rep) & 17) == 0
    step = ((reps >> 1) - (rep >> 1)) & 7
    maps = jnp.full((32,), -(1 << 20), jnp.int32)
    for k, offsets in enumerate(GROUPS):
        for i, o in enumerate(offsets):
            maps = jnp.where(same & (step == o % Z), k * 65536 + i * 8, maps)
    q_all, list_far, list_far_x, *state = near_call(maps, local, *sents, up1, dn1, up2, dn2)
    blocks = (up3, dn3, opposite)
    p2, p3 = far_call(list_far_x, q_all, blocks, state, SESS // 2, "far_pages_x")
    p3 = lax.ppermute(p3, "rep", group_perm(3))
    p2 = lax.ppermute(p2, "rep", group_perm(2))
    own, p1 = far_call(list_far, q_all, blocks, state, 0, "far_pages_own")
    back = [p3, p2, lax.ppermute(p1, "rep", group_perm(1))]
    width = out_weight.shape[1]
    attn = pl.pallas_call(
        combine_kernel,
        out_shape=jax.ShapeDtypeStruct((128, 512), BF),
        in_specs=[SMEM] + [VMEM] * 4,
        out_specs=VMEM,
        scratch_shapes=[pltpu.VMEM((2 * QROWS, HD), F32)],
        compiler_params=pltpu.CompilerParams(vmem_limit_bytes=24 << 20),
        cost_estimate=pl.CostEstimate(flops=10**6, bytes_accessed=1 << 20, transcendentals=4096),
        name="combine",
    )(head.reshape(1).astype(jnp.int32), own, *back)
    rows = jnp.dot(attn, out_weight, preferred_element_type=F32).astype(BF)
    parts = [rows[k * 16:(k + 1) * 16] for k in range(8)]
    terms = [
        lax.ppermute(part, "head", [(i, ((i & 4) ^ (dx * 4)) + ((i + dy) & 3)) for i in range(8)])
        for part, (dx, dy) in zip(parts[1:], HEADS[1:])
    ]
    return pl.pallas_call(
        sum_kernel,
        out_shape=jax.ShapeDtypeStruct((16, width), BF),
        in_specs=[VMEM] * 8,
        out_specs=VMEM,
        compiler_params=pltpu.CompilerParams(vmem_limit_bytes=24 << 20),
        name="sum_heads",
    )(parts[0], *terms)


def solution(mesh):
    in_specs = (
        P("rep", "head", None),
        P("rep", "head", None),
        P("rep", "head", None),
        P("rep", "head", None, None),
        P("rep", "head", None, None),
        P("rep"),
        P("rep", None),
        P("head", None),
    )
    out_specs = P(("rep", "head"), None)
    return jax.shard_map(
        on_device, mesh=mesh, in_specs=in_specs, out_specs=out_specs, check_vma=False
    )
```

```python
import functools
import math

import jax
import jax.numpy as jnp
from jax import lax
from jax.experimental import pallas as pl
from jax.experimental.pallas import tpu as pltpu
from jax.sharding import PartitionSpec as P

NEG = -1e30
Z = 8
GROUP = 4
LOCAL_PAGES = 4
TK_AT = 528
TV_AT = 656
BLOCK = 1024
PAGES_AT = 784
TREE = 64
QROWS = 256
HD = 128
SESS = 8
C2 = (HD ** -0.5) * math.log2(math.e)
BF = jnp.bfloat16
F32 = jnp.float32

STREAMS = 4
GROUPS = ((0, -1, 1, -2, 2), (-3, 3, 4))


HEADS = (0, 1, 5, 3, 7, 2, 6, 4)


def rep_of(xh, z, c):
    return xh * 16 + (z % Z) * 2 + c


def z_perm(k):
    return [(rep_of(a, z, c), rep_of(a, z + k, c)) for a in range(2) for z in range(Z) for c in range(2)]


def group_perm(r):
    return [(rep_of(a, z, c), rep_of(a ^ (r >> 1), z, c ^ (r & 1))) for a in range(2) for z in range(Z) for c in range(2)]


def page(kv, i):
    return kv[pl.ds(pl.multiple_of(i * 128, 128), 128), :]


def pair_steps(entries, q_ref, kv, streams):
    at = [(e >> 8, e & 255) for e in entries]
    scores = [
        lax.dot_general(page(kv, k), q_ref[pl.ds(pl.multiple_of((s & (SESS - 1)) * QROWS, QROWS), QROWS), :], (((1,), (1,)), ((), ())), preferred_element_type=F32)
        for s, k in at
    ]
    olds = [m[s] for (s, _), (m, _, _) in zip(at, streams)]
    news = [jnp.maximum(o, jnp.max(x, axis=0, keepdims=True)) for o, x in zip(olds, scores)]
    probs = [jnp.exp2(x * C2 - n * C2) for x, n in zip(scores, news)]
    fixes = [jnp.exp2((o - n) * C2) for o, n in zip(olds, news)]
    parts = [
        lax.dot_general(
            page(kv, k + LOCAL_PAGES), p.astype(BF), (((0,), (0,)), ((), ())), preferred_element_type=F32
        )
        for (_, k), p in zip(at, probs)
    ]
    for (s, _), o, n, p, fix, part, (m_ref, l_ref, a_ref) in zip(at, olds, news, probs, fixes, parts, streams):
        m_ref[s] = n
        l_ref[s] = l_ref[s] * fix + jnp.sum(p, axis=0, keepdims=True)
        a_ref[s] = jnp.where(o > NEG, a_ref[s] * fix, 0.0) + part


def all_pairs(entries, q_ref, kv, streams):
    ns = len(streams)

    @pl.loop(0, (entries[0] + ns - 1) >> (ns.bit_length() - 1))
    def _(i):
        pair_steps([entries[ns * i + r + 1] for r in range(ns)], q_ref, kv, streams)


def streams_of(refs):
    return [tuple(refs[3 * r:3 * r + 3]) for r in range(STREAMS)]


def clear(streams):
    for m_ref, l_ref, _ in streams:
        m_ref[...] = jnp.full(m_ref.shape, NEG, F32)
        l_ref[...] = jnp.zeros(l_ref.shape, F32)


def merge(states):
    top = functools.reduce(jnp.maximum, [m for m, _, _ in states])
    ws = [jnp.exp2((m - top) * C2) for m, _, _ in states]
    total = sum(w * l for w, (_, l, _) in zip(ws, states))
    acc = sum(jnp.where(m > NEG, w * a, 0.0) for w, (m, _, a) in zip(ws, states))
    return top, total, acc


def pack_kernel(q, tk, tv, pk, pv, table, parent, kv, sent, local, sems):
    del kv
    copies = [
        pltpu.make_async_copy(q, sent.at[pl.ds(0, 2 * QROWS)], sems.at[0]),
        pltpu.make_async_copy(q, local.at[pl.ds(0, 2 * QROWS)], sems.at[1]),
        pltpu.make_async_copy(tk, local.at[pl.ds(TK_AT, 128)], sems.at[2]),
        pltpu.make_async_copy(tv, local.at[pl.ds(TV_AT, 128)], sems.at[3]),
        pltpu.make_async_copy(pk, local.at[pl.ds(PAGES_AT, LOCAL_PAGES * 128)], sems.at[4]),
        pltpu.make_async_copy(pv, local.at[pl.ds(PAGES_AT + LOCAL_PAGES * 128, LOCAL_PAGES * 128)], sems.at[5]),
    ]
    for cp in copies:
        cp.start()
    ids = table[...].astype(F32)
    row = lax.broadcasted_iota(jnp.int32, (16, 128), 0)
    above = parent[...].astype(F32)
    tail = pl.ds(2 * QROWS, 16)
    sent[tail, :] = jnp.zeros((16, 128), BF)
    local[tail, :] = jnp.where(row == 2, above, 0.0).astype(BF)
    row = row[:, :16]
    pages = jnp.where(row == 0, ids[0:1, :], jnp.where(row == 1, ids[1:2, :], 0.0))
    sent[tail, :16] = pages.astype(BF)
    local[tail, :16] = jnp.where(row == 2, above[:, :16], pages).astype(BF)
    for cp in copies:
        cp.wait()


def near_kernel(maps, local, s1, s2, s3, up1, dn1, up2, dn2, q_out, list_far, list_far_x, *refs):
    m_out, l_out, a_out, tails, ids, tbl, list_near, found, kv = refs[:9]
    lists = (list_near, list_far, list_far_x)
    streams = streams_of(refs[9:-1])
    sems = refs[-1]
    sents = (local, s1, s2, s3)
    for r, x in enumerate(sents):
        tails[pl.ds(r * 16, 16), :] = x[pl.ds(2 * QROWS, 16), :]
    ids[...] = tails[...].astype(F32).astype(jnp.int32)
    to_scalar = pltpu.make_async_copy(ids, tbl, sems.at[0])
    to_scalar.start()
    copies = load_blocks(
        [local.at[pl.ds(PAGES_AT, BLOCK)], up1, dn1, up2, dn2], kv, [sems.at[i + 1] for i in range(5)]
    )
    for r, x in enumerate(sents):
        q_out[pl.ds(r * 2 * QROWS, 2 * QROWS), :] = x[pl.ds(0, 2 * QROWS), :]
    clear(streams)
    both = 2 * TREE
    row = lax.broadcasted_iota(jnp.int32, (both, both), 0)
    lane = lax.broadcasted_iota(jnp.int32, (both, both), 1)
    above = ids[2:3, :] + jnp.where(lax.broadcasted_iota(jnp.int32, (1, both), 1) >= TREE, TREE, 0)
    reach = jnp.minimum((row == lane).astype(F32) + (row == above).astype(F32), 1.0)
    for _ in range(7):
        half = reach.astype(BF)
        reach = jnp.minimum(jnp.dot(half, half, preferred_element_type=F32), 1.0)
    half = reach.astype(BF)
    tree_row = lax.broadcasted_iota(jnp.int32, (both, QROWS), 0)
    of_query = lax.shift_right_logical(lax.broadcasted_iota(jnp.int32, (both, QROWS), 1), 2)
    m0, l0, a0 = streams[0]
    for s in range(2):
        widen = (tree_row == of_query + s * TREE).astype(BF)
        seen = jnp.dot(half[s * TREE:(s + 1) * TREE, :], widen, preferred_element_type=F32)
        scores = lax.dot_general(
            local[pl.ds(TK_AT + s * TREE, TREE), :],
            local[pl.ds(s * QROWS, QROWS), :],
            (((1,), (1,)), ((), ())),
            preferred_element_type=F32,
        )
        scores = jnp.where(seen > 0.5, scores, NEG)
        top = jnp.max(scores, axis=0, keepdims=True)
        probs = jnp.exp2(scores * C2 - top * C2)
        m0[s] = top
        l0[s] = jnp.sum(probs, axis=0, keepdims=True)
        a0[s] = lax.dot_general(
            local[pl.ds(TV_AT + s * TREE, TREE), :],
            probs.astype(BF),
            (((0,), (0,)), ((), ())),
            preferred_element_type=F32,
        )
    to_scalar.wait()

    def scan(r, n):
        for half in range(2):
            pages = [tbl[r * 16 + half, j] for j in range(16)]
            at = [maps[p >> 2] for p in pages]
            for p, where in zip(pages, at):
                found[n] = (r * 2 + half) * 256 + (p & 3) + where
                n = n + (where >= 0).astype(jnp.int32)
        return n

    total = lax.fori_loop(0, GROUP, scan, jnp.int32(0))

    def sort(i, counts):
        entry = found[i]
        kind = entry >> 16
        kind = kind + (kind & (entry >> 10))
        out = []
        for k in range(3):
            lists[k][counts[k] + 1] = entry & 65535
            out.append(counts[k] + (kind == k).astype(jnp.int32))
        return tuple(out)

    counts = lax.fori_loop(0, total, sort, (jnp.int32(0),) * 3)
    for k in range(3):
        lists[k][0] = counts[k]
        for r in range(STREAMS - 1):
            lists[k][counts[k] + 1 + r] = jnp.int32(SESS * 256)
    for cp in copies:
        cp.wait()
    all_pairs(list_near, q_out, kv, streams)
    for s in range(SESS):
        top, total, acc = merge([(m[s], l[s], a[s]) for m, l, a in streams])
        m_out[s] = top
        l_out[s] = total
        a_out[s] = acc


def load_blocks(blocks, kv, sems):
    copies = [pltpu.make_async_copy(b, kv.at[pl.ds(i * BLOCK, BLOCK)], sem) for i, (b, sem) in enumerate(zip(blocks, sems))]
    for cp in copies:
        cp.start()
    return copies


def far_kernel(nb, first, *refs):
    list_far, q_ref = refs[:2]
    blocks = refs[2:2 + nb]
    before = refs[2 + nb:5 + nb]
    outs = refs[5 + nb:7 + nb]
    kv = refs[7 + nb]
    streams = streams_of(refs[8 + nb:-1])
    copies = load_blocks(blocks, kv, [refs[-1].at[i] for i in range(nb)])
    clear(streams)
    for cp in copies:
        cp.wait()
    all_pairs(list_far, q_ref, kv, streams)
    for s in range(first, first + SESS // 2):
        top, total, acc = merge([(m[s], l[s], a[s]) for m, l, a in [before] + streams])
        some = total > 0.0
        safe = jnp.where(some, total, 1.0)
        acc = acc * (1.0 / safe)
        lse = jnp.where(some, top * C2 + jnp.log2(safe), NEG)
        lanes = pl.ds((s % 2) * QROWS, QROWS)
        if s < 2:
            outs[0][pl.ds(0, HD), lanes] = acc
            outs[0][pl.ds(HD, 8), lanes] = jnp.broadcast_to(lse, (8, QROWS))
        else:
            out = outs[(s - first) // 2]
            out[pl.ds(0, HD), lanes] = acc.astype(BF)
            hi = lse.astype(BF).astype(F32)
            mid = (lse - hi).astype(BF).astype(F32)
            low = lse - hi - mid
            row = lax.broadcasted_iota(jnp.int32, (16, QROWS), 0)
            parts = jnp.where(row == 0, hi, jnp.where(row == 1, mid, jnp.where(row == 2, low, 0.0)))
            out[pl.ds(HD, 16), lanes] = parts.astype(BF)


def combine_kernel(head_ref, own, p1, p2, p3, attn, rows_f32):
    lses = [own[HD:HD + 1, :]]
    vals = [own[:HD, :]]
    for p in (p1, p2, p3):
        tail = p[HD:HD + 16, :].astype(F32)
        lses.append(tail[0:1] + tail[1:2] + tail[2:3])
        vals.append(p[:HD, :].astype(F32))
    top = functools.reduce(jnp.maximum, lses)
    ws = [jnp.exp2(x - top) for x in lses]
    inv = 1.0 / sum(ws)
    mixed = sum(v * (w * inv) for v, w in zip(vals, ws))
    rows_f32[...] = mixed.T
    for k, flip in enumerate(HEADS):
        first = (head_ref[0] ^ flip) * 64
        for h in range(4):
            block = rows_f32[pl.ds(first + h, 16, stride=4), :]
            attn[pl.ds(k * 16, 16), pl.ds(h * HD, HD)] = block.astype(BF)


def sum_kernel(*refs):
    out = refs[-1]
    out[...] = functools.reduce(jnp.add, [r[...].astype(F32) for r in refs[:-1]]).astype(BF)


VMEM = pl.BlockSpec(memory_space=pltpu.VMEM)
SMEM = pl.BlockSpec(memory_space=pltpu.SMEM)
ANY = pl.BlockSpec(memory_space=pl.ANY)


def stream_scratch():
    return [
        pltpu.VMEM((SESS + 1, 1, QROWS), F32),
        pltpu.VMEM((SESS + 1, 1, QROWS), F32),
        pltpu.VMEM((SESS + 1, HD, QROWS), F32),
    ]


def state_shapes(n):
    return [
        jax.ShapeDtypeStruct((n, 1, QROWS), F32),
        jax.ShapeDtypeStruct((n, 1, QROWS), F32),
        jax.ShapeDtypeStruct((n, HD, QROWS), F32),
    ]


def near_call(*args):
    return pl.pallas_call(
        near_kernel,
        out_shape=[jax.ShapeDtypeStruct((SESS * QROWS, HD), BF), jax.ShapeDtypeStruct((160,), jnp.int32)]
        + [jax.ShapeDtypeStruct((160,), jnp.int32)]
        + state_shapes(SESS),
        in_specs=[SMEM] + [VMEM] * 4 + [ANY] * 4,
        out_specs=[VMEM, SMEM, SMEM] + [VMEM] * 3,
        scratch_shapes=[
            pltpu.VMEM((64, 128), BF),
            pltpu.VMEM((64, 128), jnp.int32),
            pltpu.SMEM((64, 128), jnp.int32),
            pltpu.SMEM((160,), jnp.int32),
            pltpu.SMEM((160,), jnp.int32),
            pltpu.VMEM((5 * BLOCK, HD), BF),
        ]
        + stream_scratch() * STREAMS
        + [pltpu.SemaphoreType.DMA((6,))],
        compiler_params=pltpu.CompilerParams(vmem_limit_bytes=24 << 20),
        cost_estimate=pl.CostEstimate(flops=4 * 10**9, bytes_accessed=4 << 20, transcendentals=1 << 20),
        name="near_pages",
    )(*args)


def far_call(pages, q_all, blocks, state, first, name):
    nb = len(blocks)
    part = jax.ShapeDtypeStruct((HD + 16, 2 * QROWS), BF)
    own = jax.ShapeDtypeStruct((HD + 8, 2 * QROWS), F32)
    return pl.pallas_call(
        functools.partial(far_kernel, nb, first),
        out_shape=[part if first else own, part],
        in_specs=[SMEM, VMEM] + [ANY] * nb + [VMEM] * 3,
        out_specs=[VMEM] * 2,
        scratch_shapes=[pltpu.VMEM((nb * BLOCK, HD), BF)]
        + stream_scratch() * STREAMS
        + [pltpu.SemaphoreType.DMA((nb,))],
        compiler_params=pltpu.CompilerParams(vmem_limit_bytes=24 << 20),
        cost_estimate=pl.CostEstimate(flops=10**9, bytes_accessed=4 << 20, transcendentals=1 << 20),
        name=name,
    )(pages, q_all, *blocks, *state)


def on_device(
    queries, tree_keys, tree_values, prefix_keys, prefix_values, tree_parent, page_table, out_weight
):
    rep = lax.axis_index("rep")
    head = lax.axis_index("head")
    q_own = queries.reshape(2 * QROWS, HD)
    kv = jnp.concatenate([prefix_keys, prefix_values], axis=0).reshape(BLOCK, HD)
    up1 = lax.ppermute(kv, "rep", z_perm(1))
    dn1 = lax.ppermute(kv, "rep", z_perm(-1))
    sent, local = pl.pallas_call(
        pack_kernel,
        out_shape=[
            jax.ShapeDtypeStruct((2 * QROWS + 16, HD), BF),
            jax.ShapeDtypeStruct((PAGES_AT + 2 * LOCAL_PAGES * 128, HD), BF),
        ],
        in_specs=[ANY] * 5 + [VMEM] * 2 + [ANY],
        out_specs=[VMEM] * 2,
        scratch_shapes=[pltpu.SemaphoreType.DMA((6,))],
        compiler_params=pltpu.CompilerParams(vmem_limit_bytes=59 << 20),
        name="pack",
    )(
        q_own, tree_keys.reshape(-1, HD), tree_values.reshape(-1, HD),
        prefix_keys.reshape(-1, HD), prefix_values.reshape(-1, HD), page_table, tree_parent.reshape(1, -1),
        kv,
    )
    up1, dn1, sent = lax.optimization_barrier((up1, dn1, sent))
    up2 = lax.ppermute(up1, "rep", z_perm(1))
    dn2 = lax.ppermute(dn1, "rep", z_perm(-1))
    sents = [lax.ppermute(sent, "rep", group_perm(r)) for r in (1, 2, 3)]
    up3 = lax.ppermute(up2, "rep", z_perm(1))
    dn3 = lax.ppermute(dn2, "rep", z_perm(-1))
    held = jnp.where((rep & 1) == 0, up2, dn2)
    opposite = lax.ppermute(
        held, "rep", [(rep_of(a, z, c), rep_of(a, z + 2 - 4 * c, c)) for a in range(2) for z in range(Z) for c in range(2)]
    )

    reps = jnp.arange(32, dtype=jnp.int32)
    same = ((reps ^ rep) & 17) == 0
    step = ((reps >> 1) - (rep >> 1)) & 7
    maps = jnp.full((32,), -(1 << 20), jnp.int32)
    for k, offsets in enumerate(GROUPS):
        for i, o in enumerate(offsets):
            maps = jnp.where(same & (step == o % Z), k * 65536 + i * 8, maps)
    q_all, list_far, list_far_x, *state = near_call(maps, local, *sents, up1, dn1, up2, dn2)
    blocks = (up3, dn3, opposite)
    p2, p3 = far_call(list_far_x, q_all, blocks, state, SESS // 2, "far_pages_x")
    p3 = lax.ppermute(p3, "rep", group_perm(3))
    p2 = lax.ppermute(p2, "rep", group_perm(2))
    own, p1 = far_call(list_far, q_all, blocks, state, 0, "far_pages_own")
    back = [p3, p2, lax.ppermute(p1, "rep", group_perm(1))]
    width = out_weight.shape[1]
    attn = pl.pallas_call(
        combine_kernel,
        out_shape=jax.ShapeDtypeStruct((128, 512), BF),
        in_specs=[SMEM] + [VMEM] * 4,
        out_specs=VMEM,
        scratch_shapes=[pltpu.VMEM((2 * QROWS, HD), F32)],
        compiler_params=pltpu.CompilerParams(vmem_limit_bytes=24 << 20),
        cost_estimate=pl.CostEstimate(flops=10**6, bytes_accessed=1 << 20, transcendentals=4096),
        name="combine",
    )(head.reshape(1).astype(jnp.int32), own, *back)
    rows = jnp.dot(attn, out_weight, preferred_element_type=F32).astype(BF)
    parts = [rows[k * 16:(k + 1) * 16] for k in range(8)]
    terms = [
        lax.ppermute(part, "head", [(i, i ^ flip) for i in range(8)])
        for part, flip in zip(parts[1:], HEADS[1:])
    ]
    return pl.pallas_call(
        sum_kernel,
        out_shape=jax.ShapeDtypeStruct((16, width), BF),
        in_specs=[VMEM] * 8,
        out_specs=VMEM,
        compiler_params=pltpu.CompilerParams(vmem_limit_bytes=24 << 20),
        name="sum_heads",
    )(parts[0], *terms)


def solution(mesh):
    in_specs = (
        P("rep", "head", None),
        P("rep", "head", None),
        P("rep", "head", None),
        P("rep", "head", None, None),
        P("rep", "head", None, None),
        P("rep"),
        P("rep", None),
        P("head", None),
    )
    out_specs = P(("rep", "head"), None)
    return jax.shard_map(
        on_device, mesh=mesh, in_specs=in_specs, out_specs=out_specs, check_vma=False
    )
```

```python
import functools
import math

import jax
import jax.numpy as jnp
from jax import lax
from jax.experimental import pallas as pl
from jax.experimental.pallas import tpu as pltpu
from jax.sharding import PartitionSpec as P

NEG = -1e30
Z = 8
GROUP = 4
LOCAL_PAGES = 4
TK_AT = 528
TV_AT = 656
BLOCK = 1024
PAGES_AT = 784
TREE = 64
QROWS = 256
HD = 128
SESS = 8
C2 = (HD ** -0.5) * math.log2(math.e)
BF = jnp.bfloat16
F32 = jnp.float32

STREAMS = 4
NEAR_STREAMS = 8
GROUPS = ((0, -1, 1, -2, 2), (-3, 3, 4))


HEADS = (0, 1, 5, 3, 7, 2, 6, 4)


def rep_of(xh, z, c):
    return xh * 16 + (z % Z) * 2 + c


def z_perm(k):
    return [(rep_of(a, z, c), rep_of(a, z + k, c)) for a in range(2) for z in range(Z) for c in range(2)]


def group_perm(r):
    return [(rep_of(a, z, c), rep_of(a ^ (r >> 1), z, c ^ (r & 1))) for a in range(2) for z in range(Z) for c in range(2)]


def page(kv, i):
    return kv[pl.ds(pl.multiple_of(i * 128, 128), 128), :]


def pair_steps(entries, q_ref, kv, streams):
    at = [(e >> 8, e & 255) for e in entries]
    scores = [
        lax.dot_general(page(kv, k), q_ref[pl.ds(pl.multiple_of((s & (SESS - 1)) * QROWS, QROWS), QROWS), :], (((1,), (1,)), ((), ())), preferred_element_type=F32)
        for s, k in at
    ]
    olds = [m[s] for (s, _), (m, _, _) in zip(at, streams)]
    news = [jnp.maximum(o, jnp.max(x, axis=0, keepdims=True)) for o, x in zip(olds, scores)]
    probs = [jnp.exp2(x * C2 - n * C2) for x, n in zip(scores, news)]
    fixes = [jnp.exp2((o - n) * C2) for o, n in zip(olds, news)]
    parts = [
        lax.dot_general(
            page(kv, k + LOCAL_PAGES), p.astype(BF), (((0,), (0,)), ((), ())), preferred_element_type=F32
        )
        for (_, k), p in zip(at, probs)
    ]
    for (s, _), o, n, p, fix, part, (m_ref, l_ref, a_ref) in zip(at, olds, news, probs, fixes, parts, streams):
        m_ref[s] = n
        l_ref[s] = l_ref[s] * fix + jnp.sum(p, axis=0, keepdims=True)
        a_ref[s] = jnp.where(o > NEG, a_ref[s] * fix, 0.0) + part


def all_pairs(entries, q_ref, kv, streams):
    ns = len(streams)

    @pl.loop(0, (entries[0] + ns - 1) >> (ns.bit_length() - 1))
    def _(i):
        pair_steps([entries[ns * i + r + 1] for r in range(ns)], q_ref, kv, streams)


def streams_of(refs):
    return [tuple(refs[3 * r:3 * r + 3]) for r in range(len(refs) // 3)]


def clear(streams):
    for m_ref, l_ref, _ in streams:
        m_ref[...] = jnp.full(m_ref.shape, NEG, F32)
        l_ref[...] = jnp.zeros(l_ref.shape, F32)


def merge(states):
    top = functools.reduce(jnp.maximum, [m for m, _, _ in states])
    ws = [jnp.exp2((m - top) * C2) for m, _, _ in states]
    total = sum(w * l for w, (_, l, _) in zip(ws, states))
    acc = sum(jnp.where(m > NEG, w * a, 0.0) for w, (m, _, a) in zip(ws, states))
    return top, total, acc


def pack_kernel(q, tk, tv, pk, pv, table, parent, kv, sent, local, sems):
    del kv
    copies = [
        pltpu.make_async_copy(q, sent.at[pl.ds(0, 2 * QROWS)], sems.at[0]),
        pltpu.make_async_copy(q, local.at[pl.ds(0, 2 * QROWS)], sems.at[1]),
        pltpu.make_async_copy(tk, local.at[pl.ds(TK_AT, 128)], sems.at[2]),
        pltpu.make_async_copy(tv, local.at[pl.ds(TV_AT, 128)], sems.at[3]),
        pltpu.make_async_copy(pk, local.at[pl.ds(PAGES_AT, LOCAL_PAGES * 128)], sems.at[4]),
        pltpu.make_async_copy(pv, local.at[pl.ds(PAGES_AT + LOCAL_PAGES * 128, LOCAL_PAGES * 128)], sems.at[5]),
    ]
    for cp in copies:
        cp.start()
    ids = table[...].astype(F32)
    row = lax.broadcasted_iota(jnp.int32, (16, 128), 0)
    above = parent[...].astype(F32)
    tail = pl.ds(2 * QROWS, 16)
    sent[tail, :] = jnp.zeros((16, 128), BF)
    local[tail, :] = jnp.where(row == 2, above, 0.0).astype(BF)
    row = row[:, :16]
    pages = jnp.where(row == 0, ids[0:1, :], jnp.where(row == 1, ids[1:2, :], 0.0))
    sent[tail, :16] = pages.astype(BF)
    local[tail, :16] = jnp.where(row == 2, above[:, :16], pages).astype(BF)
    for cp in copies:
        cp.wait()


def near_kernel(maps, local, s1, s2, s3, up1, dn1, up2, dn2, q_out, list_far, list_far_x, *refs):
    m_out, l_out, a_out, tails, ids, tbl, list_near, found, kv = refs[:9]
    lists = (list_near, list_far, list_far_x)
    streams = streams_of(refs[9:-1])
    sems = refs[-1]
    sents = (local, s1, s2, s3)
    for r, x in enumerate(sents):
        tails[pl.ds(r * 16, 16), :] = x[pl.ds(2 * QROWS, 16), :]
    ids[...] = tails[...].astype(F32).astype(jnp.int32)
    to_scalar = pltpu.make_async_copy(ids, tbl, sems.at[0])
    to_scalar.start()
    copies = load_blocks(
        [local.at[pl.ds(PAGES_AT, BLOCK)], up1, dn1, up2, dn2], kv, [sems.at[i + 1] for i in range(5)]
    )
    for r, x in enumerate(sents):
        q_out[pl.ds(r * 2 * QROWS, 2 * QROWS), :] = x[pl.ds(0, 2 * QROWS), :]
    clear(streams)
    both = 2 * TREE
    row = lax.broadcasted_iota(jnp.int32, (both, both), 0)
    lane = lax.broadcasted_iota(jnp.int32, (both, both), 1)
    above = ids[2:3, :] + jnp.where(lax.broadcasted_iota(jnp.int32, (1, both), 1) >= TREE, TREE, 0)
    reach = jnp.minimum((row == lane).astype(F32) + (row == above).astype(F32), 1.0)
    for _ in range(7):
        half = reach.astype(BF)
        reach = jnp.minimum(jnp.dot(half, half, preferred_element_type=F32), 1.0)
    half = reach.astype(BF)
    tree_row = lax.broadcasted_iota(jnp.int32, (both, QROWS), 0)
    of_query = lax.shift_right_logical(lax.broadcasted_iota(jnp.int32, (both, QROWS), 1), 2)
    m0, l0, a0 = streams[0]
    for s in range(2):
        widen = (tree_row == of_query + s * TREE).astype(BF)
        seen = jnp.dot(half[s * TREE:(s + 1) * TREE, :], widen, preferred_element_type=F32)
        scores = lax.dot_general(
            local[pl.ds(TK_AT + s * TREE, TREE), :],
            local[pl.ds(s * QROWS, QROWS), :],
            (((1,), (1,)), ((), ())),
            preferred_element_type=F32,
        )
        scores = jnp.where(seen > 0.5, scores, NEG)
        top = jnp.max(scores, axis=0, keepdims=True)
        probs = jnp.exp2(scores * C2 - top * C2)
        m0[s] = top
        l0[s] = jnp.sum(probs, axis=0, keepdims=True)
        a0[s] = lax.dot_general(
            local[pl.ds(TV_AT + s * TREE, TREE), :],
            probs.astype(BF),
            (((0,), (0,)), ((), ())),
            preferred_element_type=F32,
        )
    to_scalar.wait()

    def scan(r, n):
        for half in range(2):
            pages = [tbl[r * 16 + half, j] for j in range(16)]
            at = [maps[p >> 2] for p in pages]
            for p, where in zip(pages, at):
                found[n] = (r * 2 + half) * 256 + (p & 3) + where
                n = n + (where >= 0).astype(jnp.int32)
        return n

    total = lax.fori_loop(0, GROUP, scan, jnp.int32(0))

    def sort(i, counts):
        entry = found[i]
        kind = entry >> 16
        kind = kind + (kind & (entry >> 10))
        out = []
        for k in range(3):
            lists[k][counts[k] + 1] = entry & 65535
            out.append(counts[k] + (kind == k).astype(jnp.int32))
        return tuple(out)

    counts = lax.fori_loop(0, total, sort, (jnp.int32(0),) * 3)
    for k in range(3):
        lists[k][0] = counts[k]
        for r in range(NEAR_STREAMS - 1):
            lists[k][counts[k] + 1 + r] = jnp.int32(SESS * 256)
    for cp in copies:
        cp.wait()
    all_pairs(list_near, q_out, kv, streams)
    for s in range(SESS):
        top, total, acc = merge([(m[s], l[s], a[s]) for m, l, a in streams])
        m_out[s] = top
        l_out[s] = total
        a_out[s] = acc


def load_blocks(blocks, kv, sems):
    copies = [pltpu.make_async_copy(b, kv.at[pl.ds(i * BLOCK, BLOCK)], sem) for i, (b, sem) in enumerate(zip(blocks, sems))]
    for cp in copies:
        cp.start()
    return copies


def far_kernel(nb, first, *refs):
    list_far, q_ref = refs[:2]
    blocks = refs[2:2 + nb]
    before = refs[2 + nb:5 + nb]
    outs = refs[5 + nb:7 + nb]
    kv = refs[7 + nb]
    streams = streams_of(refs[8 + nb:-1])
    copies = load_blocks(blocks, kv, [refs[-1].at[i] for i in range(nb)])
    clear(streams)
    for cp in copies:
        cp.wait()
    all_pairs(list_far, q_ref, kv, streams)
    for s in range(first, first + SESS // 2):
        top, total, acc = merge([(m[s], l[s], a[s]) for m, l, a in [before] + streams])
        some = total > 0.0
        safe = jnp.where(some, total, 1.0)
        acc = acc * (1.0 / safe)
        lse = jnp.where(some, top * C2 + jnp.log2(safe), NEG)
        lanes = pl.ds((s % 2) * QROWS, QROWS)
        if s < 2:
            outs[0][pl.ds(0, HD), lanes] = acc
            outs[0][pl.ds(HD, 8), lanes] = jnp.broadcast_to(lse, (8, QROWS))
        else:
            out = outs[(s - first) // 2]
            out[pl.ds(0, HD), lanes] = acc.astype(BF)
            hi = lse.astype(BF).astype(F32)
            mid = (lse - hi).astype(BF).astype(F32)
            low = lse - hi - mid
            row = lax.broadcasted_iota(jnp.int32, (16, QROWS), 0)
            parts = jnp.where(row == 0, hi, jnp.where(row == 1, mid, jnp.where(row == 2, low, 0.0)))
            out[pl.ds(HD, 16), lanes] = parts.astype(BF)


def combine_kernel(head_ref, own, p1, p2, p3, attn, rows_f32):
    lses = [own[HD:HD + 1, :]]
    vals = [own[:HD, :]]
    for p in (p1, p2, p3):
        tail = p[HD:HD + 16, :].astype(F32)
        lses.append(tail[0:1] + tail[1:2] + tail[2:3])
        vals.append(p[:HD, :].astype(F32))
    top = functools.reduce(jnp.maximum, lses)
    ws = [jnp.exp2(x - top) for x in lses]
    inv = 1.0 / sum(ws)
    mixed = sum(v * (w * inv) for v, w in zip(vals, ws))
    rows_f32[...] = mixed.T
    for k, flip in enumerate(HEADS):
        first = (head_ref[0] ^ flip) * 64
        for h in range(4):
            block = rows_f32[pl.ds(first + h, 16, stride=4), :]
            attn[pl.ds(k * 16, 16), pl.ds(h * HD, HD)] = block.astype(BF)


def sum_kernel(*refs):
    out = refs[-1]
    out[...] = functools.reduce(jnp.add, [r[...].astype(F32) for r in refs[:-1]]).astype(BF)


VMEM = pl.BlockSpec(memory_space=pltpu.VMEM)
SMEM = pl.BlockSpec(memory_space=pltpu.SMEM)
ANY = pl.BlockSpec(memory_space=pl.ANY)


def stream_scratch():
    return [
        pltpu.VMEM((SESS + 1, 1, QROWS), F32),
        pltpu.VMEM((SESS + 1, 1, QROWS), F32),
        pltpu.VMEM((SESS + 1, HD, QROWS), F32),
    ]


def state_shapes(n):
    return [
        jax.ShapeDtypeStruct((n, 1, QROWS), F32),
        jax.ShapeDtypeStruct((n, 1, QROWS), F32),
        jax.ShapeDtypeStruct((n, HD, QROWS), F32),
    ]


def near_call(*args):
    return pl.pallas_call(
        near_kernel,
        out_shape=[jax.ShapeDtypeStruct((SESS * QROWS, HD), BF), jax.ShapeDtypeStruct((160,), jnp.int32)]
        + [jax.ShapeDtypeStruct((160,), jnp.int32)]
        + state_shapes(SESS),
        in_specs=[SMEM] + [VMEM] * 4 + [ANY] * 4,
        out_specs=[VMEM, SMEM, SMEM] + [VMEM] * 3,
        scratch_shapes=[
            pltpu.VMEM((64, 128), BF),
            pltpu.VMEM((64, 128), jnp.int32),
            pltpu.SMEM((64, 128), jnp.int32),
            pltpu.SMEM((160,), jnp.int32),
            pltpu.SMEM((160,), jnp.int32),
            pltpu.VMEM((5 * BLOCK, HD), BF),
        ]
        + stream_scratch() * NEAR_STREAMS
        + [pltpu.SemaphoreType.DMA((6,))],
        compiler_params=pltpu.CompilerParams(vmem_limit_bytes=24 << 20),
        cost_estimate=pl.CostEstimate(flops=4 * 10**9, bytes_accessed=4 << 20, transcendentals=1 << 20),
        name="near_pages",
    )(*args)


def far_call(pages, q_all, blocks, state, first, name):
    nb = len(blocks)
    part = jax.ShapeDtypeStruct((HD + 16, 2 * QROWS), BF)
    own = jax.ShapeDtypeStruct((HD + 8, 2 * QROWS), F32)
    return pl.pallas_call(
        functools.partial(far_kernel, nb, first),
        out_shape=[part if first else own, part],
        in_specs=[SMEM, VMEM] + [ANY] * nb + [VMEM] * 3,
        out_specs=[VMEM] * 2,
        scratch_shapes=[pltpu.VMEM((nb * BLOCK, HD), BF)]
        + stream_scratch() * STREAMS
        + [pltpu.SemaphoreType.DMA((nb,))],
        compiler_params=pltpu.CompilerParams(vmem_limit_bytes=24 << 20),
        cost_estimate=pl.CostEstimate(flops=10**9, bytes_accessed=4 << 20, transcendentals=1 << 20),
        name=name,
    )(pages, q_all, *blocks, *state)


def on_device(
    queries, tree_keys, tree_values, prefix_keys, prefix_values, tree_parent, page_table, out_weight
):
    rep = lax.axis_index("rep")
    head = lax.axis_index("head")
    q_own = queries.reshape(2 * QROWS, HD)
    kv = jnp.concatenate([prefix_keys, prefix_values], axis=0).reshape(BLOCK, HD)
    up1 = lax.ppermute(kv, "rep", z_perm(1))
    dn1 = lax.ppermute(kv, "rep", z_perm(-1))
    sent, local = pl.pallas_call(
        pack_kernel,
        out_shape=[
            jax.ShapeDtypeStruct((2 * QROWS + 16, HD), BF),
            jax.ShapeDtypeStruct((PAGES_AT + 2 * LOCAL_PAGES * 128, HD), BF),
        ],
        in_specs=[ANY] * 5 + [VMEM] * 2 + [ANY],
        out_specs=[VMEM] * 2,
        scratch_shapes=[pltpu.SemaphoreType.DMA((6,))],
        compiler_params=pltpu.CompilerParams(vmem_limit_bytes=59 << 20),
        name="pack",
    )(
        q_own, tree_keys.reshape(-1, HD), tree_values.reshape(-1, HD),
        prefix_keys.reshape(-1, HD), prefix_values.reshape(-1, HD), page_table, tree_parent.reshape(1, -1),
        kv,
    )
    up1, dn1, sent = lax.optimization_barrier((up1, dn1, sent))
    up2 = lax.ppermute(up1, "rep", z_perm(1))
    dn2 = lax.ppermute(dn1, "rep", z_perm(-1))
    sents = [lax.ppermute(sent, "rep", group_perm(r)) for r in (1, 2, 3)]
    up3 = lax.ppermute(up2, "rep", z_perm(1))
    dn3 = lax.ppermute(dn2, "rep", z_perm(-1))
    held = jnp.where((rep & 1) == 0, up2, dn2)
    opposite = lax.ppermute(
        held, "rep", [(rep_of(a, z, c), rep_of(a, z + 2 - 4 * c, c)) for a in range(2) for z in range(Z) for c in range(2)]
    )

    reps = jnp.arange(32, dtype=jnp.int32)
    same = ((reps ^ rep) & 17) == 0
    step = ((reps >> 1) - (rep >> 1)) & 7
    maps = jnp.full((32,), -(1 << 20), jnp.int32)
    for k, offsets in enumerate(GROUPS):
        for i, o in enumerate(offsets):
            maps = jnp.where(same & (step == o % Z), k * 65536 + i * 8, maps)
    q_all, list_far, list_far_x, *state = near_call(maps, local, *sents, up1, dn1, up2, dn2)
    blocks = (up3, dn3, opposite)
    p2, p3 = far_call(list_far_x, q_all, blocks, state, SESS // 2, "far_pages_x")
    p3 = lax.ppermute(p3, "rep", group_perm(3))
    p2 = lax.ppermute(p2, "rep", group_perm(2))
    own, p1 = far_call(list_far, q_all, blocks, state, 0, "far_pages_own")
    back = [p3, p2, lax.ppermute(p1, "rep", group_perm(1))]
    width = out_weight.shape[1]
    attn = pl.pallas_call(
        combine_kernel,
        out_shape=jax.ShapeDtypeStruct((128, 512), BF),
        in_specs=[SMEM] + [VMEM] * 4,
        out_specs=VMEM,
        scratch_shapes=[pltpu.VMEM((2 * QROWS, HD), F32)],
        compiler_params=pltpu.CompilerParams(vmem_limit_bytes=24 << 20),
        cost_estimate=pl.CostEstimate(flops=10**6, bytes_accessed=1 << 20, transcendentals=4096),
        name="combine",
    )(head.reshape(1).astype(jnp.int32), own, *back)
    rows = jnp.dot(attn, out_weight, preferred_element_type=F32).astype(BF)
    parts = [rows[k * 16:(k + 1) * 16] for k in range(8)]
    terms = [
        lax.ppermute(part, "head", [(i, i ^ flip) for i in range(8)])
        for part, flip in zip(parts[1:], HEADS[1:])
    ]
    return pl.pallas_call(
        sum_kernel,
        out_shape=jax.ShapeDtypeStruct((16, width), BF),
        in_specs=[VMEM] * 8,
        out_specs=VMEM,
        compiler_params=pltpu.CompilerParams(vmem_limit_bytes=24 << 20),
        name="sum_heads",
    )(parts[0], *terms)


def solution(mesh):
    in_specs = (
        P("rep", "head", None),
        P("rep", "head", None),
        P("rep", "head", None),
        P("rep", "head", None, None),
        P("rep", "head", None, None),
        P("rep"),
        P("rep", None),
        P("head", None),
    )
    out_specs = P(("rep", "head"), None)
    return jax.shard_map(
        on_device, mesh=mesh, in_specs=in_specs, out_specs=out_specs, check_vma=False
    )
```

```python
import functools
import math

import jax
import jax.numpy as jnp
from jax import lax
from jax.experimental import pallas as pl
from jax.experimental.pallas import tpu as pltpu
from jax.sharding import PartitionSpec as P

NEG = -1e30
Z = 8
GROUP = 4
LOCAL_PAGES = 4
TK_AT = 528
TV_AT = 656
BLOCK = 1024
PAGES_AT = 784
TREE = 64
QROWS = 256
HD = 128
SESS = 8
C2 = (HD ** -0.5) * math.log2(math.e)
BF = jnp.bfloat16
F32 = jnp.float32

STREAMS = 4
GROUPS = ((0, -1, 1, -2, 2), (-3, 3, 4))


HEADS = (0, 5, 1, 7, 3, 2, 6, 4)


def rep_of(xh, z, c):
    return xh * 16 + (z % Z) * 2 + c


def z_perm(k):
    return [(rep_of(a, z, c), rep_of(a, z + k, c)) for a in range(2) for z in range(Z) for c in range(2)]


def group_perm(r):
    return [(rep_of(a, z, c), rep_of(a ^ (r >> 1), z, c ^ (r & 1))) for a in range(2) for z in range(Z) for c in range(2)]


def page(kv, i):
    return kv[pl.ds(pl.multiple_of(i * 128, 128), 128), :]


def pair_steps(entries, q_ref, kv, streams):
    at = [(e >> 8, e & 255) for e in entries]
    scores = [
        lax.dot_general(page(kv, k), q_ref[pl.ds(pl.multiple_of((s & (SESS - 1)) * QROWS, QROWS), QROWS), :], (((1,), (1,)), ((), ())), preferred_element_type=F32)
        for s, k in at
    ]
    olds = [m[s] for (s, _), (m, _, _) in zip(at, streams)]
    news = [jnp.maximum(o, jnp.max(x, axis=0, keepdims=True)) for o, x in zip(olds, scores)]
    probs = [jnp.exp2(x * C2 - n * C2) for x, n in zip(scores, news)]
    fixes = [jnp.exp2((o - n) * C2) for o, n in zip(olds, news)]
    parts = [
        lax.dot_general(
            page(kv, k + LOCAL_PAGES), p.astype(BF), (((0,), (0,)), ((), ())), preferred_element_type=F32
        )
        for (_, k), p in zip(at, probs)
    ]
    for (s, _), o, n, p, fix, part, (m_ref, l_ref, a_ref) in zip(at, olds, news, probs, fixes, parts, streams):
        m_ref[s] = n
        l_ref[s] = l_ref[s] * fix + jnp.sum(p, axis=0, keepdims=True)
        a_ref[s] = jnp.where(o > NEG, a_ref[s] * fix, 0.0) + part


def all_pairs(entries, q_ref, kv, streams):
    ns = len(streams)

    @pl.loop(0, (entries[0] + ns - 1) >> (ns.bit_length() - 1))
    def _(i):
        pair_steps([entries[ns * i + r + 1] for r in range(ns)], q_ref, kv, streams)


def streams_of(refs):
    return [tuple(refs[3 * r:3 * r + 3]) for r in range(STREAMS)]


def clear(streams):
    for m_ref, l_ref, _ in streams:
        m_ref[...] = jnp.full(m_ref.shape, NEG, F32)
        l_ref[...] = jnp.zeros(l_ref.shape, F32)


def merge(states):
    top = functools.reduce(jnp.maximum, [m for m, _, _ in states])
    ws = [jnp.exp2((m - top) * C2) for m, _, _ in states]
    total = sum(w * l for w, (_, l, _) in zip(ws, states))
    acc = sum(jnp.where(m > NEG, w * a, 0.0) for w, (m, _, a) in zip(ws, states))
    return top, total, acc


def pack_kernel(q, tk, tv, pk, pv, table, parent, kv, sent, local, sems):
    del kv
    copies = [
        pltpu.make_async_copy(q, sent.at[pl.ds(0, 2 * QROWS)], sems.at[0]),
        pltpu.make_async_copy(q, local.at[pl.ds(0, 2 * QROWS)], sems.at[1]),
        pltpu.make_async_copy(tk, local.at[pl.ds(TK_AT, 128)], sems.at[2]),
        pltpu.make_async_copy(tv, local.at[pl.ds(TV_AT, 128)], sems.at[3]),
        pltpu.make_async_copy(pk, local.at[pl.ds(PAGES_AT, LOCAL_PAGES * 128)], sems.at[4]),
        pltpu.make_async_copy(pv, local.at[pl.ds(PAGES_AT + LOCAL_PAGES * 128, LOCAL_PAGES * 128)], sems.at[5]),
    ]
    for cp in copies:
        cp.start()
    ids = table[...].astype(F32)
    row = lax.broadcasted_iota(jnp.int32, (16, 128), 0)
    above = parent[...].astype(F32)
    tail = pl.ds(2 * QROWS, 16)
    sent[tail, :] = jnp.zeros((16, 128), BF)
    local[tail, :] = jnp.where(row == 2, above, 0.0).astype(BF)
    row = row[:, :16]
    pages = jnp.where(row == 0, ids[0:1, :], jnp.where(row == 1, ids[1:2, :], 0.0))
    sent[tail, :16] = pages.astype(BF)
    local[tail, :16] = jnp.where(row == 2, above[:, :16], pages).astype(BF)
    for cp in copies:
        cp.wait()


def near_kernel(maps, local, s1, s2, s3, up1, dn1, up2, dn2, q_out, list_far, list_far_x, *refs):
    m_out, l_out, a_out, tails, ids, tbl, list_near, found, kv = refs[:9]
    lists = (list_near, list_far, list_far_x)
    streams = streams_of(refs[9:-1])
    sems = refs[-1]
    sents = (local, s1, s2, s3)
    for r, x in enumerate(sents):
        tails[pl.ds(r * 16, 16), :] = x[pl.ds(2 * QROWS, 16), :]
    ids[...] = tails[...].astype(F32).astype(jnp.int32)
    to_scalar = pltpu.make_async_copy(ids, tbl, sems.at[0])
    to_scalar.start()
    copies = load_blocks(
        [local.at[pl.ds(PAGES_AT, BLOCK)], up1, dn1, up2, dn2], kv, [sems.at[i + 1] for i in range(5)]
    )
    for r, x in enumerate(sents):
        q_out[pl.ds(r * 2 * QROWS, 2 * QROWS), :] = x[pl.ds(0, 2 * QROWS), :]
    clear(streams)
    both = 2 * TREE
    row = lax.broadcasted_iota(jnp.int32, (both, both), 0)
    lane = lax.broadcasted_iota(jnp.int32, (both, both), 1)
    above = ids[2:3, :] + jnp.where(lax.broadcasted_iota(jnp.int32, (1, both), 1) >= TREE, TREE, 0)
    reach = jnp.minimum((row == lane).astype(F32) + (row == above).astype(F32), 1.0)
    for _ in range(7):
        half = reach.astype(BF)
        reach = jnp.minimum(jnp.dot(half, half, preferred_element_type=F32), 1.0)
    half = reach.astype(BF)
    tree_row = lax.broadcasted_iota(jnp.int32, (both, QROWS), 0)
    of_query = lax.shift_right_logical(lax.broadcasted_iota(jnp.int32, (both, QROWS), 1), 2)
    m0, l0, a0 = streams[0]
    for s in range(2):
        widen = (tree_row == of_query + s * TREE).astype(BF)
        seen = jnp.dot(half[s * TREE:(s + 1) * TREE, :], widen, preferred_element_type=F32)
        scores = lax.dot_general(
            local[pl.ds(TK_AT + s * TREE, TREE), :],
            local[pl.ds(s * QROWS, QROWS), :],
            (((1,), (1,)), ((), ())),
            preferred_element_type=F32,
        )
        scores = jnp.where(seen > 0.5, scores, NEG)
        top = jnp.max(scores, axis=0, keepdims=True)
        probs = jnp.exp2(scores * C2 - top * C2)
        m0[s] = top
        l0[s] = jnp.sum(probs, axis=0, keepdims=True)
        a0[s] = lax.dot_general(
            local[pl.ds(TV_AT + s * TREE, TREE), :],
            probs.astype(BF),
            (((0,), (0,)), ((), ())),
            preferred_element_type=F32,
        )
    to_scalar.wait()

    def scan(r, n):
        for half in range(2):
            pages = [tbl[r * 16 + half, j] for j in range(16)]
            at = [maps[p >> 2] for p in pages]
            for p, where in zip(pages, at):
                found[n] = (r * 2 + half) * 256 + (p & 3) + where
                n = n + (where >= 0).astype(jnp.int32)
        return n

    total = lax.fori_loop(0, GROUP, scan, jnp.int32(0))

    def sort(i, counts):
        entry = found[i]
        kind = entry >> 16
        kind = kind + (kind & (entry >> 10))
        out = []
        for k in range(3):
            lists[k][counts[k] + 1] = entry & 65535
            out.append(counts[k] + (kind == k).astype(jnp.int32))
        return tuple(out)

    counts = lax.fori_loop(0, total, sort, (jnp.int32(0),) * 3)
    for k in range(3):
        lists[k][0] = counts[k]
        for r in range(STREAMS - 1):
            lists[k][counts[k] + 1 + r] = jnp.int32(SESS * 256)
    for cp in copies:
        cp.wait()
    all_pairs(list_near, q_out, kv, streams)
    for s in range(SESS):
        top, total, acc = merge([(m[s], l[s], a[s]) for m, l, a in streams])
        m_out[s] = top
        l_out[s] = total
        a_out[s] = acc


def load_blocks(blocks, kv, sems):
    copies = [pltpu.make_async_copy(b, kv.at[pl.ds(i * BLOCK, BLOCK)], sem) for i, (b, sem) in enumerate(zip(blocks, sems))]
    for cp in copies:
        cp.start()
    return copies


def far_kernel(nb, first, *refs):
    list_far, q_ref = refs[:2]
    blocks = refs[2:2 + nb]
    before = refs[2 + nb:5 + nb]
    outs = refs[5 + nb:7 + nb]
    kv = refs[7 + nb]
    streams = streams_of(refs[8 + nb:-1])
    copies = load_blocks(blocks, kv, [refs[-1].at[i] for i in range(nb)])
    clear(streams)
    for cp in copies:
        cp.wait()
    all_pairs(list_far, q_ref, kv, streams)
    for s in range(first, first + SESS // 2):
        top, total, acc = merge([(m[s], l[s], a[s]) for m, l, a in [before] + streams])
        some = total > 0.0
        safe = jnp.where(some, total, 1.0)
        acc = acc * (1.0 / safe)
        lse = jnp.where(some, top * C2 + jnp.log2(safe), NEG)
        lanes = pl.ds((s % 2) * QROWS, QROWS)
        if s < 2:
            outs[0][pl.ds(0, HD), lanes] = acc
            outs[0][pl.ds(HD, 8), lanes] = jnp.broadcast_to(lse, (8, QROWS))
        else:
            out = outs[(s - first) // 2]
            out[pl.ds(0, HD), lanes] = acc.astype(BF)
            hi = lse.astype(BF).astype(F32)
            mid = (lse - hi).astype(BF).astype(F32)
            low = lse - hi - mid
            row = lax.broadcasted_iota(jnp.int32, (16, QROWS), 0)
            parts = jnp.where(row == 0, hi, jnp.where(row == 1, mid, jnp.where(row == 2, low, 0.0)))
            out[pl.ds(HD, 16), lanes] = parts.astype(BF)


def combine_kernel(head_ref, own, p1, p2, p3, attn, rows_f32):
    lses = [own[HD:HD + 1, :]]
    vals = [own[:HD, :]]
    for p in (p1, p2, p3):
        tail = p[HD:HD + 16, :].astype(F32)
        lses.append(tail[0:1] + tail[1:2] + tail[2:3])
        vals.append(p[:HD, :].astype(F32))
    top = functools.reduce(jnp.maximum, lses)
    ws = [jnp.exp2(x - top) for x in lses]
    inv = 1.0 / sum(ws)
    mixed = sum(v * (w * inv) for v, w in zip(vals, ws))
    rows_f32[...] = mixed.T
    for k, flip in enumerate(HEADS):
        first = (head_ref[0] ^ flip) * 64
        for h in range(4):
            block = rows_f32[pl.ds(first + h, 16, stride=4), :]
            attn[pl.ds(k * 16, 16), pl.ds(h * HD, HD)] = block.astype(BF)


def sum_kernel(*refs):
    out = refs[-1]
    out[...] = functools.reduce(jnp.add, [r[...].astype(F32) for r in refs[:-1]]).astype(BF)


VMEM = pl.BlockSpec(memory_space=pltpu.VMEM)
SMEM = pl.BlockSpec(memory_space=pltpu.SMEM)
ANY = pl.BlockSpec(memory_space=pl.ANY)


def stream_scratch():
    return [
        pltpu.VMEM((SESS + 1, 1, QROWS), F32),
        pltpu.VMEM((SESS + 1, 1, QROWS), F32),
        pltpu.VMEM((SESS + 1, HD, QROWS), F32),
    ]


def state_shapes(n):
    return [
        jax.ShapeDtypeStruct((n, 1, QROWS), F32),
        jax.ShapeDtypeStruct((n, 1, QROWS), F32),
        jax.ShapeDtypeStruct((n, HD, QROWS), F32),
    ]


def near_call(*args):
    return pl.pallas_call(
        near_kernel,
        out_shape=[jax.ShapeDtypeStruct((SESS * QROWS, HD), BF), jax.ShapeDtypeStruct((160,), jnp.int32)]
        + [jax.ShapeDtypeStruct((160,), jnp.int32)]
        + state_shapes(SESS),
        in_specs=[SMEM] + [VMEM] * 4 + [ANY] * 4,
        out_specs=[VMEM, SMEM, SMEM] + [VMEM] * 3,
        scratch_shapes=[
            pltpu.VMEM((64, 128), BF),
            pltpu.VMEM((64, 128), jnp.int32),
            pltpu.SMEM((64, 128), jnp.int32),
            pltpu.SMEM((160,), jnp.int32),
            pltpu.SMEM((160,), jnp.int32),
            pltpu.VMEM((5 * BLOCK, HD), BF),
        ]
        + stream_scratch() * STREAMS
        + [pltpu.SemaphoreType.DMA((6,))],
        compiler_params=pltpu.CompilerParams(vmem_limit_bytes=24 << 20),
        cost_estimate=pl.CostEstimate(flops=4 * 10**9, bytes_accessed=4 << 20, transcendentals=1 << 20),
        name="near_pages",
    )(*args)


def far_call(pages, q_all, blocks, state, first, name):
    nb = len(blocks)
    part = jax.ShapeDtypeStruct((HD + 16, 2 * QROWS), BF)
    own = jax.ShapeDtypeStruct((HD + 8, 2 * QROWS), F32)
    return pl.pallas_call(
        functools.partial(far_kernel, nb, first),
        out_shape=[part if first else own, part],
        in_specs=[SMEM, VMEM] + [ANY] * nb + [VMEM] * 3,
        out_specs=[VMEM] * 2,
        scratch_shapes=[pltpu.VMEM((nb * BLOCK, HD), BF)]
        + stream_scratch() * STREAMS
        + [pltpu.SemaphoreType.DMA((nb,))],
        compiler_params=pltpu.CompilerParams(vmem_limit_bytes=24 << 20),
        cost_estimate=pl.CostEstimate(flops=10**9, bytes_accessed=4 << 20, transcendentals=1 << 20),
        name=name,
    )(pages, q_all, *blocks, *state)


def on_device(
    queries, tree_keys, tree_values, prefix_keys, prefix_values, tree_parent, page_table, out_weight
):
    rep = lax.axis_index("rep")
    head = lax.axis_index("head")
    q_own = queries.reshape(2 * QROWS, HD)
    kv = jnp.concatenate([prefix_keys, prefix_values], axis=0).reshape(BLOCK, HD)
    up1 = lax.ppermute(kv, "rep", z_perm(1))
    dn1 = lax.ppermute(kv, "rep", z_perm(-1))
    sent, local = pl.pallas_call(
        pack_kernel,
        out_shape=[
            jax.ShapeDtypeStruct((2 * QROWS + 16, HD), BF),
            jax.ShapeDtypeStruct((PAGES_AT + 2 * LOCAL_PAGES * 128, HD), BF),
        ],
        in_specs=[ANY] * 5 + [VMEM] * 2 + [ANY],
        out_specs=[VMEM] * 2,
        scratch_shapes=[pltpu.SemaphoreType.DMA((6,))],
        compiler_params=pltpu.CompilerParams(vmem_limit_bytes=59 << 20),
        name="pack",
    )(
        q_own, tree_keys.reshape(-1, HD), tree_values.reshape(-1, HD),
        prefix_keys.reshape(-1, HD), prefix_values.reshape(-1, HD), page_table, tree_parent.reshape(1, -1),
        kv,
    )
    up1, dn1, sent = lax.optimization_barrier((up1, dn1, sent))
    up2 = lax.ppermute(up1, "rep", z_perm(1))
    dn2 = lax.ppermute(dn1, "rep", z_perm(-1))
    sents = [lax.ppermute(sent, "rep", group_perm(r)) for r in (1, 2, 3)]
    up3 = lax.ppermute(up2, "rep", z_perm(1))
    dn3 = lax.ppermute(dn2, "rep", z_perm(-1))
    held = jnp.where((rep & 1) == 0, up2, dn2)
    opposite = lax.ppermute(
        held, "rep", [(rep_of(a, z, c), rep_of(a, z + 2 - 4 * c, c)) for a in range(2) for z in range(Z) for c in range(2)]
    )

    reps = jnp.arange(32, dtype=jnp.int32)
    same = ((reps ^ rep) & 17) == 0
    step = ((reps >> 1) - (rep >> 1)) & 7
    maps = jnp.full((32,), -(1 << 20), jnp.int32)
    for k, offsets in enumerate(GROUPS):
        for i, o in enumerate(offsets):
            maps = jnp.where(same & (step == o % Z), k * 65536 + i * 8, maps)
    q_all, list_far, list_far_x, *state = near_call(maps, local, *sents, up1, dn1, up2, dn2)
    blocks = (up3, dn3, opposite)
    p2, p3 = far_call(list_far_x, q_all, blocks, state, SESS // 2, "far_pages_x")
    p3 = lax.ppermute(p3, "rep", group_perm(3))
    p2 = lax.ppermute(p2, "rep", group_perm(2))
    own, p1 = far_call(list_far, q_all, blocks, state, 0, "far_pages_own")
    back = [p3, p2, lax.ppermute(p1, "rep", group_perm(1))]
    width = out_weight.shape[1]
    attn = pl.pallas_call(
        combine_kernel,
        out_shape=jax.ShapeDtypeStruct((128, 512), BF),
        in_specs=[SMEM] + [VMEM] * 4,
        out_specs=VMEM,
        scratch_shapes=[pltpu.VMEM((2 * QROWS, HD), F32)],
        compiler_params=pltpu.CompilerParams(vmem_limit_bytes=24 << 20),
        cost_estimate=pl.CostEstimate(flops=10**6, bytes_accessed=1 << 20, transcendentals=4096),
        name="combine",
    )(head.reshape(1).astype(jnp.int32), own, *back)
    rows = jnp.dot(attn, out_weight, preferred_element_type=F32).astype(BF)
    parts = [rows[k * 16:(k + 1) * 16] for k in range(8)]
    terms = [
        lax.ppermute(part, "head", [(i, i ^ flip) for i in range(8)])
        for part, flip in zip(parts[1:], HEADS[1:])
    ]
    return pl.pallas_call(
        sum_kernel,
        out_shape=jax.ShapeDtypeStruct((16, width), BF),
        in_specs=[VMEM] * 8,
        out_specs=VMEM,
        compiler_params=pltpu.CompilerParams(vmem_limit_bytes=24 << 20),
        name="sum_heads",
    )(parts[0], *terms)


def solution(mesh):
    in_specs = (
        P("rep", "head", None),
        P("rep", "head", None),
        P("rep", "head", None),
        P("rep", "head", None, None),
        P("rep", "head", None, None),
        P("rep"),
        P("rep", None),
        P("head", None),
    )
    out_specs = P(("rep", "head"), None)
    return jax.shard_map(
        on_device, mesh=mesh, in_specs=in_specs, out_specs=out_specs, check_vma=False
    )
```
